128 devices in a mesh: dp: 16 (over z, y_lo, core), mp: 8 (over x, y_hi).
Axes of the slice: x: 4, y: 4 (y_hi: 2, y_lo: 2; y = y_hi * 2 + y_lo), z: 4, core: 2. Of those that a mesh axis runs over, the one named last changes fastest.
Arguments:
- inputs: bfloat16 [8192, 6144], P('dp', 'mp'), may hold values from -6 to 6
- cotangent: bfloat16 [8192, 6144], P('dp', 'mp'), may hold values from -6 to 6
- layer_norm_gain: float32 [6144], replicated, may hold values from 0.1 to 1.9
- w_qkv: bfloat16 [6144, 3, 3072], P(None, None, 'mp'), may hold values from -0.078125 to 0.078125
- w_out: bfloat16 [3072, 6144], P('mp'), may hold values from -0.109375 to 0.109375
Outputs:
- input_grad: bfloat16 [8192, 6144], P('dp', 'mp')
- qkv_grad: bfloat16 [6144, 3, 3072], P('dp', None, 'mp')
- out_grad: bfloat16 [3072, 6144], P('mp', 'dp')
- gain_gradient: float32 [6144], P('mp')
The draws below stay inside these ranges and needn't reach their ends.
All inputs are finite; a program needn't handle non-finite values.
Results may differ from the reference program's by a relative error of at most 0.024.
Values may be sent and summed in bfloat16 or wider, within the bound.
No kernel may reach another device: no remote copies, remote signals or barrier semaphores. Data moves between devices by JAX's collectives and lax.ppermute only.
A program may use at most 192 MiB of HBM per device.

```python
import jax
import jax.numpy as jnp
from jax import lax

D = 6144
HEADS = 24
HEAD = 128
SEQ = 256
A = 3072
IMAGES = 32
TOKENS = 8192
N_DP = 16
N_MP = 8


def spiked(drawn, rng, source, target, parts, factor):
    owner, partner = [(jnp.arange(drawn.shape[axis_at]) // (drawn.shape[axis_at] // parts)).reshape([-1 if axis == axis_at else 1 for axis in range(drawn.ndim)]) for axis_at in (source, target)]
    chosen = jax.random.permutation(rng, parts)[partner]
    strong = (owner == chosen) | (owner == (partner + parts // 2) % parts)
    return jnp.where(strong, factor * drawn, drawn)


def shard_levels(rng, shape, cuts, least, largest):
    loudness = 1.0
    for position, parts in cuts:
        draws = jax.random.uniform(jax.random.fold_in(jax.random.fold_in(rng, 6), position), (parts,), jnp.float32, least / len(cuts), largest / len(cuts))
        loudness = loudness * jnp.repeat(jnp.exp(draws), shape[position] // parts).reshape((-1,) + (1,) * (len(shape) - 1 - position))
    return loudness


def centred(stream_key, dims, width, reach, shards=(), held_as=jnp.bfloat16):
    array = width * jax.random.normal(stream_key, dims, jnp.float32)
    if shards:
        array = array * shard_levels(stream_key, dims, shards, -0.22, 0.18)
    return jnp.clip(array, -reach, reach).astype(held_as)


def gaussian_with(stream_key, shape, width, reach, cuts, heavy, dtype=jnp.bfloat16):
    array = width * jax.random.normal(stream_key, shape, jnp.float32)
    if cuts:
        array = array * shard_levels(stream_key, shape, cuts, -0.22, 0.18)
    return jnp.clip(spiked(array, jax.random.fold_in(stream_key, 3), *heavy), -reach, reach).astype(dtype)


def setup_inputs(seed: int = 0) -> dict:
    key_list = jax.random.split(jax.random.key(seed), 6)
    inputs = centred(key_list[0], (TOKENS, D), 1.0, 6.0, ((0, 16), (1, 8)))
    cotangent = gaussian_with(key_list[1], (TOKENS, D), 1.0, 6.0, ((0, 16), (1, 8)), (0, 1, 16, 2.0))
    layer_norm_gain = jnp.clip(1.0 + 0.18 * jax.random.normal(key_list[2], (D,), jnp.float32), 0.1, 1.9)
    w_qkv = centred(key_list[3], (D, 3, A), D ** -0.5, 0.078125, ((2, 8),))
    w_out = centred(key_list[4], (A, D), A ** -0.5, 0.109375, ((0, 8),))
    return dict(inputs=inputs, cotangent=cotangent, layer_norm_gain=layer_norm_gain, w_qkv=w_qkv, w_out=w_out)


def head_norm(values):
    centered_input = values - lax.optimization_barrier(jnp.mean(values, axis=-1, keepdims=True))
    scale = lax.rsqrt(lax.optimization_barrier(jnp.mean(centered_input * centered_input, axis=-1, keepdims=True)) + 1e-06)
    return (centered_input * scale, scale)

def head_norm_grad(grad, normalized_rows, scale):
    return scale * (grad - lax.optimization_barrier(jnp.mean(grad, axis=-1, keepdims=True)) - normalized_rows * lax.optimization_barrier(jnp.mean(grad * normalized_rows, axis=-1, keepdims=True)))

def attend(query, keys, values, grad_out):
    factor = 1.0 / HEAD ** 0.5
    qf = query.astype(jnp.float32)
    kf = keys.astype(jnp.float32)
    vf = values.astype(jnp.float32)
    gf = grad_out.astype(jnp.float32)
    scores = jnp.einsum('shd,thd->hst', qf, kf) * factor
    weights = jnp.exp(scores)
    probs = weights / lax.optimization_barrier(jnp.sum(weights, axis=-1, keepdims=True))
    probs_b = probs.astype(jnp.bfloat16).astype(jnp.float32)
    attn = jnp.einsum('hst,thd->shd', probs_b, vf).astype(jnp.bfloat16)
    d_probs = jnp.einsum('shd,thd->hst', gf, vf)
    d_vals = jnp.einsum('hst,shd->thd', probs_b, gf)
    delta = lax.optimization_barrier(jnp.sum(probs * d_probs, axis=-1, keepdims=True))
    d_scores = (probs * (d_probs - delta) * factor).astype(jnp.bfloat16).astype(jnp.float32)
    d_query = jnp.einsum('hst,thd->shd', d_scores, kf)
    d_keys = jnp.einsum('hst,shd->thd', d_scores, qf)
    return (attn, d_query, d_keys, d_vals)

def group_sum(left, right):
    rows = TOKENS // N_DP

    def step(index, total):
        start = (index * rows).astype(jnp.int32)
        part_left = lax.dynamic_slice_in_dim(left, start, rows, 0)
        part_right = lax.dynamic_slice_in_dim(right, start, rows, 0)
        term = lax.dot_general(part_left, part_right, (((0,), (0,)), ((), ())), preferred_element_type=jnp.float32)
        return total + term.astype(jnp.bfloat16).astype(jnp.float32)
    empty = jnp.zeros((left.shape[1], right.shape[1]), jnp.float32)
    return lax.fori_loop(0, N_DP, step, empty)

def reference(inputs, cotangent, layer_norm_gain, w_qkv, w_out):
    x_rows = inputs.astype(jnp.float32)
    centered_input = x_rows - lax.optimization_barrier(jnp.mean(x_rows, axis=-1, keepdims=True))
    inverse_deviation = lax.rsqrt(lax.optimization_barrier(jnp.mean(centered_input * centered_input, axis=-1, keepdims=True)) + 1e-06)
    standardized_input = centered_input * inverse_deviation
    normalized_rows = (standardized_input * layer_norm_gain).astype(jnp.bfloat16)
    qkv = jnp.dot(normalized_rows, w_qkv.reshape(D, 3 * A), preferred_element_type=jnp.float32).reshape(TOKENS, 3, HEADS, HEAD)
    q_norm, q_scale = head_norm(qkv[:, 0])
    k_norm, k_scale = head_norm(qkv[:, 1])
    shape4 = (IMAGES, SEQ, HEADS, HEAD)
    q_b = q_norm.astype(jnp.bfloat16).reshape(shape4)
    k_b = k_norm.astype(jnp.bfloat16).reshape(shape4)
    v_b = qkv[:, 2].astype(jnp.bfloat16).reshape(shape4)
    d_attn = lax.dot_general(cotangent, w_out, (((1,), (1,)), ((), ())), preferred_element_type=jnp.float32)
    d_attn_b = d_attn.astype(jnp.bfloat16).reshape(shape4)
    attn, d_qn, d_kn, d_v = lax.map(lambda args: attend(*args), (q_b, k_b, v_b, d_attn_b))
    attn = attn.reshape(TOKENS, A)
    out_grad = group_sum(attn, cotangent).astype(jnp.bfloat16)
    d_q = head_norm_grad(d_qn.reshape(TOKENS, HEADS, HEAD), q_norm, q_scale)
    d_k = head_norm_grad(d_kn.reshape(TOKENS, HEADS, HEAD), k_norm, k_scale)
    d_qkv = jnp.stack([d_q.reshape(TOKENS, A), d_k.reshape(TOKENS, A), d_v.reshape(TOKENS, A)], axis=1).astype(jnp.bfloat16)
    qkv_grad = group_sum(normalized_rows, d_qkv.reshape(TOKENS, 3 * A)).astype(jnp.bfloat16).reshape(D, 3, A)
    block = A // N_MP
    normalized_gradient = jnp.zeros((TOKENS, D), jnp.float32)
    for index in range(N_MP):
        grad_block = d_qkv[:, :, index * block:(index + 1) * block].reshape(TOKENS, 3 * block)
        weight_block = w_qkv[:, :, index * block:(index + 1) * block].reshape(D, 3 * block)
        term = lax.dot_general(grad_block, weight_block, (((1,), (1,)), ((), ())), preferred_element_type=jnp.float32)
        normalized_gradient = normalized_gradient + term.astype(jnp.bfloat16).astype(jnp.float32)
    gain_gradient = lax.optimization_barrier(jnp.sum(normalized_gradient * standardized_input, axis=0))
    scaled_rows = normalized_gradient * layer_norm_gain
    backward_result = inverse_deviation * (scaled_rows - lax.optimization_barrier(jnp.mean(scaled_rows, axis=-1, keepdims=True)) - standardized_input * lax.optimization_barrier(jnp.mean(scaled_rows * standardized_input, axis=-1, keepdims=True)))
    input_grad = (cotangent.astype(jnp.float32) + backward_result).astype(jnp.bfloat16)
    return (input_grad, qkv_grad, out_grad, gain_gradient)
```

```python
import functools

import jax
import jax.numpy as jnp
from jax import lax
from jax.experimental import pallas as pl
from jax.experimental.pallas import tpu as pltpu
from jax.sharding import PartitionSpec as P

HEAD = 128
SEQ = 256
AXES = ("dp", "mp")
F32 = jnp.float32
BF16 = jnp.bfloat16


def place(index):
    dp, mp = divmod(index, 8)
    return mp // 2, (mp % 2) * 2 + (dp // 2) % 2, dp // 4, dp % 2


def index_of(x, y, z, core):
    x, y, z = x % 4, y % 4, z % 4
    return (z * 4 + (y % 2) * 2 + core) * 8 + x * 2 + y // 2


def shift(value, dx=0, dyhi=0, dylo=0, dz=0, dcore=0):
    pairs = []
    for index in range(128):
        x, y, z, core = place(index)
        pairs.append((index, index_of(x + dx, y ^ (2 * dyhi) ^ dylo, z + dz, core ^ dcore)))
    return lax.ppermute(value, AXES, pairs)


def after(value, *earlier):
    return lax.optimization_barrier((value, earlier))[0]


def dot(a, b, ca, cb):
    return lax.dot_general(a, b, (((ca,), (cb,)), ((), ())), preferred_element_type=F32)


def gather_first(own):
    return shift(own, dx=1), shift(own, dx=-1), shift(own, dyhi=1)


def gather_second(first):
    left, right, across = first
    half = left.shape[0] // 2
    far = jnp.concatenate([shift(left[:half], dx=1), shift(right[half:], dx=-1)])
    return {
        (3, 0): left,
        (1, 0): right,
        (0, 1): across,
        (2, 0): far,
        (3, 1): shift(across, dx=1),
        (1, 1): shift(across, dx=-1),
        (2, 1): shift(far, dyhi=1),
    }


def sum_over_mp(values):
    values = values + shift(values, dyhi=1)
    return values + shift(values, dx=1) + shift(values, dx=-1) + shift(values, dx=2)


def sum_over_dp(values):
    values = values + shift(values, dcore=1)
    values = values + shift(values, dylo=1)
    return values + shift(values, dz=1) + shift(values, dz=-1) + shift(values, dz=2)


def add(*terms):
    return sum(t.astype(F32) for t in terms)


def add_rounded(*terms):
    return add(*terms).astype(BF16)


def scatter_over_dp(blocks, ylo):
    far = blocks(2)
    from_left = shift(far[0], dz=1)
    from_right = shift(far[1], dz=-1)
    up, down = blocks(1), blocks(3)
    up = jnp.stack([add_rounded(up[0], from_left), up[1]])
    down = jnp.stack([down[0], add_rounded(down[1], from_right)])
    total = add_rounded(blocks(0), shift(up, dz=1), shift(down, dz=-1))
    mine = lax.dynamic_index_in_dim(total, ylo, 0, keepdims=False)
    other = lax.dynamic_index_in_dim(total, 1 - ylo, 0, keepdims=False)
    return add_rounded(mine, shift(other, dylo=1))


def scatter_over_mp(term):
    half = SEQ
    far_across = shift(term(2, 1), dyhi=1)
    from_left_across = shift(term(1, 1), dx=1)
    from_right_across = shift(term(3, 1), dx=-1)
    far = add_rounded(term(2, 0), far_across)
    from_left_half = shift(far[:half], dx=1)
    from_right_half = shift(far[half:], dx=-1)
    across = shift(add_rounded(term(0, 1), from_left_across, from_right_across), dyhi=1)
    right, left = term(1, 0), term(3, 0)
    right = jnp.concatenate([add_rounded(right[:half], from_left_half), right[half:]])
    left = jnp.concatenate([left[:half], add_rounded(left[half:], from_right_half)])
    return add(term(0, 0), shift(right, dx=1), shift(left, dx=-1), across)


def head_norm(values):
    centered = values - jnp.mean(values, axis=-1, keepdims=True)
    scale = lax.rsqrt(jnp.mean(centered * centered, axis=-1, keepdims=True) + 1e-06)
    return centered * scale, scale


def head_norm_grad(grad, normalized, scale):
    return scale * (
        grad
        - jnp.mean(grad, axis=-1, keepdims=True)
        - normalized * jnp.mean(grad * normalized, axis=-1, keepdims=True)
    )


def forward_kernel(q_ref, k_ref, v_ref, attn_ref, probs_ref):
    for head in range(3):
        columns = slice(head * HEAD, (head + 1) * HEAD)
        q_b = head_norm(q_ref[:, columns])[0].astype(BF16)
        k_b = head_norm(k_ref[:, columns])[0].astype(BF16)
        weights = jnp.exp(dot(q_b, k_b, 1, 1) * (1.0 / HEAD**0.5))
        probs = weights / jnp.sum(weights, axis=-1, keepdims=True)
        probs_ref[0, head] = probs
        attn_ref[:, columns] = dot(probs.astype(BF16), v_ref[:, columns].astype(BF16), 1, 0).astype(BF16)


def backward_kernel(q_ref, k_ref, v_ref, probs_ref, d_attn_ref, dq_ref, dk_ref, dv_ref):
    for head in range(3):
        columns = slice(head * HEAD, (head + 1) * HEAD)
        q_n, q_scale = head_norm(q_ref[:, columns])
        k_n, k_scale = head_norm(k_ref[:, columns])
        v_b = v_ref[:, columns].astype(BF16)
        probs = probs_ref[0, head]
        d_attn = d_attn_ref[:, columns].astype(BF16)
        d_probs = dot(d_attn, v_b, 1, 1)
        dv_ref[:, columns] = dot(probs.astype(BF16), d_attn, 0, 0).astype(BF16)
        delta = jnp.sum(probs * d_probs, axis=-1, keepdims=True)
        d_scores = (probs * (d_probs - delta) * (1.0 / HEAD**0.5)).astype(BF16)
        d_qn = dot(d_scores, k_n.astype(BF16), 1, 0)
        d_kn = dot(d_scores, q_n.astype(BF16), 0, 0)
        dq_ref[:, columns] = head_norm_grad(d_qn, q_n, q_scale).astype(BF16)
        dk_ref[:, columns] = head_norm_grad(d_kn, k_n, k_scale).astype(BF16)


ROW_BLOCK = pl.BlockSpec((SEQ, 3 * HEAD), lambda i: (i, 0))
PROBS_BLOCK = pl.BlockSpec((1, 3, SEQ, SEQ), lambda i: (i, 0, 0, 0))
PARAMS = pltpu.CompilerParams(vmem_limit_bytes=24 * 2**20)


def attention_forward(q, k, v):
    rows, width = q.shape
    return pl.pallas_call(
        forward_kernel,
        grid=(rows // SEQ,),
        in_specs=[ROW_BLOCK] * 3,
        out_specs=[ROW_BLOCK, PROBS_BLOCK],
        out_shape=[
            jax.ShapeDtypeStruct((rows, width), BF16),
            jax.ShapeDtypeStruct((rows // SEQ, 3, SEQ, SEQ), F32),
        ],
        compiler_params=PARAMS,
        cost_estimate=pl.CostEstimate(flops=10**9, bytes_accessed=5 * 10**6, transcendentals=4 * 10**5),
    )(q, k, v)


def attention_backward(q, k, v, probs, d_attn):
    rows, width = q.shape
    return pl.pallas_call(
        backward_kernel,
        grid=(rows // SEQ,),
        in_specs=[ROW_BLOCK] * 3 + [PROBS_BLOCK, ROW_BLOCK],
        out_specs=[ROW_BLOCK] * 3,
        out_shape=[jax.ShapeDtypeStruct((rows, width), BF16)] * 3,
        compiler_params=PARAMS,
        cost_estimate=pl.CostEstimate(flops=2 * 10**9, bytes_accessed=8 * 10**6, transcendentals=0),
    )(q, k, v, probs, d_attn)


def body(inputs, cotangent, layer_norm_gain, w_qkv, w_out):
    rows, shard = inputs.shape
    dp, mp = lax.axis_index("dp"), lax.axis_index("mp")
    x, yhi = mp // 2, mp % 2
    z, ylo, core = dp // 4, (dp // 2) % 2, dp % 2
    half = shard // 2

    def chunk_at(dx, dyhi):
        return lax.rem(x + dx, 4) * 2 + lax.rem(yhi + dyhi, 2)

    ct_first = gather_first(cotangent)

    x_rows = inputs.astype(F32)
    mean = jnp.mean(x_rows, axis=-1)
    spread = jnp.sum(jnp.square(x_rows - mean[:, None]), axis=-1)
    own_stats = jnp.stack([mean, spread])

    def joined(parts, count):
        joined_mean = sum(p[0] for p in parts) / len(parts)
        joined_spread = sum(p[1] + count * jnp.square(p[0] - joined_mean) for p in parts)
        return jnp.stack([joined_mean, joined_spread])

    pair = joined([own_stats, shift(own_stats, dyhi=1)], float(shard))
    stats = joined([pair, shift(pair, dx=1), shift(pair, dx=-1), shift(pair, dx=2)], 2.0 * shard)
    inverse_deviation = lax.rsqrt(stats[1] / (8 * shard) + 1e-06)[:, None]
    standardized = (x_rows - stats[0][:, None]) * inverse_deviation
    gain = lax.dynamic_slice_in_dim(layer_norm_gain, mp * shard, shard, 0)
    normed_own = (standardized * gain).astype(BF16)

    normed = {(0, 0): normed_own, **gather_second(gather_first(normed_own))}
    ct_first = after(ct_first, normed[3, 1], normed[1, 1], normed[2, 0])
    ct = {(0, 0): cotangent, **gather_second(ct_first)}

    weights = [w_qkv[:, j, :] for j in range(3)]

    def weight_rows(j, chunk):
        return lax.dynamic_slice_in_dim(weights[j], chunk * shard, shard, 0)

    order = [(0, 0), (3, 0), (1, 0), (0, 1), (2, 0), (3, 1), (1, 1), (2, 1)]
    qkv = [None] * 3
    for key in order:
        for j in range(3):
            term = dot(normed[key], weight_rows(j, chunk_at(*key)), 1, 0)
            qkv[j] = term if qkv[j] is None else qkv[j] + term
    q, k, v = qkv
    attn, probs = attention_forward(q, k, v)

    def halves(chunks):
        kept = jnp.zeros((8, rows, half), BF16)
        given = jnp.zeros((8, rows, half), BF16)
        for key in order:
            chunk = chunks[key]
            at = chunk_at(*key)
            mine = lax.dynamic_slice_in_dim(chunk, core * half, half, 1)
            other = lax.dynamic_slice_in_dim(chunk, (1 - core) * half, half, 1)
            kept = lax.dynamic_update_index_in_dim(kept, mine, at, 0)
            given = lax.dynamic_update_index_in_dim(given, other, at, 0)
        return kept, shift(given, dcore=1)

    normed_kept, normed_got = halves(normed)
    ct_kept, ct_got = halves(ct)

    d_attn = None
    for key in order:
        term = dot(ct[key], lax.dynamic_slice_in_dim(w_out, chunk_at(*key) * shard, shard, 1), 1, 1)
        d_attn = term if d_attn is None else d_attn + term

    attn_got = shift(attn, dcore=1)

    def pair_at(stacked, dz):
        return lax.dynamic_slice_in_dim(stacked, lax.rem(z + dz, 4) * 2, 2, 0)

    def out_blocks(dz):
        kept, got = pair_at(ct_kept, dz), pair_at(ct_got, dz)
        return jnp.stack([add_rounded(dot(attn, kept[i], 0, 0) + dot(attn_got, got[i], 0, 0)) for i in range(2)])

    out_grad = scatter_over_dp(out_blocks, ylo)

    d_qkv = attention_backward(q, k, v, probs, d_attn)
    d_qkv_got = [shift(d, dcore=1) for d in d_qkv]

    def qkv_blocks(j):
        def blocks(dz):
            kept, got = pair_at(normed_kept, dz), pair_at(normed_got, dz)
            return jnp.stack(
                [add_rounded(dot(kept[i], d_qkv[j], 0, 0) + dot(got[i], d_qkv_got[j], 0, 0)) for i in range(2)]
            )

        return blocks

    def normed_term(dx, dyhi):
        chunk = chunk_at(dx, dyhi)
        return sum(dot(d_qkv[j], weight_rows(j, chunk), 1, 1) for j in range(3)).astype(BF16)

    d_normed = scatter_over_mp(normed_term)
    qkv_grad = jnp.stack([scatter_over_dp(qkv_blocks(j), ylo) for j in (2, 0, 1)])
    qkv_grad = jnp.stack([qkv_grad[1], qkv_grad[2], qkv_grad[0]], axis=1)

    scaled = d_normed * gain
    sums = jnp.stack([jnp.sum(scaled, axis=-1), jnp.sum(scaled * standardized, axis=-1)])
    means = sum_over_mp(sums) / (8 * shard)
    gain_gradient = sum_over_dp(jnp.sum(d_normed * standardized, axis=0).reshape(6, -1)).reshape(shard)
    back = inverse_deviation * (scaled - means[0][:, None] - standardized * means[1][:, None])
    input_grad = (cotangent.astype(F32) + back).astype(BF16)
    return input_grad, qkv_grad, out_grad, gain_gradient


def solution(mesh):
    in_specs = (P("dp", "mp"), P("dp", "mp"), P(), P(None, None, "mp"), P("mp", None))
    out_specs = (P("dp", "mp"), P("dp", None, "mp"), P("mp", "dp"), P("mp"))
    return jax.shard_map(body, mesh=mesh, in_specs=in_specs, out_specs=out_specs, check_vma=False)
```

```python
import functools

import jax
import jax.numpy as jnp
from jax import lax
from jax.experimental import pallas as pl
from jax.experimental.pallas import tpu as pltpu
from jax.sharding import PartitionSpec as P

HEAD = 128
SEQ = 256
AXES = ("dp", "mp")
F32 = jnp.float32
BF16 = jnp.bfloat16


def place(index):
    dp, mp = divmod(index, 8)
    return mp // 2, (mp % 2) * 2 + (dp // 2) % 2, dp // 4, dp % 2


def index_of(x, y, z, core):
    x, y, z = x % 4, y % 4, z % 4
    return (z * 4 + (y % 2) * 2 + core) * 8 + x * 2 + y // 2


def shift(value, dx=0, dyhi=0, dylo=0, dz=0, dcore=0):
    pairs = []
    for index in range(128):
        x, y, z, core = place(index)
        pairs.append((index, index_of(x + dx, y ^ (2 * dyhi) ^ dylo, z + dz, core ^ dcore)))
    return lax.ppermute(value, AXES, pairs)


def fence(*values):
    return lax.optimization_barrier(values)


def dot(a, b, ca, cb):
    return lax.dot_general(a, b, (((ca,), (cb,)), ((), ())), preferred_element_type=F32)


def sum_over_mp(values):
    values = values + shift(values, dyhi=1)
    return values + shift(values, dx=1) + shift(values, dx=-1) + shift(values, dx=2)


def sum_over_dp(values):
    values = values + shift(values, dcore=1)
    values = values + shift(values, dylo=1)
    return values + shift(values, dz=1) + shift(values, dz=-1) + shift(values, dz=2)


def add(*terms):
    return sum(t.astype(F32) for t in terms)


def add_rounded(*terms):
    return add(*terms).astype(BF16)


def head_norm(values):
    centered = values - jnp.mean(values, axis=-1, keepdims=True)
    scale = lax.rsqrt(jnp.mean(centered * centered, axis=-1, keepdims=True) + 1e-06)
    return centered * scale, scale


def head_norm_grad(grad, normalized, scale):
    return scale * (
        grad
        - jnp.mean(grad, axis=-1, keepdims=True)
        - normalized * jnp.mean(grad * normalized, axis=-1, keepdims=True)
    )


def forward_kernel(q_ref, k_ref, v_ref, attn_ref, probs_ref):
    for head in range(3):
        columns = slice(head * HEAD, (head + 1) * HEAD)
        q_b = head_norm(q_ref[:, columns])[0].astype(BF16)
        k_b = head_norm(k_ref[:, columns])[0].astype(BF16)
        weights = jnp.exp(dot(q_b, k_b, 1, 1) * (1.0 / HEAD**0.5))
        probs = weights / jnp.sum(weights, axis=-1, keepdims=True)
        probs_ref[0, head] = probs
        attn_ref[:, columns] = dot(probs.astype(BF16), v_ref[:, columns].astype(BF16), 1, 0).astype(BF16)


def backward_kernel(q_ref, k_ref, v_ref, probs_ref, d_attn_ref, grad_ref):
    for head in range(3):
        columns = slice(head * HEAD, (head + 1) * HEAD)
        q_n, q_scale = head_norm(q_ref[:, columns])
        k_n, k_scale = head_norm(k_ref[:, columns])
        v_b = v_ref[:, columns].astype(BF16)
        probs = probs_ref[0, head]
        d_attn = d_attn_ref[:, columns].astype(BF16)
        d_probs = dot(d_attn, v_b, 1, 1)
        grad_ref[2, :, columns] = dot(probs.astype(BF16), d_attn, 0, 0).astype(BF16)
        delta = jnp.sum(probs * d_probs, axis=-1, keepdims=True)
        d_scores = (probs * (d_probs - delta) * (1.0 / HEAD**0.5)).astype(BF16)
        d_qn = dot(d_scores, k_n.astype(BF16), 1, 0)
        d_kn = dot(d_scores, q_n.astype(BF16), 0, 0)
        grad_ref[0, :, columns] = head_norm_grad(d_qn, q_n, q_scale).astype(BF16)
        grad_ref[1, :, columns] = head_norm_grad(d_kn, k_n, k_scale).astype(BF16)


ROW_BLOCK = pl.BlockSpec((SEQ, 3 * HEAD), lambda i: (i, 0))
PROBS_BLOCK = pl.BlockSpec((1, 3, SEQ, SEQ), lambda i: (i, 0, 0, 0))
PARAMS = pltpu.CompilerParams(vmem_limit_bytes=24 * 2**20)


def attention_forward(q, k, v):
    rows, width = q.shape
    return pl.pallas_call(
        forward_kernel,
        grid=(rows // SEQ,),
        in_specs=[ROW_BLOCK] * 3,
        out_specs=[ROW_BLOCK, PROBS_BLOCK],
        out_shape=[
            jax.ShapeDtypeStruct((rows, width), BF16),
            jax.ShapeDtypeStruct((rows // SEQ, 3, SEQ, SEQ), F32),
        ],
        compiler_params=PARAMS,
        cost_estimate=pl.CostEstimate(flops=10**9, bytes_accessed=5 * 10**6, transcendentals=4 * 10**5),
    )(q, k, v)


def attention_backward(q, k, v, probs, d_attn):
    rows, width = q.shape
    return pl.pallas_call(
        backward_kernel,
        grid=(rows // SEQ,),
        in_specs=[ROW_BLOCK] * 3 + [PROBS_BLOCK, ROW_BLOCK],
        out_specs=pl.BlockSpec((3, SEQ, width), lambda i: (0, i, 0)),
        out_shape=jax.ShapeDtypeStruct((3, rows, width), BF16),
        compiler_params=PARAMS,
        cost_estimate=pl.CostEstimate(flops=2 * 10**9, bytes_accessed=8 * 10**6, transcendentals=0),
    )(q, k, v, probs, d_attn)


def pack_kernel(transposed, place_ref, mine_ref, other_ref, *refs):
    for source, target in zip((mine_ref, other_ref), refs[-2:]):
        target[0] = source[...].T if transposed else source[...]


def pack(chunk, at, core, buffers, transposed):
    rows, half = chunk.shape[0], chunk.shape[1] // 2
    block = (1, half, rows) if transposed else (1, rows, half)
    return pl.pallas_call(
        functools.partial(pack_kernel, transposed),
        grid_spec=pltpu.PrefetchScalarGridSpec(
            num_scalar_prefetch=1,
            grid=(1,),
            in_specs=[
                pl.BlockSpec((rows, half), lambda i, place: (0, place[1])),
                pl.BlockSpec((rows, half), lambda i, place: (0, 1 - place[1])),
            ]
            + [pl.BlockSpec(memory_space=pl.ANY)] * len(buffers),
            out_specs=[pl.BlockSpec(block, lambda i, place: (place[0], 0, 0))] * 2,
        ),
        out_shape=[jax.ShapeDtypeStruct((8,) + block[1:], BF16)] * 2,
        input_output_aliases={3: 0, 4: 1} if buffers else {},
        compiler_params=PARAMS,
        cost_estimate=pl.CostEstimate(flops=0, bytes_accessed=4 * rows * half * 2, transcendentals=0),
    )(jnp.stack([at, core]), chunk, chunk, *buffers)


def block_kernel(offsets, parts, place_ref, left_ref, left_got_ref, right_ref, right_got_ref, *refs):
    total = dot(left_ref[0], right_ref[0], 1, 0) + dot(left_got_ref[0], right_got_ref[0], 1, 0)
    size = total.shape[0] // parts
    for part in range(parts):
        piece = total[part * size : (part + 1) * size]
        for start, ref in zip(offsets, refs):
            if ref.shape[1] == total.shape[0]:
                piece = piece + ref[0, part * size : (part + 1) * size].astype(F32)
            elif start == part * size:
                piece = piece + ref[0].astype(F32)
        refs[len(offsets) + part][0] = piece.astype(BF16)


def block_term(at, left, right, added=(), parts=1, split=False):
    count = 1 if left[0].shape[0] == 1 else right[0].shape[0]
    rows, depth = left[0].shape[1:]
    columns = right[0].shape[2]
    if left[0].shape[0] == 1:
        left_map, right_map = lambda j, place: (0, 0, 0), lambda j, place: (place[0], 0, 0)
    else:
        left_map, right_map = lambda j, place: (place[0], 0, 0), lambda j, place: (j, 0, 0)
    each = lambda j, place: (j, 0, 0)
    halves = 2 if split else 1
    parts = 2 if split or any(a.shape[1] < rows for _, a in added) else 1
    body = functools.partial(block_kernel, tuple(start for start, _ in added), parts)
    if parts > halves:
        def body(*refs):
            base = 5 + len(added)
            out = refs[base]
            size = rows // 2
            views = [out.at[:, pl.ds(i * size, size), :] for i in range(2)]
            block_kernel(tuple(start for start, _ in added), 2, *refs[:base], *views)
    outs = [jax.ShapeDtypeStruct((count, rows // halves, columns), BF16)] * halves
    result = pl.pallas_call(
        body,
        grid_spec=pltpu.PrefetchScalarGridSpec(
            num_scalar_prefetch=1,
            grid=(count,),
            in_specs=[pl.BlockSpec((1, rows, depth), left_map)] * 2
            + [pl.BlockSpec((1, depth, columns), right_map)] * 2
            + [pl.BlockSpec((1,) + a.shape[1:], each) for _, a in added],
            out_specs=[pl.BlockSpec((1, rows // halves, columns), each)] * halves,
        ),
        out_shape=outs,
        compiler_params=PARAMS,
        cost_estimate=pl.CostEstimate(
            flops=count * 4 * rows * depth * columns, bytes_accessed=2 * count * rows * depth * 4, transcendentals=0
        ),
    )(at[None], *left, *right, *[a for _, a in added])
    return result if split else result[0]


def body(inputs, cotangent, layer_norm_gain, w_qkv, w_out):
    rows, shard = inputs.shape
    dp, mp = lax.axis_index("dp"), lax.axis_index("mp")
    x, yhi = mp // 2, mp % 2
    z, ylo, core = dp // 4, (dp // 2) % 2, dp % 2
    half = shard // 2
    seq = SEQ

    def chunk_at(key):
        return lax.rem(x + key[0], 4) * 2 + lax.rem(yhi + key[1], 2)

    weights = jnp.transpose(w_qkv, (1, 0, 2))

    def weight_rows(j, key):
        start = chunk_at(key) * shard
        return lax.dynamic_slice(weights, (j, start, 0), (1, shard, weights.shape[2]))[0]

    def add_qkv(totals, chunks, keys):
        for key in keys:
            terms = [dot(chunks[key], weight_rows(j, key), 1, 0) for j in range(3)]
            totals = terms if totals is None else [a + b for a, b in zip(totals, terms)]
        return totals

    def add_d_attn(total, chunks, keys):
        for key in keys:
            term = dot(chunks[key], lax.dynamic_slice_in_dim(w_out, chunk_at(key) * shard, shard, 1), 1, 1)
            total = term if total is None else total + term
        return total

    def pack_all(buffers, chunks, keys, transposed):
        for key in keys:
            buffers = pack(chunks[key], chunk_at(key), core, buffers, transposed)
        return buffers

    own, left, right, across, far = (0, 0), (3, 0), (1, 0), (0, 1), (2, 0)
    near = [own, left, right, across]
    last = [(3, 1), (1, 1), (2, 1)]

    ct = {own: cotangent, left: shift(cotangent, dx=1), right: shift(cotangent, dx=-1), across: shift(cotangent, dyhi=1)}
    x_rows = inputs.astype(F32)
    mean = jnp.mean(x_rows, axis=-1)
    spread = jnp.sum(jnp.square(x_rows - mean[:, None]), axis=-1)
    own_stats = jnp.stack([mean, spread])

    def joined(parts, count):
        joined_mean = sum(p[0] for p in parts) / len(parts)
        joined_spread = sum(p[1] + count * jnp.square(p[0] - joined_mean) for p in parts)
        return jnp.stack([joined_mean, joined_spread])

    pair = joined([own_stats, shift(own_stats, dyhi=1)], float(shard))
    stats = joined([pair, shift(pair, dx=1), shift(pair, dx=-1), shift(pair, dx=2)], 2.0 * shard)
    inverse_deviation = lax.rsqrt(stats[1] / (8 * shard) + 1e-06)[:, None]
    standardized = (x_rows - stats[0][:, None]) * inverse_deviation
    gain = lax.dynamic_slice_in_dim(layer_norm_gain, mp * shard, shard, 0)
    normed_own = (standardized * gain).astype(BF16)
    ct, normed_own = fence(ct, normed_own)

    normed = {own: normed_own}
    normed[left], normed[right], normed[across] = (
        shift(normed_own, dx=1),
        shift(normed_own, dx=-1),
        shift(normed_own, dyhi=1),
    )
    d_attn = add_d_attn(None, ct, near)
    qkv = add_qkv(None, normed, [own])
    normed, d_attn, qkv = fence(normed, d_attn, qkv)

    normed[far] = jnp.concatenate([shift(normed[left][:seq], dx=1), shift(normed[right][seq:], dx=-1)])
    qkv = add_qkv(qkv, normed, [left, right, across])
    normed, qkv, ct, d_attn = fence(normed, qkv, ct, d_attn)

    normed[3, 1], normed[1, 1] = shift(normed[across], dx=1), shift(normed[across], dx=-1)
    normed[2, 1] = shift(normed[far], dyhi=1)
    qkv = add_qkv(qkv, normed, [far])
    normed_packs = pack_all((), normed, near + [far], True)
    ct_packs = pack_all((), ct, near, False)
    normed, qkv, normed_packs, ct, ct_packs = fence(normed, qkv, normed_packs, ct, ct_packs)

    ct[far] = jnp.concatenate([shift(ct[left][:seq], dx=1), shift(ct[right][seq:], dx=-1)])
    q, k, v = add_qkv(qkv, normed, last)
    attn, probs = attention_forward(q, k, v)
    ct, q, k, v, attn, probs, normed, normed_packs = fence(ct, q, k, v, attn, probs, normed, normed_packs)

    ct[3, 1], ct[1, 1] = shift(ct[across], dx=1), shift(ct[across], dx=-1)
    ct[2, 1] = shift(ct[far], dyhi=1)
    normed_packs = pack_all(normed_packs, normed, last, True)
    normed_sides = (normed_packs[0], shift(normed_packs[1], dcore=1))
    attn_t = attn.T[None]
    attn_sides = (attn_t, shift(attn_t, dcore=1))
    d_attn = add_d_attn(d_attn, ct, [far])
    ct_packs = pack_all(ct_packs, ct, [far], False)
    ct, normed_sides, attn_sides, d_attn, ct_packs = fence(ct, normed_sides, attn_sides, d_attn, ct_packs)

    ct_packs = pack_all(ct_packs, ct, last, False)
    ct, ct_packs = fence(ct, ct_packs)
    ct_sides = (ct_packs[0], shift(ct_packs[1], dcore=1))
    d_attn = add_d_attn(d_attn, ct, last)
    ct_sides, d_attn = fence(ct_sides, d_attn)

    def at(dz, mine):
        return lax.rem(z + dz, 4) * 2 + (ylo if mine else 1 - ylo)

    def out_term(dz, mine, added=(), split=False):
        return block_term(at(dz, mine), attn_sides, ct_sides, added, split=split)

    out_far = [out_term(2, mine, split=True) for mine in (False, True)]
    out_far, q, k, v, probs, d_attn = fence(out_far, q, k, v, probs, d_attn)
    out_far = [(shift(a, dz=1), shift(b, dz=-1)) for a, b in out_far]

    d_qkv = attention_backward(q, k, v, probs, d_attn)
    out_far, d_qkv = fence(out_far, d_qkv)

    def normed_term(key):
        return sum(dot(d_qkv[j], weight_rows(j, key), 1, 1) for j in range(3)).astype(BF16)

    def qkv_term(dz, mine, added=(), split=False):
        return block_term(at(dz, mine), normed_sides, qkv_sides, added, split=split)

    def up_down(term, far_halves, mine):
        up, down = term(1, mine, [(0, far_halves[0])]), term(3, mine, [(half // 2, far_halves[1])])
        return up, down

    qkv_sides = (d_qkv, shift(d_qkv, dcore=1))
    far_across, left_across, right_across = normed_term((2, 1)), normed_term((1, 1)), normed_term((3, 1))
    out_other = up_down(out_term, out_far[0], False)
    out_mine = up_down(out_term, out_far[1], True)
    qkv_sides, far_across, left_across, right_across, out_other, out_mine = fence(
        qkv_sides, far_across, left_across, right_across, out_other, out_mine
    )

    far_across, left_across, right_across = (
        shift(far_across, dyhi=1),
        shift(left_across, dx=1),
        shift(right_across, dx=-1),
    )
    out_other, out_mine = [(shift(up, dz=1), shift(down, dz=-1)) for up, down in (out_other, out_mine)]
    far_halves = [qkv_term(2, mine, split=True) for mine in (False, True)]
    far_halves = [(shift(a, dz=1), shift(b, dz=-1)) for a, b in far_halves]
    far_term, across_term = normed_term((2, 0)), normed_term((0, 1))
    far_across, left_across, right_across, out_other, out_mine, far_halves, far_term, across_term = fence(
        far_across, left_across, right_across, out_other, out_mine, far_halves, far_term, across_term
    )

    far_term = add_rounded(far_term, far_across)
    far_left, far_right = shift(far_term[:seq], dx=1), shift(far_term[seq:], dx=-1)
    across_sum = shift(add_rounded(across_term, left_across, right_across), dyhi=1)
    up, down = up_down(qkv_term, far_halves[0], False)
    other = (shift(up, dz=1), shift(down, dz=-1))
    right_term, left_term, own_term = normed_term(right), normed_term(left), normed_term(own)
    out_other = out_term(0, False, [(0, out_other[0]), (0, out_other[1])])
    out_other_got = shift(out_other, dylo=1)
    far_left, far_right, right_term, left_term, own_term, far_halves = fence(
        far_left, far_right, right_term, left_term, own_term, far_halves
    )

    right_term = jnp.concatenate([add_rounded(right_term[:seq], far_left), right_term[seq:]])
    left_term = jnp.concatenate([left_term[:seq], add_rounded(left_term[seq:], far_right)])
    from_left, from_right = shift(right_term, dx=1), shift(left_term, dx=-1)
    up, down = up_down(qkv_term, far_halves[1], True)
    up, down, other, from_left, from_right, across_sum = fence(up, down, other, from_left, from_right, across_sum)
    mine = (shift(up, dz=1), shift(down, dz=-1))
    other = qkv_term(0, False, [(0, other[0]), (0, other[1])])
    other_got = shift(other, dylo=1)

    d_normed = add(own_term, from_left, from_right, across_sum)
    scaled = d_normed * gain
    sums = jnp.stack([jnp.sum(scaled, axis=-1), jnp.sum(scaled * standardized, axis=-1)])
    means = sum_over_mp(sums) / (8 * shard)
    gain_gradient = sum_over_dp(jnp.sum(d_normed * standardized, axis=0).reshape(6, -1)).reshape(shard)
    back = inverse_deviation * (scaled - means[0][:, None] - standardized * means[1][:, None])
    input_grad = (cotangent.astype(F32) + back).astype(BF16)
    out_grad = out_term(0, True, [(0, out_mine[0]), (0, out_mine[1]), (0, out_other_got)])[0]
    input_grad, out_grad, mine, other_got = fence(input_grad, out_grad, mine, other_got)

    qkv_grad = qkv_term(0, True, [(0, mine[0]), (0, mine[1]), (0, other_got)])
    return input_grad, jnp.transpose(qkv_grad, (1, 0, 2)), out_grad, gain_gradient


def solution(mesh):
    in_specs = (P("dp", "mp"), P("dp", "mp"), P(), P(None, None, "mp"), P("mp", None))
    out_specs = (P("dp", "mp"), P("dp", None, "mp"), P("mp", "dp"), P("mp"))
    return jax.shard_map(body, mesh=mesh, in_specs=in_specs, out_specs=out_specs, check_vma=False)
```

```python
import functools

import jax
import jax.numpy as jnp
from jax import lax
from jax.experimental import pallas as pl
from jax.experimental.pallas import tpu as pltpu
from jax.sharding import PartitionSpec as P

HEAD = 128
SEQ = 256
AXES = ("dp", "mp")
F32 = jnp.float32
BF16 = jnp.bfloat16


def place(index):
    dp, mp = divmod(index, 8)
    return mp // 2, (mp % 2) * 2 + (dp // 2) % 2, dp // 4, dp % 2


def index_of(x, y, z, core):
    x, y, z = x % 4, y % 4, z % 4
    return (z * 4 + (y % 2) * 2 + core) * 8 + x * 2 + y // 2


def shift(value, dx=0, dyhi=0, dylo=0, dz=0, dcore=0):
    pairs = []
    for index in range(128):
        x, y, z, core = place(index)
        pairs.append((index, index_of(x + dx, y ^ (2 * dyhi) ^ dylo, z + dz, core ^ dcore)))
    return lax.ppermute(value, AXES, pairs)


def fence(*values):
    return lax.optimization_barrier(values)


def dot(a, b, ca, cb):
    return lax.dot_general(a, b, (((ca,), (cb,)), ((), ())), preferred_element_type=F32)


def add(*terms):
    return sum(t.astype(F32) for t in terms)


def add_rounded(*terms):
    return add(*terms).astype(BF16)


def head_norm(values):
    centered = values - jnp.mean(values, axis=-1, keepdims=True)
    scale = lax.rsqrt(jnp.mean(centered * centered, axis=-1, keepdims=True) + 1e-06)
    return centered * scale, scale


def head_norm_grad(grad, normalized, scale):
    return scale * (
        grad
        - jnp.mean(grad, axis=-1, keepdims=True)
        - normalized * jnp.mean(grad * normalized, axis=-1, keepdims=True)
    )


def forward_kernel(q_ref, k_ref, v_ref, attn_ref, probs_ref):
    for head in range(3):
        columns = slice(head * HEAD, (head + 1) * HEAD)
        q_b = head_norm(q_ref[:, columns])[0].astype(BF16)
        k_b = head_norm(k_ref[:, columns])[0].astype(BF16)
        weights = jnp.exp(dot(q_b, k_b, 1, 1) * (1.0 / HEAD**0.5))
        probs = weights / jnp.sum(weights, axis=-1, keepdims=True)
        probs_ref[0, head] = probs
        attn_ref[columns, :] = dot(probs.astype(BF16), v_ref[:, columns].astype(BF16), 1, 0).T.astype(BF16)


def backward_kernel(q_ref, k_ref, v_ref, probs_ref, d_attn_ref, grad_ref):
    for head in range(3):
        columns = slice(head * HEAD, (head + 1) * HEAD)
        q_n, q_scale = head_norm(q_ref[:, columns])
        k_n, k_scale = head_norm(k_ref[:, columns])
        v_b = v_ref[:, columns].astype(BF16)
        probs = probs_ref[0, head]
        d_attn = d_attn_ref[:, columns].astype(BF16)
        d_probs = dot(d_attn, v_b, 1, 1)
        grad_ref[2, :, columns] = dot(probs.astype(BF16), d_attn, 0, 0).astype(BF16)
        delta = jnp.sum(probs * d_probs, axis=-1, keepdims=True)
        d_scores = (probs * (d_probs - delta) * (1.0 / HEAD**0.5)).astype(BF16)
        d_qn = dot(d_scores, k_n.astype(BF16), 1, 0)
        d_kn = dot(d_scores, q_n.astype(BF16), 0, 0)
        grad_ref[0, :, columns] = head_norm_grad(d_qn, q_n, q_scale).astype(BF16)
        grad_ref[1, :, columns] = head_norm_grad(d_kn, k_n, k_scale).astype(BF16)


ROW_BLOCK = pl.BlockSpec((SEQ, 3 * HEAD), lambda i: (i, 0))
PROBS_BLOCK = pl.BlockSpec((1, 3, SEQ, SEQ), lambda i: (i, 0, 0, 0))
PARAMS = pltpu.CompilerParams(vmem_limit_bytes=32 * 2**20)


def attention_forward(q, k, v):
    rows, width = q.shape
    return pl.pallas_call(
        forward_kernel,
        grid=(rows // SEQ,),
        in_specs=[ROW_BLOCK] * 3,
        out_specs=[pl.BlockSpec((width, SEQ), lambda i: (0, i)), PROBS_BLOCK],
        out_shape=[
            jax.ShapeDtypeStruct((width, rows), BF16),
            jax.ShapeDtypeStruct((rows // SEQ, 3, SEQ, SEQ), F32),
        ],
        compiler_params=PARAMS,
        cost_estimate=pl.CostEstimate(flops=10**9, bytes_accessed=5 * 10**6, transcendentals=4 * 10**5),
    )(q, k, v)


def attention_backward(q, k, v, probs, d_attn):
    rows, width = q.shape
    return pl.pallas_call(
        backward_kernel,
        grid=(rows // SEQ,),
        in_specs=[ROW_BLOCK] * 3 + [PROBS_BLOCK, ROW_BLOCK],
        out_specs=pl.BlockSpec((3, SEQ, width), lambda i: (0, i, 0)),
        out_shape=jax.ShapeDtypeStruct((3, rows, width), BF16),
        compiler_params=PARAMS,
        cost_estimate=pl.CostEstimate(flops=2 * 10**9, bytes_accessed=8 * 10**6, transcendentals=0),
    )(q, k, v, probs, d_attn)


def cost(flops, moved):
    return pl.CostEstimate(flops=int(flops), bytes_accessed=int(moved), transcendentals=0)


def whole(array):
    return pl.BlockSpec(array.shape, lambda i, place: (0,) * array.ndim)


def own_half(core, half, mine):
    return pl.ds(pl.multiple_of((core if mine else 1 - core) * half, HEAD), half)


ANYWHERE = pl.BlockSpec(memory_space=pl.ANY)


def pack_kernel(count, place_ref, *refs):
    kept_ref, given_ref = refs[-2:]
    core, half = place_ref[count], kept_ref.shape[1]
    for step in range(count):

        @pl.when(pl.program_id(0) == step)
        def _():
            kept_ref[0] = refs[step][:, own_half(core, half, True)].T
            given_ref[0] = refs[step][:, own_half(core, half, False)].T


def pack(chunks, place, buffers):
    count = len(chunks)
    rows, width = chunks[0].shape
    block = (1, width // 2, rows)
    return pl.pallas_call(
        functools.partial(pack_kernel, count),
        grid_spec=pltpu.PrefetchScalarGridSpec(
            num_scalar_prefetch=1,
            grid=(count,),
            in_specs=[whole(c) for c in chunks] + [ANYWHERE] * len(buffers),
            out_specs=[pl.BlockSpec(block, lambda i, place: (place[i], 0, 0))] * 2,
        ),
        out_shape=[jax.ShapeDtypeStruct((8,) + block[1:], BF16)] * 2,
        input_output_aliases={count + 1: 0, count + 2: 1} if buffers else {},
        compiler_params=PARAMS,
        cost_estimate=cost(0, 4 * count * rows * width),
    )(place, *chunks, *buffers)


def cotangent_kernel(count, has_weight, has_total, has_attn, place_ref, *refs):
    chunks, refs = refs[:count], list(refs[count:])
    weight_ref = refs.pop(0) if has_weight else None
    total_in_ref = refs.pop(0) if has_total else None
    attn_ref = refs.pop(0) if has_attn else None
    total_ref = refs[-3] if has_weight and has_attn else refs[-1]
    core = place_ref[count]
    for step in range(count):

        @pl.when(pl.program_id(0) == step)
        def _():
            if has_weight:
                term = dot(chunks[step][...], weight_ref[...], 1, 1)
                if step:
                    total_ref[...] += term
                else:
                    total_ref[...] = total_in_ref[...] + term if has_total else term
            if has_attn:
                half = refs[-1].shape[2]
                for ref, mine in ((refs[-2], True), (refs[-1], False)):
                    ref[0] = dot(attn_ref[...], chunks[step][:, own_half(core, half, mine)], 1, 0).astype(BF16)


def cotangent_terms(chunks, place, w_out=None, total=None, attn_t=None, buffers=()):
    count = len(chunks)
    rows, width = chunks[0].shape
    heads = (w_out if w_out is not None else attn_t).shape[0]
    operands, in_specs = list(chunks), [whole(c) for c in chunks]
    out_specs, out_shape = [], []
    flops = 0
    if w_out is not None:
        operands.append(w_out)
        in_specs.append(pl.BlockSpec((heads, width), lambda i, place: (0, place[i])))
        out_shape.append(jax.ShapeDtypeStruct((rows, heads), F32))
        out_specs.append(whole(out_shape[-1]))
        flops += count * 2 * rows * width * heads
    if total is not None:
        operands.append(total)
        in_specs.append(whole(total))
    aliases = {}
    if attn_t is not None:
        operands.append(attn_t)
        in_specs.append(whole(attn_t))
        if buffers:
            aliases = {1 + len(operands) + i: len(out_shape) + i for i in range(2)}
            operands += buffers
            in_specs += [ANYWHERE] * 2
        out_specs += [pl.BlockSpec((1, heads, width // 2), lambda i, place: (place[i], 0, 0))] * 2
        out_shape += [jax.ShapeDtypeStruct((8, heads, width // 2), BF16)] * 2
        flops += count * 2 * rows * width * heads
    return pl.pallas_call(
        functools.partial(cotangent_kernel, count, w_out is not None, total is not None, attn_t is not None),
        grid_spec=pltpu.PrefetchScalarGridSpec(
            num_scalar_prefetch=1, grid=(count,), in_specs=in_specs, out_specs=out_specs
        ),
        out_shape=out_shape,
        input_output_aliases=aliases,
        compiler_params=PARAMS,
        cost_estimate=cost(flops, count * (2 * rows * width + 4 * heads * width)),
    )(place, *operands)


def normed_kernel(count, place_ref, grad_ref, weight_ref, *out_refs):
    for step in range(count):

        @pl.when(pl.program_id(0) == step)
        def _():
            out_refs[step][...] = sum(dot(grad_ref[j], weight_ref[j], 1, 1) for j in range(3)).astype(BF16)


def normed_terms(d_qkv, weights, place, shard):
    count = place.shape[0]
    _, rows, columns = d_qkv.shape
    out_shape = [jax.ShapeDtypeStruct((rows, shard), BF16)] * count
    return pl.pallas_call(
        functools.partial(normed_kernel, count),
        grid_spec=pltpu.PrefetchScalarGridSpec(
            num_scalar_prefetch=1,
            grid=(count,),
            in_specs=[whole(d_qkv), pl.BlockSpec((3, shard, columns), lambda i, place: (0, place[i], 0))],
            out_specs=[whole(s) for s in out_shape],
        ),
        out_shape=out_shape,
        compiler_params=PARAMS,
        cost_estimate=cost(count * 6 * rows * shard * columns, count * (6 * shard * columns + 2 * rows * shard)),
    )(place, d_qkv, weights)


def block_kernel(place_ref, left_ref, left_got_ref, right_ref, right_got_ref, *out_refs):
    size = out_refs[0].shape[2]
    for j in range(3):
        total = dot(left_ref[0], right_ref[j], 1, 0) + dot(left_got_ref[0], right_got_ref[j], 1, 0)
        for part, ref in enumerate(out_refs):
            ref[0, j] = total[part * size : (part + 1) * size].astype(BF16)


def qkv_blocks(place, left, right, parts):
    count = place.shape[0]
    _, size, rows = left[0].shape
    columns = right[0].shape[2]
    block = (1, 3, size // parts, columns)
    return pl.pallas_call(
        block_kernel,
        grid_spec=pltpu.PrefetchScalarGridSpec(
            num_scalar_prefetch=1,
            grid=(count,),
            in_specs=[pl.BlockSpec((1, size, rows), lambda i, place: (place[i], 0, 0))] * 2 + [whole(r) for r in right],
            out_specs=[pl.BlockSpec(block, lambda i, place: (i, 0, 0, 0))] * parts,
        ),
        out_shape=[jax.ShapeDtypeStruct((count,) + block[1:], BF16)] * parts,
        compiler_params=PARAMS,
        cost_estimate=cost(count * 12 * size * rows * columns, count * (4 * size * rows + 6 * size * columns)),
    )(place, *left, *right)


def add_first(block, part):
    half = part.shape[-2]
    return jnp.concatenate([add_rounded(block[..., :half, :], part), block[..., half:, :]], axis=-2)


def add_last(block, part):
    half = part.shape[-2]
    return jnp.concatenate([block[..., :half, :], add_rounded(block[..., half:, :], part)], axis=-2)


def body(inputs, cotangent, layer_norm_gain, w_qkv, w_out):
    rows, shard = inputs.shape
    dp, mp = lax.axis_index("dp"), lax.axis_index("mp")
    x, yhi = mp // 2, mp % 2
    z, ylo, core = dp // 4, (dp // 2) % 2, dp % 2
    seq = SEQ

    def chunk_at(key):
        return lax.rem(x + key[0], 4) * 2 + lax.rem(yhi + key[1], 2)

    def places(keys):
        return jnp.stack([chunk_at(key) for key in keys] + [core])

    def pick(chunks, keys):
        return [chunks[key] for key in keys]

    weights = jnp.transpose(w_qkv, (1, 0, 2))

    def add_qkv(totals, chunks, keys):
        for key in keys:
            terms = [
                dot(chunks[key], lax.dynamic_slice(weights, (j, chunk_at(key) * shard, 0), (1, shard, weights.shape[2]))[0], 1, 0)
                for j in range(3)
            ]
            totals = terms if totals is None else [a + b for a, b in zip(totals, terms)]
        return totals

    own, left, right, across, far = (0, 0), (3, 0), (1, 0), (0, 1), (2, 0)
    near = [own, left, right, across]
    last = [(3, 1), (1, 1), (2, 1)]

    x_rows = inputs.astype(F32)
    mean = jnp.mean(x_rows, axis=-1)
    spread = jnp.sum(jnp.square(x_rows - mean[:, None]), axis=-1)
    own_stats = jnp.stack([mean, spread])

    def joined(parts, count):
        joined_mean = sum(p[0] for p in parts) / len(parts)
        joined_spread = sum(p[1] + count * jnp.square(p[0] - joined_mean) for p in parts)
        return jnp.stack([joined_mean, joined_spread])

    other_stats = shift(own_stats, dyhi=1)
    other_stats, ct_y = fence(other_stats, cotangent)
    pair = joined([own_stats, other_stats], float(shard))
    others = [shift(pair, dx=1), shift(pair, dx=-1), shift(pair, dx=2)]
    others, ct_x = fence(others, cotangent)
    ct = {own: cotangent, left: shift(ct_x, dx=1), right: shift(ct_x, dx=-1), across: shift(ct_y, dyhi=1)}
    stats = joined([pair] + others, 2.0 * shard)
    inverse_deviation = lax.rsqrt(stats[1] / (8 * shard) + 1e-06)[:, None]
    standardized = (x_rows - stats[0][:, None]) * inverse_deviation
    gain = lax.dynamic_slice_in_dim(layer_norm_gain, mp * shard, shard, 0)
    normed_own = (standardized * gain).astype(BF16)
    normed = {
        own: normed_own,
        left: shift(normed_own, dx=1),
        right: shift(normed_own, dx=-1),
        across: shift(normed_own, dyhi=1),
    }
    qkv = add_qkv(None, normed, [own])
    d_attn = cotangent_terms(pick(ct, near), places(near), w_out=w_out)[0]
    ct, normed, qkv, d_attn = fence(ct, normed, qkv, d_attn)

    normed[far] = jnp.concatenate([shift(normed[left][:seq], dx=1), shift(normed[right][seq:], dx=-1)])
    ct[far] = jnp.concatenate([shift(ct[left][:seq], dx=1), shift(ct[right][seq:], dx=-1)])
    qkv = add_qkv(qkv, normed, [left, right, across])
    packs = pack(pick(normed, near), places(near), ())
    normed, ct, qkv, packs = fence(normed, ct, qkv, packs)

    normed[3, 1], normed[1, 1] = shift(normed[across], dx=1), shift(normed[across], dx=-1)
    normed[2, 1] = shift(normed[far], dyhi=1)
    qkv = add_qkv(qkv, normed, [far])
    packs = pack([normed[far]], places([far]), packs)
    d_attn = cotangent_terms([ct[far]], places([far]), w_out=w_out, total=d_attn)[0]
    normed, ct, qkv, packs, d_attn = fence(normed, ct, qkv, packs, d_attn)

    ct[3, 1], ct[1, 1] = shift(ct[across], dx=1), shift(ct[across], dx=-1)
    ct[2, 1] = shift(ct[far], dyhi=1)
    q, k, v = add_qkv(qkv, normed, last)
    attn_t, probs = attention_forward(q, k, v)
    packs = pack(pick(normed, last), places(last), packs)
    normed_sides = (packs[0], shift(packs[1], dcore=1))
    out_sides = cotangent_terms(pick(ct, near + [far]), places(near + [far]), attn_t=attn_t)
    ct, q, k, v, attn_t, probs, normed_sides, out_sides = fence(ct, q, k, v, attn_t, probs, normed_sides, out_sides)

    d_attn, *out_sides = cotangent_terms(pick(ct, last), places(last), w_out, d_attn, attn_t, out_sides)
    out_kept, out_got = out_sides[0], shift(out_sides[1], dcore=1)
    d_qkv = attention_backward(q, k, v, probs, d_attn)
    d_qkv, out_got = fence(d_qkv, out_got)

    def along_z(dz):
        return lax.rem(z + dz, 4) * 2

    def out_pair(dz):
        pairs = [lax.dynamic_slice_in_dim(side, along_z(dz), 2, 0) for side in (out_kept, out_got)]
        return add_rounded(*pairs)

    def block_places(dzs):
        return jnp.stack([along_z(dz) + e for dz, e in dzs])

    qkv_sides = (d_qkv, shift(d_qkv, dcore=1))
    first_keys = [(2, 1), (1, 1), (3, 1)]
    far_across, left_across, right_across = normed_terms(d_qkv, weights, places(first_keys)[:3], shard)
    far_blocks = qkv_blocks(block_places([(2, 1 - ylo), (2, ylo)]), normed_sides, qkv_sides, 2)
    out_far = out_pair(2)
    out_far = [out_far[:, : out_far.shape[1] // 2], out_far[:, out_far.shape[1] // 2 :]]
    qkv_sides, far_across, left_across, right_across, far_blocks, out_far = fence(
        qkv_sides, far_across, left_across, right_across, far_blocks, out_far
    )

    far_across, left_across, right_across = (
        shift(far_across, dyhi=1),
        shift(left_across, dx=1),
        shift(right_across, dx=-1),
    )
    out_far = [shift(out_far[0], dz=1), shift(out_far[1], dz=-1)]
    far_blocks = [shift(far_blocks[0], dz=1), shift(far_blocks[1], dz=-1)]
    terms = normed_terms(d_qkv, weights, places([far, across, right, left, own])[:5], shard)
    blocks = qkv_blocks(
        block_places([(1, 1 - ylo), (3, 1 - ylo), (1, ylo), (3, ylo), (0, 1 - ylo), (0, ylo)]), normed_sides, qkv_sides, 1
    )[0]
    out_up, out_down, out_own = out_pair(1), out_pair(3), out_pair(0)
    far_across, left_across, right_across, out_far, far_blocks, terms, blocks, out_up, out_down, out_own = fence(
        far_across, left_across, right_across, out_far, far_blocks, terms, blocks, out_up, out_down, out_own
    )

    far_term, across_term, right_term, left_term, own_term = terms
    far_term = add_rounded(far_term, far_across)
    far_left, far_right = shift(far_term[:seq], dx=1), shift(far_term[seq:], dx=-1)
    across_sum = shift(add_rounded(across_term, left_across, right_across), dyhi=1)
    up, down = add_first(blocks[0], far_blocks[0][0]), add_last(blocks[1], far_blocks[1][0])
    other = (shift(up, dz=1), shift(down, dz=-1))
    out_up, out_down = shift(add_first(out_up, out_far[0]), dz=1), shift(add_last(out_down, out_far[1]), dz=-1)
    far_left, far_right = fence(far_left, far_right)
    from_left, from_right = shift(add_first(right_term, far_left), dx=1), shift(add_last(left_term, far_right), dx=-1)
    up, down = add_first(blocks[2], far_blocks[0][1]), add_last(blocks[3], far_blocks[1][1])

    d_normed = add(own_term, from_left, from_right, across_sum)
    scaled = d_normed * gain
    sums = jnp.stack([jnp.sum(scaled, axis=-1), jnp.sum(scaled * standardized, axis=-1)])
    sums = sums + shift(sums, dyhi=1)
    gain_sum = jnp.sum(d_normed * standardized, axis=0).reshape(6, -1)
    gain_sum = gain_sum + shift(gain_sum, dcore=1)
    gain_sum = gain_sum + shift(gain_sum, dylo=1)
    up, down, other, out_up, out_down, sums, gain_sum = fence(up, down, other, out_up, out_down, sums, gain_sum)

    mine = (shift(up, dz=1), shift(down, dz=-1))
    other_got = shift(add_rounded(blocks[4], *other), dylo=1)
    out_total = add_rounded(out_own, out_up, out_down)
    out_mine = lax.dynamic_index_in_dim(out_total, ylo, 0, keepdims=False)
    out_other = lax.dynamic_index_in_dim(out_total, 1 - ylo, 0, keepdims=False)
    out_grad = add_rounded(out_mine, shift(out_other, dylo=1))

    means = (sums + shift(sums, dx=1) + shift(sums, dx=-1) + shift(sums, dx=2)) / (8 * shard)
    gain_gradient = (gain_sum + shift(gain_sum, dz=1) + shift(gain_sum, dz=-1) + shift(gain_sum, dz=2)).reshape(shard)
    back = inverse_deviation * (scaled - means[0][:, None] - standardized * means[1][:, None])
    input_grad = (cotangent.astype(F32) + back).astype(BF16)
    qkv_grad = add_rounded(blocks[5], *mine, other_got)
    return input_grad, jnp.transpose(qkv_grad, (1, 0, 2)), out_grad, gain_gradient


def solution(mesh):
    in_specs = (P("dp", "mp"), P("dp", "mp"), P(), P(None, None, "mp"), P("mp", None))
    out_specs = (P("dp", "mp"), P("dp", None, "mp"), P("mp", "dp"), P("mp"))
    return jax.shard_map(body, mesh=mesh, in_specs=in_specs, out_specs=out_specs, check_vma=False)
```

```python
import functools

import jax
import jax.numpy as jnp
from jax import lax
from jax.experimental import pallas as pl
from jax.experimental.pallas import tpu as pltpu
from jax.sharding import PartitionSpec as P

HEAD = 128
SEQ = 256
AXES = ("dp", "mp")
F32 = jnp.float32
BF16 = jnp.bfloat16


def place(index):
    dp, mp = divmod(index, 8)
    return mp // 2, (mp % 2) * 2 + (dp // 2) % 2, dp // 4, dp % 2


def index_of(x, y, z, core):
    x, y, z = x % 4, y % 4, z % 4
    return (z * 4 + (y % 2) * 2 + core) * 8 + x * 2 + y // 2


def shift(value, dx=0, dyhi=0, dylo=0, dz=0, dcore=0):
    pairs = []
    for index in range(128):
        x, y, z, core = place(index)
        pairs.append((index, index_of(x + dx, y ^ (2 * dyhi) ^ dylo, z + dz, core ^ dcore)))
    return lax.ppermute(value, AXES, pairs)


def fence(*values):
    return lax.optimization_barrier(values)


def dot(a, b, ca, cb):
    return lax.dot_general(a, b, (((ca,), (cb,)), ((), ())), preferred_element_type=F32)


def add(*terms):
    return sum(t.astype(F32) for t in terms)


def add_rounded(*terms):
    return add(*terms).astype(BF16)


def head_norm(values):
    centered = values - jnp.mean(values, axis=-1, keepdims=True)
    scale = lax.rsqrt(jnp.mean(centered * centered, axis=-1, keepdims=True) + 1e-06)
    return centered * scale, scale


def head_norm_grad(grad, normalized, scale):
    return scale * (
        grad
        - jnp.mean(grad, axis=-1, keepdims=True)
        - normalized * jnp.mean(grad * normalized, axis=-1, keepdims=True)
    )


def forward_kernel(qkv_ref, attn_ref, probs_ref):
    for head in range(3):
        columns = slice(head * HEAD, (head + 1) * HEAD)
        q_b = head_norm(qkv_ref[0, :, columns])[0].astype(BF16)
        k_b = head_norm(qkv_ref[1, :, columns])[0].astype(BF16)
        weights = jnp.exp(dot(q_b, k_b, 1, 1) * (1.0 / HEAD**0.5))
        probs = weights / jnp.sum(weights, axis=-1, keepdims=True)
        probs_ref[0, head] = probs
        attn_ref[columns, :] = dot(probs.astype(BF16), qkv_ref[2, :, columns].astype(BF16), 1, 0).T.astype(BF16)


def weight_copies(place_ref, weights_ref, held_ref, sems):
    count, _, shard, _ = held_ref.shape
    return [
        pltpu.make_async_copy(
            weights_ref.at[:, pl.ds(pl.multiple_of(place_ref[key] * shard, shard), shard), :],
            held_ref.at[key],
            sems.at[key],
        )
        for key in range(count)
    ]


def tail_kernel(count, place_ref, *refs):
    chunks, refs = refs[:count], refs[count:]
    outs, refs = refs[:count], refs[count:]
    total_ref, qkv_ref, probs_ref, weights_ref, grad_ref, *term_refs = refs[:-2]
    held_ref, sems = refs[-2:]
    first = pl.program_id(0) == 0

    @pl.when(first)
    def _():
        for copy in weight_copies(place_ref, weights_ref, held_ref, sems):
            copy.start()

    d_attn_all = total_ref[...] + sum(dot(c[...], w[...], 1, 1) for c, w in zip(chunks, outs))
    d_attn_all = d_attn_all.astype(BF16)
    for head in range(3):
        columns = slice(head * HEAD, (head + 1) * HEAD)
        q_n, q_scale = head_norm(qkv_ref[0, :, columns])
        k_n, k_scale = head_norm(qkv_ref[1, :, columns])
        v_b = qkv_ref[2, :, columns].astype(BF16)
        probs = probs_ref[0, head]
        d_attn = d_attn_all[:, columns]
        d_probs = dot(d_attn, v_b, 1, 1)
        grad_ref[2, :, columns] = dot(probs.astype(BF16), d_attn, 0, 0).astype(BF16)
        delta = jnp.sum(probs * d_probs, axis=-1, keepdims=True)
        d_scores = (probs * (d_probs - delta) * (1.0 / HEAD**0.5)).astype(BF16)
        d_qn = dot(d_scores, k_n.astype(BF16), 1, 0)
        d_kn = dot(d_scores, q_n.astype(BF16), 0, 0)
        grad_ref[0, :, columns] = head_norm_grad(d_qn, q_n, q_scale).astype(BF16)
        grad_ref[1, :, columns] = head_norm_grad(d_kn, k_n, k_scale).astype(BF16)

    @pl.when(first)
    def _():
        for copy in weight_copies(place_ref, weights_ref, held_ref, sems):
            copy.wait()

    for key, ref in enumerate(term_refs):
        ref[...] = sum(dot(grad_ref[j], held_ref[key, j], 1, 1) for j in range(3)).astype(BF16)


PROBS_BLOCK = pl.BlockSpec((1, 3, SEQ, SEQ), lambda i, *_: (i, 0, 0, 0))
PARAMS = pltpu.CompilerParams(vmem_limit_bytes=40 * 2**20)


def attention_forward(qkv):
    _, rows, width = qkv.shape
    return pl.pallas_call(
        forward_kernel,
        grid=(rows // SEQ,),
        in_specs=[pl.BlockSpec((3, SEQ, width), lambda i: (0, i, 0))],
        out_specs=[pl.BlockSpec((width, SEQ), lambda i: (0, i)), PROBS_BLOCK],
        out_shape=[
            jax.ShapeDtypeStruct((width, rows), BF16),
            jax.ShapeDtypeStruct((rows // SEQ, 3, SEQ, SEQ), F32),
        ],
        compiler_params=PARAMS,
        cost_estimate=pl.CostEstimate(flops=10**9, bytes_accessed=5 * 10**6, transcendentals=4 * 10**5),
    )(qkv)


def attention_tail(chunks, chunk_places, w_out, total, qkv, probs, weights, term_places):
    _, rows, width = qkv.shape
    shard, count, terms = chunks[0].shape[1], len(chunks), len(term_places)
    row_block = lambda columns: pl.BlockSpec((SEQ, columns), lambda i, place: (i, 0))
    qkv_block = pl.BlockSpec((3, SEQ, width), lambda i, place: (0, i, 0))
    out_blocks = [
        pl.BlockSpec((width, shard), functools.partial(lambda at, i, place: (0, place[at]), terms + key)) for key in range(count)
    ]
    return pl.pallas_call(
        functools.partial(tail_kernel, count),
        grid_spec=pltpu.PrefetchScalarGridSpec(
            num_scalar_prefetch=1,
            grid=(rows // SEQ,),
            in_specs=[row_block(shard)] * count
            + out_blocks
            + [row_block(width), qkv_block, PROBS_BLOCK, pl.BlockSpec(memory_space=pl.ANY)],
            out_specs=[qkv_block] + [row_block(shard)] * terms,
            scratch_shapes=[pltpu.VMEM((terms, 3, shard, width), BF16), pltpu.SemaphoreType.DMA((terms,))],
        ),
        out_shape=[jax.ShapeDtypeStruct((3, rows, width), BF16)] + [jax.ShapeDtypeStruct((rows, shard), BF16)] * terms,
        compiler_params=PARAMS,
        cost_estimate=pl.CostEstimate(flops=6 * 10**9, bytes_accessed=20 * 10**6, transcendentals=0),
    )(jnp.stack(term_places + chunk_places), *chunks, *[w_out] * count, total, qkv, probs, weights)


def qkv_kernel(count, has_total, place_ref, *refs):
    chunks, (weight_ref, *_, total_ref) = refs[:count], refs[count:]
    for step in range(count):

        @pl.when(pl.program_id(0) == step)
        def _():
            for j in range(3):
                term = dot(chunks[step][...], weight_ref[j], 1, 0)
                if step:
                    total_ref[j] += term
                else:
                    total_ref[j] = refs[count + 1][j] + term if has_total else term


def qkv_terms(chunks, place, weights, total=None):
    count = len(chunks)
    rows, shard = chunks[0].shape
    columns = weights.shape[2]
    out = jax.ShapeDtypeStruct((3, rows, columns), F32)
    totals = [] if total is None else [total]
    return pl.pallas_call(
        functools.partial(qkv_kernel, count, bool(totals)),
        grid_spec=pltpu.PrefetchScalarGridSpec(
            num_scalar_prefetch=1,
            grid=(count,),
            in_specs=[whole(c) for c in chunks]
            + [pl.BlockSpec((3, shard, columns), lambda i, place: (0, place[i], 0))]
            + [whole(t) for t in totals],
            out_specs=whole(out),
        ),
        out_shape=out,
        compiler_params=PARAMS,
        cost_estimate=cost(count * 6 * rows * shard * columns, count * (6 * shard * columns + 2 * rows * shard)),
    )(place, *chunks, weights, *totals)


def cost(flops, moved):
    return pl.CostEstimate(flops=int(flops), bytes_accessed=int(moved), transcendentals=0)


def whole(array):
    return pl.BlockSpec(array.shape, lambda i, place: (0,) * array.ndim)


def own_half(core, half, mine):
    return pl.ds(pl.multiple_of((core if mine else 1 - core) * half, HEAD), half)


ANYWHERE = pl.BlockSpec(memory_space=pl.ANY)


def pack_kernel(count, place_ref, *refs):
    kept_ref, given_ref = refs[-2:]
    core, half = place_ref[count], kept_ref.shape[1]
    for step in range(count):

        @pl.when(pl.program_id(0) == step)
        def _():
            kept_ref[0] = refs[step][:, own_half(core, half, True)].T
            given_ref[0] = refs[step][:, own_half(core, half, False)].T


def pack(chunks, place, buffers):
    count = len(chunks)
    rows, width = chunks[0].shape
    block = (1, width // 2, rows)
    return pl.pallas_call(
        functools.partial(pack_kernel, count),
        grid_spec=pltpu.PrefetchScalarGridSpec(
            num_scalar_prefetch=1,
            grid=(count,),
            in_specs=[whole(c) for c in chunks] + [ANYWHERE] * len(buffers),
            out_specs=[pl.BlockSpec(block, lambda i, place: (place[i], 0, 0))] * 2,
        ),
        out_shape=[jax.ShapeDtypeStruct((8,) + block[1:], BF16)] * 2,
        input_output_aliases={count + 1: 0, count + 2: 1} if buffers else {},
        compiler_params=PARAMS,
        cost_estimate=cost(0, 4 * count * rows * width),
    )(place, *chunks, *buffers)


def cotangent_kernel(count, has_weight, has_total, has_attn, place_ref, *refs):
    chunks, refs = refs[:count], list(refs[count:])
    weight_ref = refs.pop(0) if has_weight else None
    total_in_ref = refs.pop(0) if has_total else None
    attn_ref = refs.pop(0) if has_attn else None
    total_ref = refs[-3] if has_weight and has_attn else refs[-1]
    core = place_ref[count]
    for step in range(count):

        @pl.when(pl.program_id(0) == step)
        def _():
            if has_weight:
                term = dot(chunks[step][...], weight_ref[...], 1, 1)
                if step:
                    total_ref[...] += term
                else:
                    total_ref[...] = total_in_ref[...] + term if has_total else term
            if has_attn:
                half = refs[-1].shape[2]
                for ref, mine in ((refs[-2], True), (refs[-1], False)):
                    ref[0] = dot(attn_ref[...], chunks[step][:, own_half(core, half, mine)], 1, 0).astype(BF16)


def cotangent_terms(chunks, place, w_out=None, total=None, attn_t=None, buffers=()):
    count = len(chunks)
    rows, width = chunks[0].shape
    heads = (w_out if w_out is not None else attn_t).shape[0]
    operands, in_specs = list(chunks), [whole(c) for c in chunks]
    out_specs, out_shape = [], []
    flops = 0
    if w_out is not None:
        operands.append(w_out)
        in_specs.append(pl.BlockSpec((heads, width), lambda i, place: (0, place[i])))
        out_shape.append(jax.ShapeDtypeStruct((rows, heads), F32))
        out_specs.append(whole(out_shape[-1]))
        flops += count * 2 * rows * width * heads
    if total is not None:
        operands.append(total)
        in_specs.append(whole(total))
    aliases = {}
    if attn_t is not None:
        operands.append(attn_t)
        in_specs.append(whole(attn_t))
        if buffers:
            aliases = {1 + len(operands) + i: len(out_shape) + i for i in range(2)}
            operands += buffers
            in_specs += [ANYWHERE] * 2
        out_specs += [pl.BlockSpec((1, heads, width // 2), lambda i, place: (place[i], 0, 0))] * 2
        out_shape += [jax.ShapeDtypeStruct((8, heads, width // 2), BF16)] * 2
        flops += count * 2 * rows * width * heads
    return pl.pallas_call(
        functools.partial(cotangent_kernel, count, w_out is not None, total is not None, attn_t is not None),
        grid_spec=pltpu.PrefetchScalarGridSpec(
            num_scalar_prefetch=1, grid=(count,), in_specs=in_specs, out_specs=out_specs
        ),
        out_shape=out_shape,
        input_output_aliases=aliases,
        compiler_params=PARAMS,
        cost_estimate=cost(flops, count * (2 * rows * width + 4 * heads * width)),
    )(place, *operands)


def normed_kernel(count, place_ref, grad_ref, weight_ref, *out_refs):
    for step in range(count):

        @pl.when(pl.program_id(0) == step)
        def _():
            out_refs[step][...] = sum(dot(grad_ref[j], weight_ref[j], 1, 1) for j in range(3)).astype(BF16)


def normed_terms(d_qkv, weights, place, shard):
    count = place.shape[0]
    _, rows, columns = d_qkv.shape
    out_shape = [jax.ShapeDtypeStruct((rows, shard), BF16)] * count
    return pl.pallas_call(
        functools.partial(normed_kernel, count),
        grid_spec=pltpu.PrefetchScalarGridSpec(
            num_scalar_prefetch=1,
            grid=(count,),
            in_specs=[whole(d_qkv), pl.BlockSpec((3, shard, columns), lambda i, place: (0, place[i], 0))],
            out_specs=[whole(s) for s in out_shape],
        ),
        out_shape=out_shape,
        compiler_params=PARAMS,
        cost_estimate=cost(count * 6 * rows * shard * columns, count * (6 * shard * columns + 2 * rows * shard)),
    )(place, d_qkv, weights)


def block_kernel(place_ref, left_ref, left_got_ref, right_ref, right_got_ref, *out_refs):
    size = out_refs[0].shape[2]
    for j in range(3):
        total = dot(left_ref[0], right_ref[j], 1, 0) + dot(left_got_ref[0], right_got_ref[j], 1, 0)
        for part, ref in enumerate(out_refs):
            ref[0, j] = total[part * size : (part + 1) * size].astype(BF16)


def qkv_blocks(place, left, right, parts):
    count = place.shape[0]
    _, size, rows = left[0].shape
    columns = right[0].shape[2]
    block = (1, 3, size // parts, columns)
    return pl.pallas_call(
        block_kernel,
        grid_spec=pltpu.PrefetchScalarGridSpec(
            num_scalar_prefetch=1,
            grid=(count,),
            in_specs=[pl.BlockSpec((1, size, rows), lambda i, place: (place[i], 0, 0))] * 2 + [whole(r) for r in right],
            out_specs=[pl.BlockSpec(block, lambda i, place: (i, 0, 0, 0))] * parts,
        ),
        out_shape=[jax.ShapeDtypeStruct((count,) + block[1:], BF16)] * parts,
        compiler_params=PARAMS,
        cost_estimate=cost(count * 12 * size * rows * columns, count * (4 * size * rows + 6 * size * columns)),
    )(place, *left, *right)


def add_first(block, part):
    half = part.shape[-2]
    return jnp.concatenate([add_rounded(block[..., :half, :], part), block[..., half:, :]], axis=-2)


def add_last(block, part):
    half = part.shape[-2]
    return jnp.concatenate([block[..., :half, :], add_rounded(block[..., half:, :], part)], axis=-2)


def body(inputs, cotangent, layer_norm_gain, w_qkv, w_out):
    rows, shard = inputs.shape
    dp, mp = lax.axis_index("dp"), lax.axis_index("mp")
    x, yhi = mp // 2, mp % 2
    z, ylo, core = dp // 4, (dp // 2) % 2, dp % 2
    seq = SEQ

    def chunk_at(key):
        return lax.rem(x + key[0], 4) * 2 + lax.rem(yhi + key[1], 2)

    def places(keys):
        return jnp.stack([chunk_at(key) for key in keys] + [core])

    def pick(chunks, keys):
        return [chunks[key] for key in keys]

    weights = jnp.transpose(w_qkv, (1, 0, 2))
    own, left, right, across, far = (0, 0), (3, 0), (1, 0), (0, 1), (2, 0)
    near = [own, left, right, across]
    last = [(3, 1), (1, 1), (2, 1)]

    def first_steps(value):
        return {own: value, left: shift(value, dx=1), right: shift(value, dx=-1), across: shift(value, dyhi=1)}

    def pass_halves(chunks):
        chunks[far] = jnp.concatenate([shift(chunks[left][:seq], dx=1), shift(chunks[right][seq:], dx=-1)])

    def last_steps(chunks):
        chunks[3, 1], chunks[1, 1] = shift(chunks[across], dx=1), shift(chunks[across], dx=-1)
        chunks[2, 1] = shift(chunks[far], dyhi=1)

    raw, ct = first_steps(inputs), first_steps(cotangent)
    x_rows = inputs.astype(F32)
    mean = jnp.mean(x_rows, axis=-1)
    spread = jnp.sum(jnp.square(x_rows - mean[:, None]), axis=-1)
    own_stats = jnp.stack([mean, spread])

    def joined(parts, count):
        joined_mean = sum(p[0] for p in parts) / len(parts)
        joined_spread = sum(p[1] + count * jnp.square(p[0] - joined_mean) for p in parts)
        return jnp.stack([joined_mean, joined_spread])

    pair = joined([own_stats, shift(own_stats, dyhi=1)], float(shard))
    raw, ct, pair = fence(raw, ct, pair)

    stats = joined([pair, shift(pair, dx=1), shift(pair, dx=-1), shift(pair, dx=2)], 2.0 * shard)
    pass_halves(raw)
    pass_halves(ct)
    d_attn = cotangent_terms(pick(ct, near), places(near), w_out=w_out)[0]
    raw, ct, stats, d_attn = fence(raw, ct, stats, d_attn)
    stats_mean = stats[0][:, None]
    inverse_deviation = lax.rsqrt(stats[1] / (8 * shard) + 1e-06)[:, None]

    def standardize(chunk):
        return (chunk.astype(F32) - stats_mean) * inverse_deviation

    def gain_at(key):
        return lax.dynamic_slice_in_dim(layer_norm_gain, chunk_at(key) * shard, shard, 0)

    def normalize(chunks, keys):
        return [(standardize(chunks[key]) * gain_at(key)).astype(BF16) for key in keys]

    last_steps(raw)
    normed = normalize(raw, near + [far])
    qkv = qkv_terms(normed, places(near + [far]), weights)
    packs = pack(normed, places(near + [far]), ())
    d_attn = cotangent_terms([ct[far]], places([far]), w_out=w_out, total=d_attn)[0]
    raw, ct, qkv, packs, d_attn = fence(raw, ct, qkv, packs, d_attn)

    last_steps(ct)
    normed = normalize(raw, last)
    qkv = qkv_terms(normed, places(last), weights, qkv)
    attn_t, probs = attention_forward(qkv)
    packs = pack(normed, places(last), packs)
    normed_sides = (packs[0], shift(packs[1], dcore=1))
    out_sides = cotangent_terms(pick(ct, near + [far]), places(near + [far]), attn_t=attn_t)
    ct, qkv, attn_t, probs, normed_sides, out_sides = fence(ct, qkv, attn_t, probs, normed_sides, out_sides)

    d_qkv, far_across, left_across, right_across = attention_tail(
        pick(ct, last),
        [chunk_at(key) for key in last],
        w_out,
        d_attn,
        qkv,
        probs,
        weights,
        [chunk_at(key) for key in [(2, 1), (1, 1), (3, 1)]],
    )
    ct, d_qkv, far_across, left_across, right_across = fence(ct, d_qkv, far_across, left_across, right_across)

    def along_z(dz):
        return lax.rem(z + dz, 4) * 2

    def block_places(dzs):
        return jnp.stack([along_z(dz) + e for dz, e in dzs])

    far_across, left_across, right_across = (
        shift(far_across, dyhi=1),
        shift(left_across, dx=1),
        shift(right_across, dx=-1),
    )
    qkv_sides = (d_qkv, shift(d_qkv, dcore=1))
    out_kept, out_given = cotangent_terms(pick(ct, last), places(last), attn_t=attn_t, buffers=out_sides)
    far_blocks = qkv_blocks(block_places([(2, 1 - ylo), (2, ylo)]), normed_sides, qkv_sides, 2)
    far_blocks = [shift(far_blocks[0], dz=1), shift(far_blocks[1], dz=-1)]
    terms = normed_terms(d_qkv, weights, places([far, across, right, left, own])[:5], shard)
    blocks = qkv_blocks(
        block_places([(1, 1 - ylo), (3, 1 - ylo), (1, ylo), (3, ylo), (0, 1 - ylo), (0, ylo)]), normed_sides, qkv_sides, 1
    )[0]
    far_across, left_across, right_across, far_blocks, terms, blocks, out_kept, out_given = fence(
        far_across, left_across, right_across, far_blocks, terms, blocks, out_kept, out_given
    )

    far_term, across_term, right_term, left_term, own_term = terms
    far_term = add_rounded(far_term, far_across)
    far_left, far_right = shift(far_term[:seq], dx=1), shift(far_term[seq:], dx=-1)
    across_sum = shift(add_rounded(across_term, left_across, right_across), dyhi=1)
    up, down = add_first(blocks[0], far_blocks[0][0]), add_last(blocks[1], far_blocks[1][0])
    other = (shift(up, dz=1), shift(down, dz=-1))
    out_got = shift(out_given, dcore=1)
    far_left, far_right, across_sum, other, out_got, far_blocks = fence(
        far_left, far_right, across_sum, other, out_got, far_blocks
    )

    def out_pair(dz):
        return add_rounded(*[lax.dynamic_slice_in_dim(side, along_z(dz), 2, 0) for side in (out_kept, out_got)])

    from_left, from_right = shift(add_first(right_term, far_left), dx=1), shift(add_last(left_term, far_right), dx=-1)
    up, down = add_first(blocks[2], far_blocks[0][1]), add_last(blocks[3], far_blocks[1][1])
    mine = (shift(up, dz=1), shift(down, dz=-1))
    other_got = shift(add_rounded(blocks[4], *other), dylo=1)
    out_far = out_pair(2)
    half = out_far.shape[1] // 2
    out_far = [shift(out_far[:, :half], dz=1), shift(out_far[:, half:], dz=-1)]
    out_up, out_down, out_own = out_pair(1), out_pair(3), out_pair(0)
    from_left, from_right, mine, other_got, out_far, out_up, out_down, out_own = fence(
        from_left, from_right, mine, other_got, out_far, out_up, out_down, out_own
    )

    gain = gain_at(own)
    standardized = standardize(inputs)
    d_normed = add(own_term, from_left, from_right, across_sum)
    scaled = d_normed * gain
    sums = jnp.stack([jnp.sum(scaled, axis=-1), jnp.sum(scaled * standardized, axis=-1)])
    sums = sums + shift(sums, dyhi=1)
    gain_sum = jnp.sum(d_normed * standardized, axis=0).reshape(6, -1)
    gain_sum = gain_sum + shift(gain_sum, dcore=1)
    gain_sum = gain_sum + shift(gain_sum, dylo=1)
    means = (sums + shift(sums, dx=1) + shift(sums, dx=-1) + shift(sums, dx=2)) / (8 * shard)
    out_up, out_down = shift(add_first(out_up, out_far[0]), dz=1), shift(add_last(out_down, out_far[1]), dz=-1)
    qkv_grad = add_rounded(blocks[5], *mine, other_got)
    out_up, out_down, means, gain_sum, qkv_grad = fence(out_up, out_down, means, gain_sum, qkv_grad)

    out_total = add_rounded(out_own, out_up, out_down)
    out_mine = lax.dynamic_index_in_dim(out_total, ylo, 0, keepdims=False)
    out_other = lax.dynamic_index_in_dim(out_total, 1 - ylo, 0, keepdims=False)
    out_grad = add_rounded(out_mine, shift(out_other, dylo=1))
    gain_gradient = (gain_sum + shift(gain_sum, dz=1) + shift(gain_sum, dz=-1) + shift(gain_sum, dz=2)).reshape(shard)
    back = inverse_deviation * (scaled - means[0][:, None] - standardized * means[1][:, None])
    input_grad = (cotangent.astype(F32) + back).astype(BF16)
    return input_grad, jnp.transpose(qkv_grad, (1, 0, 2)), out_grad, gain_gradient


def solution(mesh):
    in_specs = (P("dp", "mp"), P("dp", "mp"), P(), P(None, None, "mp"), P("mp", None))
    out_specs = (P("dp", "mp"), P("dp", None, "mp"), P("mp", "dp"), P("mp"))
    return jax.shard_map(body, mesh=mesh, in_specs=in_specs, out_specs=out_specs, check_vma=False)
```

```python
import functools

import jax
import jax.numpy as jnp
from jax import lax
from jax.experimental import pallas as pl
from jax.experimental.pallas import tpu as pltpu
from jax.sharding import PartitionSpec as P

HEAD = 128
SEQ = 256
AXES = ("dp", "mp")
F32 = jnp.float32
BF16 = jnp.bfloat16


def place(index):
    dp, mp = divmod(index, 8)
    return mp // 2, (mp % 2) * 2 + (dp // 2) % 2, dp // 4, dp % 2


def index_of(x, y, z, core):
    x, y, z = x % 4, y % 4, z % 4
    return (z * 4 + (y % 2) * 2 + core) * 8 + x * 2 + y // 2


def shift(value, dx=0, dyhi=0, dylo=0, dz=0, dcore=0):
    pairs = []
    for index in range(128):
        x, y, z, core = place(index)
        pairs.append((index, index_of(x + dx, y ^ (2 * dyhi) ^ dylo, z + dz, core ^ dcore)))
    return lax.ppermute(value, AXES, pairs)


def fence(*values):
    return lax.optimization_barrier(values)


def dot(a, b, ca, cb):
    return lax.dot_general(a, b, (((ca,), (cb,)), ((), ())), preferred_element_type=F32)


def add(*terms):
    return sum(t.astype(F32) for t in terms)


def add_rounded(*terms):
    return add(*terms).astype(BF16)


def head_norm(values):
    centered = values - jnp.mean(values, axis=-1, keepdims=True)
    scale = lax.rsqrt(jnp.mean(centered * centered, axis=-1, keepdims=True) + 1e-06)
    return centered * scale, scale


def head_norm_grad(grad, normalized, scale):
    return scale * (
        grad
        - jnp.mean(grad, axis=-1, keepdims=True)
        - normalized * jnp.mean(grad * normalized, axis=-1, keepdims=True)
    )


FREE = pl.CostEstimate(flops=0, bytes_accessed=0, transcendentals=0)
PARAMS = pltpu.CompilerParams(vmem_limit_bytes=60 * 2**20)


def whole(array):
    return pl.BlockSpec(array.shape, lambda i, table: (0,) * array.ndim)


def by_core(core, values):
    half = values.shape[1] // 2
    low, high = values[:, :half], values[:, half:]
    return jnp.where(core == 0, low, high), jnp.where(core == 0, high, low)


OWN, LEFT, RIGHT, ACROSS, FAR = (0, 0), (3, 0), (1, 0), (0, 1), (2, 0)
KEYS = [OWN, LEFT, RIGHT, ACROSS, FAR, (2, 1), (1, 1), (3, 1)]
CORE, FAR_BLOCKS, OTHER_BLOCKS, LAST_BLOCKS = 8, 9, 11, 13


def front_kernel(table_ref, *refs):
    chunks, (weight_ref, gain_ref) = refs[:8], refs[8:10]
    total_ref, kept_ref, given_ref, mean_ref, scale_ref, attn_ref, probs_ref = refs[10:]
    rows, shard = chunks[0].shape
    step = pl.program_id(0)

    @pl.when(step == 0)
    def _():
        @pl.loop(0, rows // 64)
        def _(index):
            at = pl.ds(pl.multiple_of(index * 64, 64), 64)
            total = sum(c[at, :].astype(F32) for c in chunks)
            mean = jnp.sum(total, axis=-1, keepdims=True) / (8 * shard)
            spread = sum(jnp.square(c[at, :].astype(F32) - mean) for c in chunks)
            variance = jnp.sum(spread, axis=-1, keepdims=True) / (8 * shard)
            mean_ref[at, :] = mean
            scale_ref[at, :] = lax.rsqrt(variance + 1e-06)

    for key in range(8):

        @pl.when(step == key)
        def _():
            standardized = (chunks[key][...].astype(F32) - mean_ref[...]) * scale_ref[...]
            normed = (standardized * gain_ref[0]).astype(BF16)
            for j in range(3):
                term = dot(normed, weight_ref[j], 1, 0)
                if key:
                    total_ref[j] += term
                else:
                    total_ref[j] = term
            kept_ref[0], given_ref[0] = by_core(table_ref[CORE], normed)

    @pl.when(step == 7)
    def _():
        for image in range(rows // SEQ):
            at = slice(image * SEQ, (image + 1) * SEQ)
            for head in range(3):
                columns = slice(head * HEAD, (head + 1) * HEAD)
                q_b = head_norm(total_ref[0, at, columns])[0].astype(BF16)
                k_b = head_norm(total_ref[1, at, columns])[0].astype(BF16)
                weights = jnp.exp(dot(q_b, k_b, 1, 1) * (1.0 / HEAD**0.5))
                probs = weights / jnp.sum(weights, axis=-1, keepdims=True)
                probs_ref[image, head] = probs
                values = total_ref[2, at, columns].astype(BF16)
                attn_ref[at, columns] = dot(probs.astype(BF16), values, 1, 0).astype(BF16)


def front(table, chunks, weights, gain):
    rows, shard = chunks[0].shape
    columns = weights.shape[2]
    half = jax.ShapeDtypeStruct((8, rows, shard // 2), BF16)
    column = jax.ShapeDtypeStruct((rows, 1), F32)
    qkv = jax.ShapeDtypeStruct((3, rows, columns), F32)
    attn = jax.ShapeDtypeStruct((rows, columns), BF16)
    probs = jax.ShapeDtypeStruct((rows // SEQ, 3, SEQ, SEQ), F32)
    half_block = pl.BlockSpec((1, rows, shard // 2), lambda i, table: (table[i], 0, 0))
    return pl.pallas_call(
        front_kernel,
        grid_spec=pltpu.PrefetchScalarGridSpec(
            num_scalar_prefetch=1,
            grid=(8,),
            in_specs=[whole(c) for c in chunks]
            + [
                pl.BlockSpec((3, shard, columns), lambda i, table: (0, table[i], 0)),
                pl.BlockSpec((1, 1, shard), lambda i, table: (table[i], 0, 0)),
            ],
            out_specs=[whole(qkv), half_block, half_block, whole(column), whole(column), whole(attn), whole(probs)],
        ),
        out_shape=[qkv, half, half, column, column, attn, probs],
        compiler_params=PARAMS,
        cost_estimate=FREE,
    )(table, *chunks, weights, gain.reshape(8, 1, shard))


def near_kernel(table_ref, *refs):
    chunks, (weight_ref, total_ref) = refs[:4], refs[4:]
    for step in range(4):

        @pl.when(pl.program_id(0) == step)
        def _():
            term = dot(chunks[step][...], weight_ref[...], 1, 1)
            if step:
                total_ref[...] += term
            else:
                total_ref[...] = term


def near_d_attn(table, chunks, w_out):
    rows, shard = chunks[0].shape
    heads = w_out.shape[0]
    out = jax.ShapeDtypeStruct((rows, heads), F32)
    return pl.pallas_call(
        near_kernel,
        grid_spec=pltpu.PrefetchScalarGridSpec(
            num_scalar_prefetch=1,
            grid=(4,),
            in_specs=[whole(c) for c in chunks] + [pl.BlockSpec((heads, shard), lambda i, table: (0, table[i]))],
            out_specs=whole(out),
        ),
        out_shape=out,
        compiler_params=PARAMS,
        cost_estimate=FREE,
    )(table, *chunks, w_out)


def tail_kernel(table_ref, weight_ref, attn_ref, total_ref, *refs):
    sources, (grad_ref, kept_ref, given_ref) = refs[:10], refs[10:13]
    chunk_buffer, qkv_ref, probs_ref, sum_ref, sems = refs[13:]
    rows = total_ref.shape[0]
    step = pl.program_id(0)
    targets = [chunk_buffer.at[i] for i in range(8)] + [qkv_ref, probs_ref]
    copies = [pltpu.make_async_copy(s, t, sems.at[i]) for i, (s, t) in enumerate(zip(sources, targets))]

    @pl.when(step == 0)
    def _():
        for copy in copies:
            copy.start()

    for index in range(8):

        @pl.when(step == index)
        def _():
            copies[index].wait()
            chunk = chunk_buffer[index]
            if index == 0:
                sum_ref[...] = total_ref[...] + dot(chunk, weight_ref[...], 1, 1)
            elif index < 4:
                sum_ref[...] += dot(chunk, weight_ref[...], 1, 1)
            term = dot(attn_ref[...], chunk, 0, 0).astype(BF16)
            kept_ref[0], given_ref[0] = by_core(table_ref[CORE], term)

    @pl.when(step == 4)
    def _():
        copies[8].wait()
        copies[9].wait()
        for image in range(rows // SEQ):
            at = slice(image * SEQ, (image + 1) * SEQ)
            for head in range(3):
                columns = slice(head * HEAD, (head + 1) * HEAD)
                q_n, q_scale = head_norm(qkv_ref[0, at, columns])
                k_n, k_scale = head_norm(qkv_ref[1, at, columns])
                v_b = qkv_ref[2, at, columns].astype(BF16)
                probs = probs_ref[image, head]
                d_attn = sum_ref[at, columns].astype(BF16)
                d_probs = dot(d_attn, v_b, 1, 1)
                grad_ref[2, at, columns] = dot(probs.astype(BF16), d_attn, 0, 0).astype(BF16)
                delta = jnp.sum(probs * d_probs, axis=-1, keepdims=True)
                d_scores = (probs * (d_probs - delta) * (1.0 / HEAD**0.5)).astype(BF16)
                d_qn = dot(d_scores, k_n.astype(BF16), 1, 0)
                d_kn = dot(d_scores, q_n.astype(BF16), 0, 0)
                grad_ref[0, at, columns] = head_norm_grad(d_qn, q_n, q_scale).astype(BF16)
                grad_ref[1, at, columns] = head_norm_grad(d_kn, k_n, k_scale).astype(BF16)


def tail(table, chunks, w_out, attn, total, qkv, probs):
    rows, shard = chunks[0].shape
    heads = w_out.shape[0]
    grad = jax.ShapeDtypeStruct(qkv.shape, BF16)
    half = jax.ShapeDtypeStruct((8, heads, shard // 2), BF16)
    at = lambda i, table: table[lax.rem(i + 4, 8)]
    half_block = pl.BlockSpec((1, heads, shard // 2), lambda i, table: (at(i, table), 0, 0))
    return pl.pallas_call(
        tail_kernel,
        grid_spec=pltpu.PrefetchScalarGridSpec(
            num_scalar_prefetch=1,
            grid=(8,),
            in_specs=[
                pl.BlockSpec((heads, shard), lambda i, table: (0, table[4 + jnp.minimum(i, 3)])),
                whole(attn),
                whole(total),
            ]
            + [pl.BlockSpec(memory_space=pl.ANY)] * 10,
            out_specs=[whole(grad), half_block, half_block],
            scratch_shapes=[
                pltpu.VMEM((8, rows, shard), BF16),
                pltpu.VMEM(qkv.shape, F32),
                pltpu.VMEM(probs.shape, F32),
                pltpu.VMEM((rows, heads), F32),
                pltpu.SemaphoreType.DMA((10,)),
            ],
        ),
        out_shape=[grad, half, half],
        compiler_params=PARAMS,
        cost_estimate=FREE,
    )(table, w_out, attn, total, *chunks[4:], *chunks[:4], qkv, probs)


def normed_kernel(table_ref, grad_ref, weight_ref, *out_refs):
    for step, ref in enumerate(out_refs):

        @pl.when(pl.program_id(0) == step)
        def _():
            ref[...] = sum(dot(grad_ref[j], weight_ref[j], 1, 1) for j in range(3)).astype(BF16)


def normed_terms(table, first, count, d_qkv, weights):
    _, rows, columns = d_qkv.shape
    shard = weights.shape[1] // 8
    out_shape = [jax.ShapeDtypeStruct((rows, shard), BF16)] * count
    return pl.pallas_call(
        normed_kernel,
        grid_spec=pltpu.PrefetchScalarGridSpec(
            num_scalar_prefetch=1,
            grid=(count,),
            in_specs=[whole(d_qkv), pl.BlockSpec((3, shard, columns), lambda i, table: (0, table[first + i], 0))],
            out_specs=[whole(s) for s in out_shape],
        ),
        out_shape=out_shape,
        compiler_params=PARAMS,
        cost_estimate=FREE,
    )(table, d_qkv, weights)


def block_kernel(table_ref, left_ref, left_got_ref, out_ref, out_got_ref, right_ref, right_got_ref, *out_refs):
    size = out_refs[0].shape[2]
    for j in range(4):
        if j < 3:
            total = dot(left_ref[0], right_ref[j], 0, 0) + dot(left_got_ref[0], right_got_ref[j], 0, 0)
        else:
            total = add(out_ref[0], out_got_ref[0])
        for part, ref in enumerate(out_refs):
            ref[0, j] = total[part * size : (part + 1) * size].astype(BF16)


def weight_blocks(table, first, count, left, out, right, parts=1):
    _, rows, size = left[0].shape
    columns = right[0].shape[2]
    block = (1, 4, size // parts, columns)
    at_place = lambda i, table: (table[first + i], 0, 0)
    return pl.pallas_call(
        block_kernel,
        grid_spec=pltpu.PrefetchScalarGridSpec(
            num_scalar_prefetch=1,
            grid=(count,),
            in_specs=[pl.BlockSpec((1, rows, size), at_place)] * 2
            + [pl.BlockSpec((1, size, columns), at_place)] * 2
            + [whole(r) for r in right],
            out_specs=[pl.BlockSpec(block, lambda i, table: (i, 0, 0, 0))] * parts,
        ),
        out_shape=[jax.ShapeDtypeStruct((count,) + block[1:], BF16)] * parts,
        compiler_params=PARAMS,
        cost_estimate=FREE,
    )(table, *left, *out, *right)


def split_kernel(first_ref, second_ref, first_half_ref, second_half_ref):
    first_half_ref[...] = first_ref[...]
    second_half_ref[...] = second_ref[...]


def split_halves(first, second):
    rows, width = first.shape
    half = (rows // 2, width)
    return pl.pallas_call(
        split_kernel,
        grid=(1,),
        in_specs=[pl.BlockSpec(half, functools.partial(lambda part, i: (part, 0), part)) for part in (0, 1)],
        out_specs=[pl.BlockSpec(half, lambda i: (0, 0))] * 2,
        out_shape=[jax.ShapeDtypeStruct(half, BF16)] * 2,
        compiler_params=PARAMS,
        cost_estimate=FREE,
    )(first, second)


def join_kernel(first_ref, second_ref, out_ref):
    half = first_ref.shape[0]
    out_ref[:half] = first_ref[...]
    out_ref[half:] = second_ref[...]


def join_halves(first, second):
    return pl.pallas_call(
        join_kernel,
        out_shape=jax.ShapeDtypeStruct((2 * first.shape[0], first.shape[1]), BF16),
        compiler_params=PARAMS,
        cost_estimate=FREE,
    )(first, second)


def add_first(block, part):
    half = part.shape[-2]
    return jnp.concatenate([add_rounded(block[..., :half, :], part), block[..., half:, :]], axis=-2)


def add_last(block, part):
    half = part.shape[-2]
    return jnp.concatenate([block[..., :half, :], add_rounded(block[..., half:, :], part)], axis=-2)


def body(inputs, cotangent, layer_norm_gain, w_qkv, w_out):
    shard = inputs.shape[1]
    dp, mp = lax.axis_index("dp"), lax.axis_index("mp")
    x, yhi = mp // 2, mp % 2
    z, ylo, core = dp // 4, (dp // 2) % 2, dp % 2
    weights = jnp.transpose(w_qkv, (1, 0, 2))
    places = [lax.rem(x + dx, 4) * 2 + lax.rem(yhi + dyhi, 2) for dx, dyhi in KEYS] + [core]
    for dz, e in [(2, 1 - ylo), (2, ylo), (1, 1 - ylo), (3, 1 - ylo), (1, ylo), (3, ylo), (0, 1 - ylo), (0, ylo)]:
        places.append(lax.rem(z + dz, 4) * 2 + e)
    table = jnp.stack(places)

    def first_steps(value):
        return {OWN: value, LEFT: shift(value, dx=1), RIGHT: shift(value, dx=-1), ACROSS: shift(value, dyhi=1)}

    def pick(chunks, keys=KEYS):
        return [chunks[key] for key in keys]

    raw, ct = first_steps(inputs), first_steps(cotangent)
    raw_halves = split_halves(raw[LEFT], raw[RIGHT])
    raw_halves = [shift(raw_halves[0], dx=1), shift(raw_halves[1], dx=-1)]
    raw[ACROSS], ct[LEFT], ct[RIGHT] = fence(raw[ACROSS], ct[LEFT], ct[RIGHT])
    raw[3, 1], raw[1, 1] = shift(raw[ACROSS], dx=1), shift(raw[ACROSS], dx=-1)
    ct_halves = split_halves(ct[LEFT], ct[RIGHT])
    ct_halves, raw_halves, ct = fence(ct_halves, raw_halves, ct)
    ct_halves = [shift(ct_halves[0], dx=1), shift(ct_halves[1], dx=-1)]
    raw[FAR] = join_halves(*raw_halves)
    raw[2, 1] = shift(raw[FAR], dyhi=1)
    d_attn = near_d_attn(table, pick(ct, KEYS[:4]), w_out)
    raw[3, 1], raw[1, 1], ct[ACROSS], d_attn = fence(raw[3, 1], raw[1, 1], ct[ACROSS], d_attn)
    ct[3, 1], ct[1, 1] = shift(ct[ACROSS], dx=1), shift(ct[ACROSS], dx=-1)
    ct[FAR] = join_halves(*ct_halves)
    raw, ct[FAR] = fence(raw, ct[FAR])
    ct[2, 1] = shift(ct[FAR], dyhi=1)
    qkv, *normed_sides, row_mean, row_scale, attn, probs = front(table, pick(raw), weights, layer_norm_gain)
    ct, qkv, normed_sides, attn, probs = fence(ct, qkv, normed_sides, attn, probs)

    normed_sides = (normed_sides[0], shift(normed_sides[1], dcore=1))
    d_qkv, *out_sides = tail(table, pick(ct), w_out, attn, d_attn, qkv, probs)
    d_qkv, out_sides, normed_sides = fence(d_qkv, out_sides, normed_sides)

    qkv_sides = (d_qkv, shift(d_qkv, dcore=1))
    out_sides = (out_sides[0], shift(out_sides[1], dcore=1))
    first_terms = normed_terms(table, 5, 3, d_qkv, weights)
    first_terms, out_sides, qkv_sides = fence(first_terms, out_sides, qkv_sides)
    far_blocks = weight_blocks(table, FAR_BLOCKS, 2, normed_sides, out_sides, qkv_sides, 2)
    first_terms, far_blocks, d_qkv, out_sides, qkv_sides = fence(first_terms, far_blocks, d_qkv, out_sides, qkv_sides)

    far_across, left_across, right_across = (
        shift(first_terms[0], dyhi=1),
        shift(first_terms[1], dx=1),
        shift(first_terms[2], dx=-1),
    )
    far_blocks = [shift(far_blocks[0], dz=1), shift(far_blocks[1], dz=-1)]
    own_term, left_term, right_term, across_term, far_term = normed_terms(table, 0, 5, d_qkv, weights)
    near_blocks = weight_blocks(table, OTHER_BLOCKS, 2, normed_sides, out_sides, qkv_sides)[0]
    far_across, left_across, right_across, far_blocks, near_blocks, far_term, across_term, qkv_sides = fence(
        far_across, left_across, right_across, far_blocks, near_blocks, far_term, across_term, qkv_sides
    )

    other = (shift(add_first(near_blocks[0], far_blocks[0][0]), dz=1), shift(add_last(near_blocks[1], far_blocks[1][0]), dz=-1))
    far_term = add_rounded(far_term, far_across)
    far_left, far_right = shift(far_term[:SEQ], dx=1), shift(far_term[SEQ:], dx=-1)
    across_sum = shift(add_rounded(across_term, left_across, right_across), dyhi=1)
    far_left, far_right, qkv_sides = fence(far_left, far_right, qkv_sides)
    from_left, from_right = shift(add_first(right_term, far_left), dx=1), shift(add_last(left_term, far_right), dx=-1)
    blocks = weight_blocks(table, LAST_BLOCKS, 4, normed_sides, out_sides, qkv_sides)[0]
    up, down = add_first(blocks[0], far_blocks[0][1]), add_last(blocks[1], far_blocks[1][1])
    other, up, down, across_sum, blocks, from_left, from_right = fence(
        other, up, down, across_sum, blocks, from_left, from_right
    )

    mine = (shift(up, dz=1), shift(down, dz=-1))
    other_got = shift(add_rounded(blocks[2], *other), dylo=1)
    gain = lax.dynamic_slice_in_dim(layer_norm_gain, mp * shard, shard, 0)
    standardized = (inputs.astype(F32) - row_mean) * row_scale
    d_normed = add(own_term, from_left, from_right, across_sum)
    scaled = d_normed * gain
    sums = jnp.stack([jnp.sum(scaled, axis=-1), jnp.sum(scaled * standardized, axis=-1)])
    sums = sums + shift(sums, dx=1) + shift(sums, dx=-1) + shift(sums, dx=2)
    gain_sum = jnp.sum(d_normed * standardized, axis=0).reshape(6, -1)
    gain_sum = gain_sum + shift(gain_sum, dcore=1)
    gain_sum = gain_sum + shift(gain_sum, dylo=1)
    means = (sums + shift(sums, dyhi=1)) / (8 * shard)
    mine, other_got, means, gain_sum = fence(mine, other_got, means, gain_sum)

    gain_gradient = (gain_sum + shift(gain_sum, dz=1) + shift(gain_sum, dz=-1) + shift(gain_sum, dz=2)).reshape(shard)
    back = row_scale * (scaled - means[0][:, None] - standardized * means[1][:, None])
    input_grad = (cotangent.astype(F32) + back).astype(BF16)
    total = add_rounded(blocks[3], *mine, other_got)
    return input_grad, jnp.transpose(total[:3], (1, 0, 2)), total[3], gain_gradient


def solution(mesh):
    in_specs = (P("dp", "mp"), P("dp", "mp"), P(), P(None, None, "mp"), P("mp", None))
    out_specs = (P("dp", "mp"), P("dp", None, "mp"), P("mp", "dp"), P("mp"))
    return jax.shard_map(body, mesh=mesh, in_specs=in_specs, out_specs=out_specs, check_vma=False)
```

```python
import functools

import jax
import jax.numpy as jnp
from jax import lax
from jax.experimental import pallas as pl
from jax.experimental.pallas import tpu as pltpu
from jax.sharding import PartitionSpec as P

HEAD = 128
SEQ = 256
AXES = ("dp", "mp")
F32 = jnp.float32
BF16 = jnp.bfloat16


def place(index):
    dp, mp = divmod(index, 8)
    return mp // 2, (mp % 2) * 2 + (dp // 2) % 2, dp // 4, dp % 2


def index_of(x, y, z, core):
    x, y, z = x % 4, y % 4, z % 4
    return (z * 4 + (y % 2) * 2 + core) * 8 + x * 2 + y // 2


def shift(value, dx=0, dyhi=0, dylo=0, dz=0, dcore=0):
    pairs = []
    for index in range(128):
        x, y, z, core = place(index)
        pairs.append((index, index_of(x + dx, y ^ (2 * dyhi) ^ dylo, z + dz, core ^ dcore)))
    return lax.ppermute(value, AXES, pairs)


def mirrored(flip):
    pairs = []
    for index in range(128):
        x, y, z, core = place(index)
        pairs.append((index, index_of(x, y, z ^ flip, core)))
    return pairs


def fence(*values):
    return lax.optimization_barrier(values)


def dot(a, b, ca, cb):
    return lax.dot_general(a, b, (((ca,), (cb,)), ((), ())), preferred_element_type=F32)


def add(*terms):
    return sum(t.astype(F32) for t in terms)


def add_rounded(*terms):
    return add(*terms).astype(BF16)


def head_norm(values):
    centered = values - jnp.mean(values, axis=-1, keepdims=True)
    scale = lax.rsqrt(jnp.mean(centered * centered, axis=-1, keepdims=True) + 1e-06)
    return centered * scale, scale


def head_norm_grad(grad, normalized, scale):
    return scale * (
        grad
        - jnp.mean(grad, axis=-1, keepdims=True)
        - normalized * jnp.mean(grad * normalized, axis=-1, keepdims=True)
    )


FREE = pl.CostEstimate(flops=0, bytes_accessed=0, transcendentals=0)
PARAMS = pltpu.CompilerParams(vmem_limit_bytes=60 * 2**20)


def whole(array):
    return pl.BlockSpec(array.shape, lambda i, table: (0,) * array.ndim)


def by_core(core, values):
    half = values.shape[1] // 2
    low, high = values[:, :half], values[:, half:]
    return jnp.where(core == 0, low, high), jnp.where(core == 0, high, low)


ANYWHERE = pl.BlockSpec(memory_space=pl.ANY)
OWN, LEFT, RIGHT, ACROSS, FAR = (0, 0), (3, 0), (1, 0), (0, 1), (2, 0)
KEYS = [OWN, LEFT, RIGHT, ACROSS, FAR, (2, 1), (1, 1), (3, 1)]
CORE, FAR_BLOCKS, NEXT_BLOCKS = 8, 9, 11


class Copies:
    def __init__(self, sems):
        self.sems, self.started = sems, []

    def start(self, source, target):
        copy = pltpu.make_async_copy(source, target, self.sems.at[len(self.started)])
        copy.start()
        self.started.append(copy)
        return copy


def rows_at(table_ref, index, size):
    return pl.ds(pl.multiple_of(table_ref[index] * size, size), size)


def front_kernel(table_ref, gain_ref, weights_ref, *refs):
    chunks, refs = refs[:8], refs[8:]
    kept_ref, given_ref, mean_ref, scale_ref, qkv_ref, scales_ref, attn_ref, probs_ref = refs[:8]
    chunk_buffer, weight_buffer, kept_buffer, given_buffer, total_ref, in_sems, out_sems = refs[8:]
    rows, shard = chunks[0].shape
    loads, stores = Copies(in_sems), Copies(out_sems)
    chunk_loads = [loads.start(chunks[i], chunk_buffer.at[i]) for i in range(8)]
    weight_loads = [
        loads.start(weights_ref.at[:, rows_at(table_ref, i, shard), :], weight_buffer.at[i]) for i in range(8)
    ]
    for load in chunk_loads:
        load.wait()

    @pl.loop(0, rows // 64)
    def _(index):
        at = pl.ds(pl.multiple_of(index * 64, 64), 64)
        total = sum(chunk_buffer[i, at, :].astype(F32) for i in range(8))
        mean = jnp.sum(total, axis=-1, keepdims=True) / (8 * shard)
        spread = sum(jnp.square(chunk_buffer[i, at, :].astype(F32) - mean) for i in range(8))
        variance = jnp.sum(spread, axis=-1, keepdims=True) / (8 * shard)
        mean_ref[at, :] = mean
        scale_ref[at, :] = lax.rsqrt(variance + 1e-06)

    for i in range(8):
        standardized = (chunk_buffer[i].astype(F32) - mean_ref[...]) * scale_ref[...]
        normed = (standardized * gain_ref[table_ref[i]]).astype(BF16)
        kept_buffer[i], given_buffer[i] = by_core(table_ref[CORE], normed)
        stores.start(kept_buffer.at[i], kept_ref.at[table_ref[i]])
        stores.start(given_buffer.at[i], given_ref.at[table_ref[i]])
        weight_loads[i].wait()
        for j in range(3):
            term = dot(normed, weight_buffer[i, j], 1, 0)
            if i:
                total_ref[j] += term
            else:
                total_ref[j] = term

    for image in range(rows // SEQ):
        at = slice(image * SEQ, (image + 1) * SEQ)
        for head in range(3):
            columns = slice(head * HEAD, (head + 1) * HEAD)
            q_n, scales_ref[at, head : head + 1] = head_norm(total_ref[0, at, columns])
            k_n, scales_ref[at, head + 3 : head + 4] = head_norm(total_ref[1, at, columns])
            q_b, k_b, v_b = q_n.astype(BF16), k_n.astype(BF16), total_ref[2, at, columns].astype(BF16)
            qkv_ref[0, at, columns], qkv_ref[1, at, columns], qkv_ref[2, at, columns] = q_b, k_b, v_b
            weights = jnp.exp(dot(q_b, k_b, 1, 1) * (1.0 / HEAD**0.5))
            probs = (weights / jnp.sum(weights, axis=-1, keepdims=True)).astype(BF16)
            probs_ref[image, head] = probs
            attn_ref[at, columns] = dot(probs, v_b, 1, 0).astype(BF16)
    for store in stores.started:
        store.wait()


def front(table, chunks, weights, gain):
    rows, shard = chunks[0].shape
    columns = weights.shape[2]
    half = jax.ShapeDtypeStruct((8, rows, shard // 2), BF16)
    column = jax.ShapeDtypeStruct((rows, 1), F32)
    qkv = jax.ShapeDtypeStruct((3, rows, columns), BF16)
    scales = jax.ShapeDtypeStruct((rows, 8), F32)
    attn = jax.ShapeDtypeStruct((rows, columns), BF16)
    probs = jax.ShapeDtypeStruct((rows // SEQ, 3, SEQ, SEQ), BF16)
    return pl.pallas_call(
        front_kernel,
        grid_spec=pltpu.PrefetchScalarGridSpec(
            num_scalar_prefetch=1,
            grid=(1,),
            in_specs=[whole(jax.ShapeDtypeStruct((8, 1, shard), F32))] + [ANYWHERE] * 9,
            out_specs=[ANYWHERE] * 2 + [whole(o) for o in (column, column, qkv, scales, attn, probs)],
            scratch_shapes=[
                pltpu.VMEM((8, rows, shard), BF16),
                pltpu.VMEM((8, 3, shard, columns), BF16),
                pltpu.VMEM(half.shape, BF16),
                pltpu.VMEM(half.shape, BF16),
                pltpu.VMEM(qkv.shape, F32),
                pltpu.SemaphoreType.DMA((16,)),
                pltpu.SemaphoreType.DMA((16,)),
            ],
        ),
        out_shape=[half, half, column, column, qkv, scales, attn, probs],
        compiler_params=PARAMS,
        cost_estimate=FREE,
    )(table, gain.reshape(8, 1, shard), weights, *chunks)


def near_kernel(table_ref, *refs):
    chunks, (weight_ref, total_ref) = refs[:4], refs[4:]
    for step in range(4):

        @pl.when(pl.program_id(0) == step)
        def _():
            term = dot(chunks[step][...], weight_ref[...], 1, 1)
            if step:
                total_ref[...] += term
            else:
                total_ref[...] = term


def near_d_attn(table, chunks, w_out):
    rows, shard = chunks[0].shape
    heads = w_out.shape[0]
    out = jax.ShapeDtypeStruct((rows, heads), F32)
    return pl.pallas_call(
        near_kernel,
        grid_spec=pltpu.PrefetchScalarGridSpec(
            num_scalar_prefetch=1,
            grid=(4,),
            in_specs=[whole(c) for c in chunks] + [pl.BlockSpec((heads, shard), lambda i, table: (0, table[i]))],
            out_specs=whole(out),
        ),
        out_shape=out,
        compiler_params=PARAMS,
        cost_estimate=FREE,
    )(table, *chunks, w_out)


def tail_kernel(table_ref, w_out_ref, attn_in, total_in, qkv_in, scales_in, probs_in, *refs):
    chunks, refs = refs[:8], refs[8:]
    grad_ref, kept_ref, given_ref = refs[:3]
    chunk_buffer, weight_buffer, attn_ref, total_ref, qkv_ref, scales_ref, probs_ref = refs[3:10]
    grad_buffer, kept_buffer, given_buffer, in_sems, out_sems = refs[10:]
    rows, shard = chunks[0].shape
    loads, stores = Copies(in_sems), Copies(out_sems)
    total_load = loads.start(total_in, total_ref)
    chunk_loads, weight_loads = {}, {}
    for i in range(4, 8):
        chunk_loads[i] = loads.start(chunks[i], chunk_buffer.at[i])
        columns = pl.ds(pl.multiple_of(table_ref[i] * shard, shard), shard)
        weight_loads[i] = loads.start(w_out_ref.at[:, columns], weight_buffer.at[i - 4])
    others = [
        loads.start(source, target)
        for source, target in ((qkv_in, qkv_ref), (scales_in, scales_ref), (probs_in, probs_ref), (attn_in, attn_ref))
    ]
    for i in range(4):
        chunk_loads[i] = loads.start(chunks[i], chunk_buffer.at[i])

    total_load.wait()
    for i in range(4, 8):
        chunk_loads[i].wait()
        weight_loads[i].wait()
        total_ref[...] += dot(chunk_buffer[i], weight_buffer[i - 4], 1, 1)
    for load in others:
        load.wait()
    for image in range(rows // SEQ):
        at = slice(image * SEQ, (image + 1) * SEQ)
        for head in range(3):
            columns = slice(head * HEAD, (head + 1) * HEAD)
            q_b, k_b, v_b = qkv_ref[0, at, columns], qkv_ref[1, at, columns], qkv_ref[2, at, columns]
            q_scale, k_scale = scales_ref[at, head : head + 1], scales_ref[at, head + 3 : head + 4]
            probs = probs_ref[image, head]
            d_attn = total_ref[at, columns].astype(BF16)
            d_probs = dot(d_attn, v_b, 1, 1)
            grad_buffer[2, at, columns] = dot(probs, d_attn, 0, 0).astype(BF16)
            probs = probs.astype(F32)
            delta = jnp.sum(probs * d_probs, axis=-1, keepdims=True)
            d_scores = (probs * (d_probs - delta) * (1.0 / HEAD**0.5)).astype(BF16)
            d_qn = dot(d_scores, k_b, 1, 0)
            d_kn = dot(d_scores, q_b, 0, 0)
            grad_buffer[0, at, columns] = head_norm_grad(d_qn, q_b.astype(F32), q_scale).astype(BF16)
            grad_buffer[1, at, columns] = head_norm_grad(d_kn, k_b.astype(F32), k_scale).astype(BF16)
    stores.start(grad_buffer, grad_ref)
    for i in (4, 5, 6, 7, 0, 1, 2, 3):
        if i < 4:
            chunk_loads[i].wait()
        term = dot(attn_ref[...], chunk_buffer[i], 0, 0).astype(BF16)
        kept_buffer[i], given_buffer[i] = by_core(table_ref[CORE], term)
        stores.start(kept_buffer.at[i], kept_ref.at[table_ref[i]])
        stores.start(given_buffer.at[i], given_ref.at[table_ref[i]])
    for store in stores.started:
        store.wait()


def tail(table, chunks, w_out, attn, total, qkv, scales, probs):
    rows, shard = chunks[0].shape
    heads = w_out.shape[0]
    grad = jax.ShapeDtypeStruct(qkv.shape, BF16)
    half = jax.ShapeDtypeStruct((8, heads, shard // 2), BF16)
    return pl.pallas_call(
        tail_kernel,
        grid_spec=pltpu.PrefetchScalarGridSpec(
            num_scalar_prefetch=1,
            grid=(1,),
            in_specs=[ANYWHERE] * 14,
            out_specs=[ANYWHERE] * 3,
            scratch_shapes=[
                pltpu.VMEM((8, rows, shard), BF16),
                pltpu.VMEM((4, heads, shard), BF16),
                pltpu.VMEM(attn.shape, BF16),
                pltpu.VMEM(total.shape, F32),
                pltpu.VMEM(qkv.shape, BF16),
                pltpu.VMEM(scales.shape, F32),
                pltpu.VMEM(probs.shape, BF16),
                pltpu.VMEM(grad.shape, BF16),
                pltpu.VMEM(half.shape, BF16),
                pltpu.VMEM(half.shape, BF16),
                pltpu.SemaphoreType.DMA((17,)),
                pltpu.SemaphoreType.DMA((17,)),
            ],
        ),
        out_shape=[grad, half, half],
        compiler_params=PARAMS,
        cost_estimate=FREE,
    )(table, w_out, attn, total, qkv, scales, probs, *chunks)


def normed_kernel(table_ref, grad_ref, weight_ref, *out_refs):
    for step, ref in enumerate(out_refs):

        @pl.when(pl.program_id(0) == step)
        def _():
            ref[...] = sum(dot(grad_ref[j], weight_ref[j], 1, 1) for j in range(3)).astype(BF16)


def normed_terms(table, first, count, d_qkv, weights):
    _, rows, columns = d_qkv.shape
    shard = weights.shape[1] // 8
    out_shape = [jax.ShapeDtypeStruct((rows, shard), BF16)] * count
    return pl.pallas_call(
        normed_kernel,
        grid_spec=pltpu.PrefetchScalarGridSpec(
            num_scalar_prefetch=1,
            grid=(count,),
            in_specs=[whole(d_qkv), pl.BlockSpec((3, shard, columns), lambda i, table: (0, table[first + i], 0))],
            out_specs=[whole(s) for s in out_shape],
        ),
        out_shape=out_shape,
        compiler_params=PARAMS,
        cost_estimate=FREE,
    )(table, d_qkv, weights)


def block_kernel(first, count, halves, table_ref, *refs):
    left, out, right = refs[0:2], refs[2:4], refs[4:6]
    out_refs, refs = refs[6 : 6 + (2 if halves else count)], refs[6 + (2 if halves else count) :]
    left_buffer, out_buffer, right_buffer, sum_buffer, in_sems, out_sems = refs
    size = sum_buffer.shape[2]
    loads, stores = Copies(in_sems), Copies(out_sems)
    for side in range(2):
        loads.start(right[side], right_buffer.at[side])
    for i in range(count):
        place = table_ref[first + i]
        for side in range(2):
            loads.start(left[side].at[place], left_buffer.at[i, side])
            loads.start(out[side].at[place], out_buffer.at[i, side])
    for load in loads.started[:2]:
        load.wait()
    for i in range(count):
        for load in loads.started[2 + 4 * i : 6 + 4 * i]:
            load.wait()
        for j in range(3):
            total = dot(left_buffer[i, 0], right_buffer[0, j], 0, 0) + dot(left_buffer[i, 1], right_buffer[1, j], 0, 0)
            sum_buffer[i, j] = total.astype(BF16)
        sum_buffer[i, 3] = add_rounded(out_buffer[i, 0], out_buffer[i, 1])
        if halves:
            for part in range(2):
                rows = pl.ds(part * (size // 2), size // 2)
                stores.start(sum_buffer.at[i, :, rows, :], out_refs[part].at[i])
        else:
            stores.start(sum_buffer.at[i], out_refs[i])
    for store in stores.started:
        store.wait()


def weight_blocks(table, first, count, left, out, right, halves=False):
    _, rows, size = left[0].shape
    columns = right[0].shape[2]
    if halves:
        out_shape = [jax.ShapeDtypeStruct((count, 4, size // 2, columns), BF16)] * 2
    else:
        out_shape = [jax.ShapeDtypeStruct((4, size, columns), BF16)] * count
    return pl.pallas_call(
        functools.partial(block_kernel, first, count, halves),
        grid_spec=pltpu.PrefetchScalarGridSpec(
            num_scalar_prefetch=1,
            grid=(1,),
            in_specs=[ANYWHERE] * 6,
            out_specs=[ANYWHERE] * len(out_shape),
            scratch_shapes=[
                pltpu.VMEM((count, 2, rows, size), BF16),
                pltpu.VMEM((count, 2, size, columns), BF16),
                pltpu.VMEM((2, 3, rows, columns), BF16),
                pltpu.VMEM((count, 4, size, columns), BF16),
                pltpu.SemaphoreType.DMA((2 + 4 * count,)),
                pltpu.SemaphoreType.DMA((count * (2 if halves else 1),)),
            ],
        ),
        out_shape=out_shape,
        compiler_params=PARAMS,
        cost_estimate=FREE,
    )(table, *left, *out, *right)


def split_kernel(first_ref, second_ref, first_half_ref, second_half_ref):
    first_half_ref[...] = first_ref[...]
    second_half_ref[...] = second_ref[...]


def split_halves(first, second):
    rows, width = first.shape
    half = (rows // 2, width)
    return pl.pallas_call(
        split_kernel,
        grid=(1,),
        in_specs=[pl.BlockSpec(half, functools.partial(lambda part, i: (part, 0), part)) for part in (0, 1)],
        out_specs=[pl.BlockSpec(half, lambda i: (0, 0))] * 2,
        out_shape=[jax.ShapeDtypeStruct(half, BF16)] * 2,
        compiler_params=PARAMS,
        cost_estimate=FREE,
    )(first, second)


def join_kernel(first_ref, second_ref, out_ref):
    half = first_ref.shape[0]
    out_ref[:half] = first_ref[...]
    out_ref[half:] = second_ref[...]


def join_halves(first, second):
    return pl.pallas_call(
        join_kernel,
        out_shape=jax.ShapeDtypeStruct((2 * first.shape[0], first.shape[1]), BF16),
        compiler_params=PARAMS,
        cost_estimate=FREE,
    )(first, second)


def add_kernel(up_ref, down_ref, from_left_ref, from_right_ref, up_out, down_out):
    up_out[...] = add_rounded(up_ref[...], from_left_ref[0])
    down_out[...] = add_rounded(down_ref[...], from_right_ref[0])


def add_halves(up, down, far, index):
    count, size, columns = up.shape
    part = (count, size // 2, columns)
    half = lambda which: pl.BlockSpec(part, lambda i: (0, which, 0))
    return pl.pallas_call(
        add_kernel,
        grid=(1,),
        in_specs=[half(0), half(1)] + [pl.BlockSpec((1,) + part, lambda i: (index, 0, 0, 0))] * 2,
        out_specs=[half(0), half(1)],
        out_shape=[jax.ShapeDtypeStruct(up.shape, BF16)] * 2,
        input_output_aliases={0: 0, 1: 1},
        compiler_params=PARAMS,
        cost_estimate=FREE,
    )(up, down, *far)


def add_first(block, part):
    half = part.shape[-2]
    return jnp.concatenate([add_rounded(block[..., :half, :], part), block[..., half:, :]], axis=-2)


def add_last(block, part):
    half = part.shape[-2]
    return jnp.concatenate([block[..., :half, :], add_rounded(block[..., half:, :], part)], axis=-2)


def body(inputs, cotangent, layer_norm_gain, w_qkv, w_out):
    shard = inputs.shape[1]
    dp, mp = lax.axis_index("dp"), lax.axis_index("mp")
    x, yhi = mp // 2, mp % 2
    z, ylo, core = dp // 4, (dp // 2) % 2, dp % 2
    weights = jnp.transpose(w_qkv, (1, 0, 2))
    places = [lax.rem(x + dx, 4) * 2 + lax.rem(yhi + dyhi, 2) for dx, dyhi in KEYS] + [core]
    for dz, e in [(2, 1 - ylo), (2, ylo), (1, 1 - ylo), (3, 1 - ylo), (1, ylo), (3, ylo), (0, 1 - ylo), (0, ylo)]:
        places.append(lax.rem(z + dz, 4) * 2 + e)
    table = jnp.stack(places)

    def first_steps(value):
        return {OWN: value, LEFT: shift(value, dx=1), RIGHT: shift(value, dx=-1), ACROSS: shift(value, dyhi=1)}

    def pick(chunks, keys=KEYS):
        return [chunks[key] for key in keys]

    raw, ct = first_steps(inputs), first_steps(cotangent)
    raw_halves = split_halves(raw[LEFT], raw[RIGHT])
    raw_halves = [shift(raw_halves[0], dx=1), shift(raw_halves[1], dx=-1)]
    raw[ACROSS], ct[LEFT], ct[RIGHT] = fence(raw[ACROSS], ct[LEFT], ct[RIGHT])
    raw[3, 1], raw[1, 1] = shift(raw[ACROSS], dx=1), shift(raw[ACROSS], dx=-1)
    ct_halves = split_halves(ct[LEFT], ct[RIGHT])
    ct_halves, raw_halves, ct = fence(ct_halves, raw_halves, ct)
    ct_halves = [shift(ct_halves[0], dx=1), shift(ct_halves[1], dx=-1)]
    raw[FAR] = join_halves(*raw_halves)
    raw[2, 1] = shift(raw[FAR], dyhi=1)
    d_attn = near_d_attn(table, pick(ct, KEYS[:4]), w_out)
    raw[3, 1], raw[1, 1], ct[ACROSS], d_attn = fence(raw[3, 1], raw[1, 1], ct[ACROSS], d_attn)
    ct[3, 1], ct[1, 1] = shift(ct[ACROSS], dx=1), shift(ct[ACROSS], dx=-1)
    ct[FAR] = join_halves(*ct_halves)
    raw, ct[FAR] = fence(raw, ct[FAR])
    ct[2, 1] = shift(ct[FAR], dyhi=1)
    *normed_sides, row_mean, row_scale, qkv, scales, attn, probs = front(table, pick(raw), weights, layer_norm_gain)
    ct, qkv, scales, normed_sides, attn, probs = fence(ct, qkv, scales, normed_sides, attn, probs)

    normed_sides = (normed_sides[0], shift(normed_sides[1], dcore=1))
    d_qkv, *out_sides = tail(table, pick(ct), w_out, attn, d_attn, qkv, scales, probs)
    d_qkv, out_sides, normed_sides = fence(d_qkv, out_sides, normed_sides)

    qkv_sides = (d_qkv, shift(d_qkv, dcore=1))
    out_sides = (out_sides[0], shift(out_sides[1], dcore=1))
    first_terms = normed_terms(table, 5, 3, d_qkv, weights)
    first_terms, out_sides, qkv_sides = fence(first_terms, out_sides, qkv_sides)
    far_blocks = weight_blocks(table, FAR_BLOCKS, 2, normed_sides, out_sides, qkv_sides, True)
    first_terms, far_blocks, d_qkv, out_sides, qkv_sides = fence(first_terms, far_blocks, d_qkv, out_sides, qkv_sides)

    far_across, left_across, right_across = (
        shift(first_terms[0], dyhi=1),
        shift(first_terms[1], dx=1),
        shift(first_terms[2], dx=-1),
    )
    far_blocks = [shift(far_blocks[0], dz=1), shift(far_blocks[1], dz=-1)]
    across_term, far_term = normed_terms(table, 3, 2, d_qkv, weights)
    blocks = weight_blocks(table, NEXT_BLOCKS, 6, normed_sides, out_sides, qkv_sides)
    far_across, left_across, right_across, far_blocks, blocks, far_term, across_term = fence(
        far_across, left_across, right_across, far_blocks, blocks, far_term, across_term
    )

    up, down = add_halves(blocks[0], blocks[1], far_blocks, 0)
    up, down, far_term, far_across, across_term = fence(up, down, far_term, far_across, across_term)
    other = (shift(up, dz=1), shift(down, dz=-1))
    far_term = add_rounded(far_term, far_across)
    far_left, far_right = shift(far_term[:SEQ], dx=1), shift(far_term[SEQ:], dx=-1)
    across_sum = shift(add_rounded(across_term, left_across, right_across), dyhi=1)
    far_left, far_right, d_qkv = fence(far_left, far_right, d_qkv)
    own_term, left_term, right_term = normed_terms(table, 0, 3, d_qkv, weights)
    up, down = add_halves(blocks[2], blocks[3], far_blocks, 1)
    right_term, left_term = add_first(right_term, far_left), add_last(left_term, far_right)
    other, across_sum, up, down, right_term, left_term = fence(other, across_sum, up, down, right_term, left_term)

    from_left, from_right = shift(right_term, dx=1), shift(left_term, dx=-1)
    mine = (shift(up, dz=1), shift(down, dz=-1))
    other_got = shift(add_rounded(blocks[4], *other), dylo=1)
    gain = lax.dynamic_slice_in_dim(layer_norm_gain, mp * shard, shard, 0)
    standardized = (inputs.astype(F32) - row_mean) * row_scale
    d_normed = add(own_term, from_left, from_right, across_sum)
    scaled = d_normed * gain
    sums = jnp.stack([jnp.sum(scaled, axis=-1), jnp.sum(scaled * standardized, axis=-1)])
    sums = sums + shift(sums, dx=1) + shift(sums, dx=-1) + shift(sums, dx=2)
    gain_sum = jnp.sum(d_normed * standardized, axis=0).reshape(6, -1)
    gain_sum = gain_sum + shift(gain_sum, dcore=1)
    gain_sum = gain_sum + lax.ppermute(gain_sum, AXES, mirrored(1))
    means = (sums + shift(sums, dyhi=1)) / (8 * shard)
    mine, other_got, means, gain_sum = fence(mine, other_got, means, gain_sum)

    gain_sum = gain_sum + lax.ppermute(gain_sum, AXES, mirrored(3))
    gain_gradient = (gain_sum + shift(gain_sum, dylo=1)).reshape(shard)
    back = row_scale * (scaled - means[0][:, None] - standardized * means[1][:, None])
    input_grad = (cotangent.astype(F32) + back).astype(BF16)
    total = add_rounded(blocks[5], *mine, other_got)
    return input_grad, jnp.transpose(total[:3], (1, 0, 2)), total[3], gain_gradient


def solution(mesh):
    in_specs = (P("dp", "mp"), P("dp", "mp"), P(), P(None, None, "mp"), P("mp", None))
    out_specs = (P("dp", "mp"), P("dp", None, "mp"), P("mp", "dp"), P("mp"))
    return jax.shard_map(body, mesh=mesh, in_specs=in_specs, out_specs=out_specs, check_vma=False)
```

```python
import functools

import jax
import jax.numpy as jnp
from jax import lax
from jax.experimental import pallas as pl
from jax.experimental.pallas import tpu as pltpu
from jax.sharding import PartitionSpec as P

HEAD = 128
SEQ = 256
AXES = ("dp", "mp")
F32 = jnp.float32
BF16 = jnp.bfloat16


def place(index):
    dp, mp = divmod(index, 8)
    return mp // 2, (mp % 2) * 2 + (dp // 2) % 2, dp // 4, dp % 2


def index_of(x, y, z, core):
    x, y, z = x % 4, y % 4, z % 4
    return (z * 4 + (y % 2) * 2 + core) * 8 + x * 2 + y // 2


def shift(value, dx=0, dyhi=0, dylo=0, dz=0, dcore=0):
    pairs = []
    for index in range(128):
        x, y, z, core = place(index)
        pairs.append((index, index_of(x + dx, y ^ (2 * dyhi) ^ dylo, z + dz, core ^ dcore)))
    return lax.ppermute(value, AXES, pairs)


def mirrored(flip):
    pairs = []
    for index in range(128):
        x, y, z, core = place(index)
        pairs.append((index, index_of(x, y, z ^ flip, core)))
    return pairs


def fence(*values):
    return lax.optimization_barrier(values)


def dot(a, b, ca, cb):
    return lax.dot_general(a, b, (((ca,), (cb,)), ((), ())), preferred_element_type=F32)


def add(*terms):
    return sum(t.astype(F32) for t in terms)


def add_rounded(*terms):
    return add(*terms).astype(BF16)


def head_norm(values):
    centered = values - jnp.mean(values, axis=-1, keepdims=True)
    scale = lax.rsqrt(jnp.mean(centered * centered, axis=-1, keepdims=True) + 1e-06)
    return centered * scale, scale


def head_norm_grad(grad, normalized, scale):
    return scale * (
        grad
        - jnp.mean(grad, axis=-1, keepdims=True)
        - normalized * jnp.mean(grad * normalized, axis=-1, keepdims=True)
    )


FREE = pl.CostEstimate(flops=0, bytes_accessed=0, transcendentals=0)
PARAMS = pltpu.CompilerParams(vmem_limit_bytes=60 * 2**20)


def whole(array):
    return pl.BlockSpec(array.shape, lambda i, table: (0,) * array.ndim)


def by_core(core, values):
    half = values.shape[1] // 2
    low, high = values[:, :half], values[:, half:]
    return jnp.where(core == 0, low, high), jnp.where(core == 0, high, low)


ANYWHERE = pl.BlockSpec(memory_space=pl.ANY)
OWN, LEFT, RIGHT, ACROSS, FAR = (0, 0), (3, 0), (1, 0), (0, 1), (2, 0)
KEYS = [OWN, LEFT, RIGHT, ACROSS, FAR, (2, 1), (1, 1), (3, 1)]
CORE, FAR_BLOCKS, NEXT_BLOCKS = 8, 9, 11


class Copies:
    def __init__(self, sems):
        self.sems, self.started = sems, []

    def start(self, source, target):
        copy = pltpu.make_async_copy(source, target, self.sems.at[len(self.started)])
        copy.start()
        self.started.append(copy)
        return copy


def rows_at(table_ref, index, size):
    return pl.ds(pl.multiple_of(table_ref[index] * size, size), size)


def front_kernel(table_ref, gain_ref, weights_ref, *refs):
    chunks, refs = refs[:8], refs[8:]
    kept_ref, given_ref, mean_ref, scale_ref, qkv_ref, scales_ref, attn_ref, probs_ref = refs[:8]
    chunk_buffer, weight_buffer, kept_buffer, given_buffer, total_ref, in_sems, out_sems = refs[8:]
    rows, shard = chunks[0].shape
    loads, stores = Copies(in_sems), Copies(out_sems)
    chunk_loads = [loads.start(chunks[i], chunk_buffer.at[i]) for i in range(8)]
    for load in chunk_loads:
        load.wait()
    weight_loads = [
        loads.start(weights_ref.at[:, rows_at(table_ref, i, shard), :], weight_buffer.at[i]) for i in range(8)
    ]

    @pl.loop(0, rows // 64)
    def _(index):
        at = pl.ds(pl.multiple_of(index * 64, 64), 64)
        total = sum(chunk_buffer[i, at, :].astype(F32) for i in range(8))
        mean = jnp.sum(total, axis=-1, keepdims=True) / (8 * shard)
        spread = sum(jnp.square(chunk_buffer[i, at, :].astype(F32) - mean) for i in range(8))
        variance = jnp.sum(spread, axis=-1, keepdims=True) / (8 * shard)
        mean_ref[at, :] = mean
        scale_ref[at, :] = lax.rsqrt(variance + 1e-06)

    for i in range(8):
        standardized = (chunk_buffer[i].astype(F32) - mean_ref[...]) * scale_ref[...]
        normed = (standardized * gain_ref[table_ref[i]]).astype(BF16)
        kept_buffer[i], given_buffer[i] = by_core(table_ref[CORE], normed)
        stores.start(kept_buffer.at[i], kept_ref.at[table_ref[i]])
        stores.start(given_buffer.at[i], given_ref.at[table_ref[i]])
        weight_loads[i].wait()
        for j in range(3):
            term = dot(normed, weight_buffer[i, j], 1, 0)
            if i:
                total_ref[j] += term
            else:
                total_ref[j] = term

    for image in range(rows // SEQ):
        at = slice(image * SEQ, (image + 1) * SEQ)
        for head in range(3):
            columns = slice(head * HEAD, (head + 1) * HEAD)
            q_n, scales_ref[at, head : head + 1] = head_norm(total_ref[0, at, columns])
            k_n, scales_ref[at, head + 3 : head + 4] = head_norm(total_ref[1, at, columns])
            q_b, k_b, v_b = q_n.astype(BF16), k_n.astype(BF16), total_ref[2, at, columns].astype(BF16)
            qkv_ref[0, at, columns], qkv_ref[1, at, columns], qkv_ref[2, at, columns] = q_b, k_b, v_b
            weights = jnp.exp(dot(q_b, k_b, 1, 1) * (1.0 / HEAD**0.5))
            probs = (weights / jnp.sum(weights, axis=-1, keepdims=True)).astype(BF16)
            probs_ref[image, head] = probs
            attn_ref[at, columns] = dot(probs, v_b, 1, 0).astype(BF16)
    for store in stores.started:
        store.wait()


def front(table, chunks, weights, gain):
    rows, shard = chunks[0].shape
    columns = weights.shape[2]
    half = jax.ShapeDtypeStruct((8, rows, shard // 2), BF16)
    column = jax.ShapeDtypeStruct((rows, 1), F32)
    qkv = jax.ShapeDtypeStruct((3, rows, columns), BF16)
    scales = jax.ShapeDtypeStruct((rows, 8), F32)
    attn = jax.ShapeDtypeStruct((rows, columns), BF16)
    probs = jax.ShapeDtypeStruct((rows // SEQ, 3, SEQ, SEQ), BF16)
    return pl.pallas_call(
        front_kernel,
        grid_spec=pltpu.PrefetchScalarGridSpec(
            num_scalar_prefetch=1,
            grid=(1,),
            in_specs=[whole(jax.ShapeDtypeStruct((8, 1, shard), F32))] + [ANYWHERE] * 9,
            out_specs=[ANYWHERE] * 2 + [whole(o) for o in (column, column, qkv, scales, attn, probs)],
            scratch_shapes=[
                pltpu.VMEM((8, rows, shard), BF16),
                pltpu.VMEM((8, 3, shard, columns), BF16),
                pltpu.VMEM(half.shape, BF16),
                pltpu.VMEM(half.shape, BF16),
                pltpu.VMEM(qkv.shape, F32),
                pltpu.SemaphoreType.DMA((16,)),
                pltpu.SemaphoreType.DMA((16,)),
            ],
        ),
        out_shape=[half, half, column, column, qkv, scales, attn, probs],
        compiler_params=PARAMS,
        cost_estimate=FREE,
    )(table, gain.reshape(8, 1, shard), weights, *chunks)


def near_kernel(table_ref, *refs):
    chunks, (weight_ref, total_ref) = refs[:4], refs[4:]
    for step in range(4):

        @pl.when(pl.program_id(0) == step)
        def _():
            term = dot(chunks[step][...], weight_ref[...], 1, 1)
            if step:
                total_ref[...] += term
            else:
                total_ref[...] = term


def near_d_attn(table, chunks, w_out):
    rows, shard = chunks[0].shape
    heads = w_out.shape[0]
    out = jax.ShapeDtypeStruct((rows, heads), F32)
    return pl.pallas_call(
        near_kernel,
        grid_spec=pltpu.PrefetchScalarGridSpec(
            num_scalar_prefetch=1,
            grid=(4,),
            in_specs=[whole(c) for c in chunks] + [pl.BlockSpec((heads, shard), lambda i, table: (0, table[i]))],
            out_specs=whole(out),
        ),
        out_shape=out,
        compiler_params=PARAMS,
        cost_estimate=FREE,
    )(table, *chunks, w_out)


def tail_kernel(table_ref, w_out_ref, attn_in, total_in, qkv_in, scales_in, probs_in, *refs):
    chunks, refs = refs[:10], refs[10:]
    grad_ref, kept_ref, given_ref = refs[:3]
    chunk_buffer, weight_buffer, attn_ref, total_ref, qkv_ref, scales_ref, probs_ref = refs[3:10]
    grad_buffer, kept_buffer, given_buffer, in_sems, out_sems = refs[10:]
    rows, shard = chunks[0].shape
    loads, stores = Copies(in_sems), Copies(out_sems)
    total_load = loads.start(total_in, total_ref)
    chunk_loads, weight_loads = {}, {}
    parts = [chunks[0:1], chunks[1:2], chunks[2:3], chunks[3:4], chunks[4:6], chunks[6:8], chunks[8:9], chunks[9:10]]

    def load_chunk(i):
        size = rows // len(parts[i])
        return [loads.start(c, chunk_buffer.at[i, pl.ds(n * size, size), :]) for n, c in enumerate(parts[i])]

    for i in range(4, 8):
        chunk_loads[i] = load_chunk(i)
        columns = pl.ds(pl.multiple_of(table_ref[i] * shard, shard), shard)
        weight_loads[i] = loads.start(w_out_ref.at[:, columns], weight_buffer.at[i - 4])
    others = [
        loads.start(source, target)
        for source, target in ((qkv_in, qkv_ref), (scales_in, scales_ref), (probs_in, probs_ref), (attn_in, attn_ref))
    ]
    for i in range(4):
        chunk_loads[i] = load_chunk(i)

    total_load.wait()
    for i in range(4, 8):
        for load in chunk_loads[i]:
            load.wait()
        weight_loads[i].wait()
        total_ref[...] += dot(chunk_buffer[i], weight_buffer[i - 4], 1, 1)
    for load in others:
        load.wait()
    for image in range(rows // SEQ):
        at = slice(image * SEQ, (image + 1) * SEQ)
        for head in range(3):
            columns = slice(head * HEAD, (head + 1) * HEAD)
            q_b, k_b, v_b = qkv_ref[0, at, columns], qkv_ref[1, at, columns], qkv_ref[2, at, columns]
            q_scale, k_scale = scales_ref[at, head : head + 1], scales_ref[at, head + 3 : head + 4]
            probs = probs_ref[image, head]
            d_attn = total_ref[at, columns].astype(BF16)
            d_probs = dot(d_attn, v_b, 1, 1)
            grad_buffer[2, at, columns] = dot(probs, d_attn, 0, 0).astype(BF16)
            probs = probs.astype(F32)
            delta = jnp.sum(probs * d_probs, axis=-1, keepdims=True)
            d_scores = (probs * (d_probs - delta) * (1.0 / HEAD**0.5)).astype(BF16)
            d_qn = dot(d_scores, k_b, 1, 0)
            d_kn = dot(d_scores, q_b, 0, 0)
            grad_buffer[0, at, columns] = head_norm_grad(d_qn, q_b.astype(F32), q_scale).astype(BF16)
            grad_buffer[1, at, columns] = head_norm_grad(d_kn, k_b.astype(F32), k_scale).astype(BF16)
    stores.start(grad_buffer, grad_ref)
    for i in (4, 5, 6, 7, 0, 1, 2, 3):
        if i < 4:
            chunk_loads[i][0].wait()
        term = dot(attn_ref[...], chunk_buffer[i], 0, 0).astype(BF16)
        kept_buffer[i], given_buffer[i] = by_core(table_ref[CORE], term)
        stores.start(kept_buffer.at[i], kept_ref.at[table_ref[i]])
        stores.start(given_buffer.at[i], given_ref.at[table_ref[i]])
    for store in stores.started:
        store.wait()


def tail(table, chunks, w_out, attn, total, qkv, scales, probs):
    rows, shard = chunks[0].shape
    heads = w_out.shape[0]
    grad = jax.ShapeDtypeStruct(qkv.shape, BF16)
    half = jax.ShapeDtypeStruct((8, heads, shard // 2), BF16)
    return pl.pallas_call(
        tail_kernel,
        grid_spec=pltpu.PrefetchScalarGridSpec(
            num_scalar_prefetch=1,
            grid=(1,),
            in_specs=[ANYWHERE] * 16,
            out_specs=[ANYWHERE] * 3,
            scratch_shapes=[
                pltpu.VMEM((8, rows, shard), BF16),
                pltpu.VMEM((4, heads, shard), BF16),
                pltpu.VMEM(attn.shape, BF16),
                pltpu.VMEM(total.shape, F32),
                pltpu.VMEM(qkv.shape, BF16),
                pltpu.VMEM(scales.shape, F32),
                pltpu.VMEM(probs.shape, BF16),
                pltpu.VMEM(grad.shape, BF16),
                pltpu.VMEM(half.shape, BF16),
                pltpu.VMEM(half.shape, BF16),
                pltpu.SemaphoreType.DMA((19,)),
                pltpu.SemaphoreType.DMA((17,)),
            ],
        ),
        out_shape=[grad, half, half],
        compiler_params=PARAMS,
        cost_estimate=FREE,
    )(table, w_out, attn, total, qkv, scales, probs, *jax.tree.leaves(chunks))


def normed_kernel(first, count, table_ref, grad_in, weights_ref, *refs):
    out_refs, (grad_ref, weight_buffer, out_buffer, in_sems, out_sems) = refs[:count], refs[count:]
    shard = weight_buffer.shape[2]
    loads, stores = Copies(in_sems), Copies(out_sems)

    def weight_copy(i):
        source = weights_ref.at[:, rows_at(table_ref, first + i, shard), :]
        return pltpu.make_async_copy(source, weight_buffer.at[i], in_sems.at[i + 1])

    loads.start(grad_in, grad_ref)
    for i in range(count):
        weight_copy(i).start()
    loads.started[0].wait()

    @pl.loop(0, count)
    def _(step):
        weight_copy(step).wait()
        out_buffer[step] = sum(dot(grad_ref[j], weight_buffer[step, j], 1, 1) for j in range(3)).astype(BF16)
        for i in range(count):

            @pl.when(step == i)
            def _():
                pltpu.make_async_copy(out_buffer.at[i], out_refs[i], out_sems.at[i]).start()

    for i in range(count):
        pltpu.make_async_copy(out_buffer.at[i], out_refs[i], out_sems.at[i]).wait()


def normed_terms(table, first, count, d_qkv, weights):
    _, rows, columns = d_qkv.shape
    shard = weights.shape[1] // 8
    return pl.pallas_call(
        functools.partial(normed_kernel, first, count),
        grid_spec=pltpu.PrefetchScalarGridSpec(
            num_scalar_prefetch=1,
            grid=(1,),
            in_specs=[ANYWHERE] * 2,
            out_specs=[ANYWHERE] * count,
            scratch_shapes=[
                pltpu.VMEM(d_qkv.shape, BF16),
                pltpu.VMEM((count, 3, shard, columns), BF16),
                pltpu.VMEM((count, rows, shard), BF16),
                pltpu.SemaphoreType.DMA((count + 1,)),
                pltpu.SemaphoreType.DMA((count,)),
            ],
        ),
        out_shape=[jax.ShapeDtypeStruct((rows, shard), BF16)] * count,
        compiler_params=PARAMS,
        cost_estimate=FREE,
    )(table, d_qkv, weights)


def block_kernel(first, count, halves, table_ref, *refs):
    left, out, right = refs[0:2], refs[2:4], refs[4:6]
    out_refs, refs = refs[6 : 6 + (2 if halves else count)], refs[6 + (2 if halves else count) :]
    left_buffer, out_buffer, right_buffer, sum_buffer, in_sems, out_sems = refs
    size = sum_buffer.shape[2]

    def loads(i):
        place = table_ref[first + i]
        pairs = [(left[s].at[place], left_buffer.at[i, s]) for s in range(2)]
        pairs += [(out[s].at[place], out_buffer.at[i, s]) for s in range(2)]
        return [pltpu.make_async_copy(s, t, in_sems.at[2 + 4 * i + n]) for n, (s, t) in enumerate(pairs)]

    def stores(i):
        if not halves:
            return [pltpu.make_async_copy(sum_buffer.at[i], out_refs[i], out_sems.at[i])]
        rows = [pl.ds(part * (size // 2), size // 2) for part in range(2)]
        return [
            pltpu.make_async_copy(sum_buffer.at[i, :, rows[part], :], out_refs[part].at[i], out_sems.at[2 * i + part])
            for part in range(2)
        ]

    sides = [pltpu.make_async_copy(right[s], right_buffer.at[s], in_sems.at[s]) for s in range(2)]
    for copy in sides:
        copy.start()
    for i in range(count):
        for copy in loads(i):
            copy.start()
    for copy in sides:
        copy.wait()

    @pl.loop(0, count)
    def _(step):
        for copy in loads(step):
            copy.wait()
        for j in range(3):
            total = dot(left_buffer[step, 0], right_buffer[0, j], 0, 0) + dot(left_buffer[step, 1], right_buffer[1, j], 0, 0)
            sum_buffer[step, j] = total.astype(BF16)
        sum_buffer[step, 3] = add_rounded(out_buffer[step, 0], out_buffer[step, 1])
        for i in range(count):

            @pl.when(step == i)
            def _():
                for copy in stores(i):
                    copy.start()

    for i in range(count):
        for copy in stores(i):
            copy.wait()


def weight_blocks(table, first, count, left, out, right, halves=False):
    _, rows, size = left[0].shape
    columns = right[0].shape[2]
    if halves:
        out_shape = [jax.ShapeDtypeStruct((count, 4, size // 2, columns), BF16)] * 2
    else:
        out_shape = [jax.ShapeDtypeStruct((4, size, columns), BF16)] * count
    return pl.pallas_call(
        functools.partial(block_kernel, first, count, halves),
        grid_spec=pltpu.PrefetchScalarGridSpec(
            num_scalar_prefetch=1,
            grid=(1,),
            in_specs=[ANYWHERE] * 6,
            out_specs=[ANYWHERE] * len(out_shape),
            scratch_shapes=[
                pltpu.VMEM((count, 2, rows, size), BF16),
                pltpu.VMEM((count, 2, size, columns), BF16),
                pltpu.VMEM((2, 3, rows, columns), BF16),
                pltpu.VMEM((count, 4, size, columns), BF16),
                pltpu.SemaphoreType.DMA((2 + 4 * count,)),
                pltpu.SemaphoreType.DMA((count * (2 if halves else 1),)),
            ],
        ),
        out_shape=out_shape,
        compiler_params=PARAMS,
        cost_estimate=FREE,
    )(table, *left, *out, *right)


def split_kernel(first_ref, second_ref, first_half_ref, second_half_ref):
    first_half_ref[...] = first_ref[...]
    second_half_ref[...] = second_ref[...]


def split_halves(first, second):
    rows, width = first.shape
    half = (rows // 2, width)
    return pl.pallas_call(
        split_kernel,
        grid=(1,),
        in_specs=[pl.BlockSpec(half, functools.partial(lambda part, i: (part, 0), part)) for part in (0, 1)],
        out_specs=[pl.BlockSpec(half, lambda i: (0, 0))] * 2,
        out_shape=[jax.ShapeDtypeStruct(half, BF16)] * 2,
        compiler_params=PARAMS,
        cost_estimate=FREE,
    )(first, second)


def join_kernel(first_ref, second_ref, out_ref):
    half = first_ref.shape[0]
    out_ref[:half] = first_ref[...]
    out_ref[half:] = second_ref[...]


def join_halves(first, second):
    return pl.pallas_call(
        join_kernel,
        out_shape=jax.ShapeDtypeStruct((2 * first.shape[0], first.shape[1]), BF16),
        compiler_params=PARAMS,
        cost_estimate=FREE,
    )(first, second)


def add_kernel(index, up_ref, down_ref, from_left_ref, from_right_ref, up_out, down_out, held, got, in_sems, out_sems):
    half = got.shape[2]
    pieces = [(up_ref, from_left_ref, up_out, pl.ds(0, half)), (down_ref, from_right_ref, down_out, pl.ds(half, half))]
    loads, stores = Copies(in_sems), Copies(out_sems)
    for i, (block, part, _, rows) in enumerate(pieces):
        loads.start(block.at[:, rows, :], held.at[i])
        loads.start(part.at[index], got.at[i])
    for i, (_, _, out, rows) in enumerate(pieces):
        for load in loads.started[2 * i : 2 * i + 2]:
            load.wait()
        held[i] = add_rounded(held[i], got[i])
        stores.start(held.at[i], out.at[:, rows, :])
    for store in stores.started:
        store.wait()


def add_halves(up, down, far, index):
    count, size, columns = up.shape
    half = pltpu.VMEM((2, count, size // 2, columns), BF16)
    return pl.pallas_call(
        functools.partial(add_kernel, index),
        grid=(1,),
        in_specs=[ANYWHERE] * 4,
        out_specs=[ANYWHERE] * 2,
        out_shape=[jax.ShapeDtypeStruct(up.shape, BF16)] * 2,
        scratch_shapes=[half, half, pltpu.SemaphoreType.DMA((4,)), pltpu.SemaphoreType.DMA((2,))],
        input_output_aliases={0: 0, 1: 1},
        compiler_params=PARAMS,
        cost_estimate=FREE,
    )(up, down, *far)


def add_first(block, part):
    half = part.shape[-2]
    return jnp.concatenate([add_rounded(block[..., :half, :], part), block[..., half:, :]], axis=-2)


def add_last(block, part):
    half = part.shape[-2]
    return jnp.concatenate([block[..., :half, :], add_rounded(block[..., half:, :], part)], axis=-2)


def body(inputs, cotangent, layer_norm_gain, w_qkv, w_out):
    shard = inputs.shape[1]
    dp, mp = lax.axis_index("dp"), lax.axis_index("mp")
    x, yhi = mp // 2, mp % 2
    z, ylo, core = dp // 4, (dp // 2) % 2, dp % 2
    weights = jnp.transpose(w_qkv, (1, 0, 2))
    places = [lax.rem(x + dx, 4) * 2 + lax.rem(yhi + dyhi, 2) for dx, dyhi in KEYS] + [core]
    for dz, e in [(2, 1 - ylo), (2, ylo), (1, 1 - ylo), (3, 1 - ylo), (1, ylo), (3, ylo), (0, 1 - ylo), (0, ylo)]:
        places.append(lax.rem(z + dz, 4) * 2 + e)
    table = jnp.stack(places)

    def first_steps(value):
        return {OWN: value, LEFT: shift(value, dx=1), RIGHT: shift(value, dx=-1), ACROSS: shift(value, dyhi=1)}

    def pick(chunks, keys=KEYS):
        return [chunks[key] for key in keys]

    raw, ct = first_steps(inputs), first_steps(cotangent)
    raw_halves = split_halves(raw[LEFT], raw[RIGHT])
    raw_halves = [shift(raw_halves[0], dx=1), shift(raw_halves[1], dx=-1)]
    raw[ACROSS], ct[LEFT], ct[RIGHT] = fence(raw[ACROSS], ct[LEFT], ct[RIGHT])
    raw[3, 1], raw[1, 1] = shift(raw[ACROSS], dx=1), shift(raw[ACROSS], dx=-1)
    ct_halves = split_halves(ct[LEFT], ct[RIGHT])
    ct_halves, raw_halves, ct = fence(ct_halves, raw_halves, ct)
    ct_halves = [shift(ct_halves[0], dx=1), shift(ct_halves[1], dx=-1)]
    raw[FAR] = join_halves(*raw_halves)
    raw[2, 1] = shift(raw[FAR], dyhi=1)
    d_attn = near_d_attn(table, pick(ct, KEYS[:4]), w_out)
    raw[3, 1], raw[1, 1], ct[ACROSS], d_attn = fence(raw[3, 1], raw[1, 1], ct[ACROSS], d_attn)
    ct[3, 1], ct[1, 1] = shift(ct[ACROSS], dx=1), shift(ct[ACROSS], dx=-1)
    ct[FAR] = ct_halves
    raw, ct[FAR] = fence(raw, ct[FAR])
    ct[2, 1] = [shift(part, dyhi=1) for part in ct[FAR]]
    *normed_sides, row_mean, row_scale, qkv, scales, attn, probs = front(table, pick(raw), weights, layer_norm_gain)
    ct, qkv, scales, normed_sides, attn, probs = fence(ct, qkv, scales, normed_sides, attn, probs)

    normed_sides = (normed_sides[0], shift(normed_sides[1], dcore=1))
    d_qkv, *out_sides = tail(table, pick(ct), w_out, attn, d_attn, qkv, scales, probs)
    d_qkv, out_sides, normed_sides = fence(d_qkv, out_sides, normed_sides)

    qkv_sides = (d_qkv, shift(d_qkv, dcore=1))
    out_sides = (out_sides[0], shift(out_sides[1], dcore=1))
    first_terms = normed_terms(table, 5, 3, d_qkv, weights)
    first_terms, out_sides, qkv_sides = fence(first_terms, out_sides, qkv_sides)
    far_blocks = weight_blocks(table, FAR_BLOCKS, 2, normed_sides, out_sides, qkv_sides, True)
    first_terms, far_blocks, d_qkv, out_sides, qkv_sides = fence(first_terms, far_blocks, d_qkv, out_sides, qkv_sides)

    far_across, left_across, right_across = (
        shift(first_terms[0], dyhi=1),
        shift(first_terms[1], dx=1),
        shift(first_terms[2], dx=-1),
    )
    far_blocks = [shift(far_blocks[0], dz=1), shift(far_blocks[1], dz=-1)]
    across_term, far_term = normed_terms(table, 3, 2, d_qkv, weights)
    blocks = weight_blocks(table, NEXT_BLOCKS, 6, normed_sides, out_sides, qkv_sides)
    far_across, left_across, right_across, far_blocks, blocks, far_term, across_term = fence(
        far_across, left_across, right_across, far_blocks, blocks, far_term, across_term
    )

    up, down = add_halves(blocks[0], blocks[1], far_blocks, 0)
    up, down, far_term, far_across, across_term = fence(up, down, far_term, far_across, across_term)
    other = (shift(up, dz=1), shift(down, dz=-1))
    far_term = add_rounded(far_term, far_across)
    far_left, far_right = shift(far_term[:SEQ], dx=1), shift(far_term[SEQ:], dx=-1)
    across_sum = shift(add_rounded(across_term, left_across, right_across), dyhi=1)
    far_left, far_right, d_qkv = fence(far_left, far_right, d_qkv)
    own_term, left_term, right_term = normed_terms(table, 0, 3, d_qkv, weights)
    up, down = add_halves(blocks[2], blocks[3], far_blocks, 1)
    right_term, left_term = add_first(right_term, far_left), add_last(left_term, far_right)
    standardized = (inputs.astype(F32) - row_mean) * row_scale
    gain = lax.dynamic_slice_in_dim(layer_norm_gain, mp * shard, shard, 0)
    other, across_sum, up, down, standardized, gain, right_term, left_term = fence(
        other, across_sum, up, down, standardized, gain, right_term, left_term
    )

    from_left, from_right = shift(right_term, dx=1), shift(left_term, dx=-1)
    mine = (shift(up, dz=1), shift(down, dz=-1))
    other_got = shift(add_rounded(blocks[4], *other), dylo=1)
    d_normed = add(own_term, from_left, from_right, across_sum)
    scaled = d_normed * gain
    sums = jnp.stack([jnp.sum(scaled, axis=-1), jnp.sum(scaled * standardized, axis=-1)])
    sums = sums + shift(sums, dx=1) + shift(sums, dx=-1) + shift(sums, dx=2)
    means = (sums + shift(sums, dyhi=1)) / (8 * shard)
    gain_sum = jnp.sum(d_normed * standardized, axis=0).reshape(6, -1)
    gain_sum = gain_sum + shift(gain_sum, dcore=1)
    gain_sum = gain_sum + lax.ppermute(gain_sum, AXES, mirrored(1))
    gain_sum = gain_sum + lax.ppermute(gain_sum, AXES, mirrored(3))
    total = add_rounded(blocks[5], *mine, other_got)
    qkv_grad, out_grad = jnp.transpose(total[:3], (1, 0, 2)), total[3]
    qkv_grad, out_grad, means, gain_sum = fence(qkv_grad, out_grad, means, gain_sum)

    gain_gradient = (gain_sum + shift(gain_sum, dylo=1)).reshape(shard)
    back = row_scale * (scaled - means[0][:, None] - standardized * means[1][:, None])
    input_grad = (cotangent.astype(F32) + back).astype(BF16)
    return input_grad, qkv_grad, out_grad, gain_gradient


def solution(mesh):
    in_specs = (P("dp", "mp"), P("dp", "mp"), P(), P(None, None, "mp"), P("mp", None))
    out_specs = (P("dp", "mp"), P("dp", None, "mp"), P("mp", "dp"), P("mp"))
    return jax.shard_map(body, mesh=mesh, in_specs=in_specs, out_specs=out_specs, check_vma=False)
```

```python
import functools

import jax
import jax.numpy as jnp
from jax import lax
from jax.experimental import pallas as pl
from jax.experimental.pallas import tpu as pltpu
from jax.sharding import PartitionSpec as P

HEAD = 128
SEQ = 256
AXES = ("dp", "mp")
F32 = jnp.float32
BF16 = jnp.bfloat16


def place(index):
    dp, mp = divmod(index, 8)
    return mp // 2, (mp % 2) * 2 + (dp // 2) % 2, dp // 4, dp % 2


def index_of(x, y, z, core):
    x, y, z = x % 4, y % 4, z % 4
    return (z * 4 + (y % 2) * 2 + core) * 8 + x * 2 + y // 2


def shift(value, dx=0, dyhi=0, dylo=0, dz=0, dcore=0):
    pairs = []
    for index in range(128):
        x, y, z, core = place(index)
        pairs.append((index, index_of(x + dx, y ^ (2 * dyhi) ^ dylo, z + dz, core ^ dcore)))
    return lax.ppermute(value, AXES, pairs)


def mirrored(flip):
    pairs = []
    for index in range(128):
        x, y, z, core = place(index)
        pairs.append((index, index_of(x, y, z ^ flip, core)))
    return pairs


def fence(*values):
    return lax.optimization_barrier(values)


def dot(a, b, ca, cb):
    return lax.dot_general(a, b, (((ca,), (cb,)), ((), ())), preferred_element_type=F32)


def add(*terms):
    return sum(t.astype(F32) for t in terms)


def add_rounded(*terms):
    return add(*terms).astype(BF16)


def head_norm(values):
    centered = values - jnp.mean(values, axis=-1, keepdims=True)
    scale = lax.rsqrt(jnp.mean(centered * centered, axis=-1, keepdims=True) + 1e-06)
    return centered * scale, scale


def head_norm_grad(grad, normalized, scale):
    return scale * (
        grad
        - jnp.mean(grad, axis=-1, keepdims=True)
        - normalized * jnp.mean(grad * normalized, axis=-1, keepdims=True)
    )


FREE = pl.CostEstimate(flops=0, bytes_accessed=0, transcendentals=0)
PARAMS = pltpu.CompilerParams(vmem_limit_bytes=60 * 2**20)


def whole(array):
    return pl.BlockSpec(array.shape, lambda i, table: (0,) * array.ndim)


def by_core(core, values):
    half = values.shape[1] // 2
    low, high = values[:, :half], values[:, half:]
    return jnp.where(core == 0, low, high), jnp.where(core == 0, high, low)


ANYWHERE = pl.BlockSpec(memory_space=pl.ANY)
OWN, LEFT, RIGHT, ACROSS, FAR = (0, 0), (3, 0), (1, 0), (0, 1), (2, 0)
KEYS = [OWN, LEFT, RIGHT, ACROSS, FAR, (2, 1), (1, 1), (3, 1)]
CORE, FAR_BLOCKS, NEXT_BLOCKS, LAST_BLOCK = 8, 9, 11, 16


class Copies:
    def __init__(self, sems):
        self.sems, self.started = sems, []

    def start(self, source, target):
        copy = pltpu.make_async_copy(source, target, self.sems.at[len(self.started)])
        copy.start()
        self.started.append(copy)
        return copy


def rows_at(table_ref, index, size):
    return pl.ds(pl.multiple_of(table_ref[index] * size, size), size)


def front_kernel(table_ref, gain_ref, weights_ref, *refs):
    chunks, refs = refs[:8], refs[8:]
    kept_ref, given_ref, mean_ref, scale_ref, qkv_ref, scales_ref, attn_ref, probs_ref = refs[:8]
    chunk_buffer, weight_buffer, kept_buffer, given_buffer, total_ref, in_sems, out_sems = refs[8:]
    rows, shard = chunks[0].shape
    loads, stores = Copies(in_sems), Copies(out_sems)
    chunk_loads = [loads.start(chunks[i], chunk_buffer.at[i]) for i in range(8)]
    for load in chunk_loads:
        load.wait()
    weight_loads = [
        loads.start(weights_ref.at[:, rows_at(table_ref, i, shard), :], weight_buffer.at[i]) for i in range(8)
    ]

    @pl.loop(0, rows // 64)
    def _(index):
        at = pl.ds(pl.multiple_of(index * 64, 64), 64)
        total = sum(chunk_buffer[i, at, :].astype(F32) for i in range(8))
        mean = jnp.sum(total, axis=-1, keepdims=True) / (8 * shard)
        spread = sum(jnp.square(chunk_buffer[i, at, :].astype(F32) - mean) for i in range(8))
        variance = jnp.sum(spread, axis=-1, keepdims=True) / (8 * shard)
        mean_ref[at, :] = mean
        scale_ref[at, :] = lax.rsqrt(variance + 1e-06)

    for i in range(8):
        standardized = (chunk_buffer[i].astype(F32) - mean_ref[...]) * scale_ref[...]
        normed = (standardized * gain_ref[table_ref[i]]).astype(BF16)
        kept_buffer[i], given_buffer[i] = by_core(table_ref[CORE], normed)
        stores.start(kept_buffer.at[i], kept_ref.at[table_ref[i]])
        stores.start(given_buffer.at[i], given_ref.at[table_ref[i]])
        weight_loads[i].wait()
        for j in range(3):
            term = dot(normed, weight_buffer[i, j], 1, 0)
            if i:
                total_ref[j] += term
            else:
                total_ref[j] = term

    for image in range(rows // SEQ):
        at = slice(image * SEQ, (image + 1) * SEQ)
        for head in range(3):
            columns = slice(head * HEAD, (head + 1) * HEAD)
            q_n, scales_ref[at, head : head + 1] = head_norm(total_ref[0, at, columns])
            k_n, scales_ref[at, head + 3 : head + 4] = head_norm(total_ref[1, at, columns])
            q_b, k_b, v_b = q_n.astype(BF16), k_n.astype(BF16), total_ref[2, at, columns].astype(BF16)
            qkv_ref[0, at, columns], qkv_ref[1, at, columns], qkv_ref[2, at, columns] = q_b, k_b, v_b
            weights = jnp.exp(dot(q_b, k_b, 1, 1) * (1.0 / HEAD**0.5))
            probs = (weights / jnp.sum(weights, axis=-1, keepdims=True)).astype(BF16)
            probs_ref[image, head] = probs
            attn_ref[at, columns] = dot(probs, v_b, 1, 0).astype(BF16)
    for store in stores.started:
        store.wait()


def front(table, chunks, weights, gain):
    rows, shard = chunks[0].shape
    columns = weights.shape[2]
    half = jax.ShapeDtypeStruct((8, rows, shard // 2), BF16)
    column = jax.ShapeDtypeStruct((rows, 1), F32)
    qkv = jax.ShapeDtypeStruct((3, rows, columns), BF16)
    scales = jax.ShapeDtypeStruct((rows, 8), F32)
    attn = jax.ShapeDtypeStruct((rows, columns), BF16)
    probs = jax.ShapeDtypeStruct((rows // SEQ, 3, SEQ, SEQ), BF16)
    return pl.pallas_call(
        front_kernel,
        grid_spec=pltpu.PrefetchScalarGridSpec(
            num_scalar_prefetch=1,
            grid=(1,),
            in_specs=[whole(jax.ShapeDtypeStruct((8, 1, shard), F32))] + [ANYWHERE] * 9,
            out_specs=[ANYWHERE] * 2 + [whole(o) for o in (column, column, qkv, scales, attn, probs)],
            scratch_shapes=[
                pltpu.VMEM((8, rows, shard), BF16),
                pltpu.VMEM((8, 3, shard, columns), BF16),
                pltpu.VMEM(half.shape, BF16),
                pltpu.VMEM(half.shape, BF16),
                pltpu.VMEM(qkv.shape, F32),
                pltpu.SemaphoreType.DMA((16,)),
                pltpu.SemaphoreType.DMA((16,)),
            ],
        ),
        out_shape=[half, half, column, column, qkv, scales, attn, probs],
        compiler_params=PARAMS,
        cost_estimate=FREE,
    )(table, gain.reshape(8, 1, shard), weights, *chunks)


def near_kernel(table_ref, *refs):
    chunks, (weight_ref, total_ref) = refs[:4], refs[4:]
    for step in range(4):

        @pl.when(pl.program_id(0) == step)
        def _():
            term = dot(chunks[step][...], weight_ref[...], 1, 1)
            if step:
                total_ref[...] += term
            else:
                total_ref[...] = term


def near_d_attn(table, chunks, w_out):
    rows, shard = chunks[0].shape
    heads = w_out.shape[0]
    out = jax.ShapeDtypeStruct((rows, heads), F32)
    return pl.pallas_call(
        near_kernel,
        grid_spec=pltpu.PrefetchScalarGridSpec(
            num_scalar_prefetch=1,
            grid=(4,),
            in_specs=[whole(c) for c in chunks] + [pl.BlockSpec((heads, shard), lambda i, table: (0, table[i]))],
            out_specs=whole(out),
        ),
        out_shape=out,
        compiler_params=PARAMS,
        cost_estimate=FREE,
    )(table, *chunks, w_out)


def tail_kernel(table_ref, w_out_ref, attn_in, total_in, qkv_in, scales_in, probs_in, *refs):
    chunks, refs = refs[:10], refs[10:]
    grad_ref, kept_ref, given_ref = refs[:3]
    chunk_buffer, weight_buffer, attn_ref, total_ref, qkv_ref, scales_ref, probs_ref = refs[3:10]
    grad_buffer, kept_buffer, given_buffer, in_sems, out_sems = refs[10:]
    rows, shard = chunks[0].shape
    loads, stores = Copies(in_sems), Copies(out_sems)
    total_load = loads.start(total_in, total_ref)
    chunk_loads, weight_loads = {}, {}
    parts = [chunks[0:1], chunks[1:2], chunks[2:3], chunks[3:4], chunks[4:6], chunks[6:8], chunks[8:9], chunks[9:10]]

    def load_chunk(i):
        size = rows // len(parts[i])
        return [loads.start(c, chunk_buffer.at[i, pl.ds(n * size, size), :]) for n, c in enumerate(parts[i])]

    for i in range(4, 8):
        chunk_loads[i] = load_chunk(i)
        columns = pl.ds(pl.multiple_of(table_ref[i] * shard, shard), shard)
        weight_loads[i] = loads.start(w_out_ref.at[:, columns], weight_buffer.at[i - 4])
    others = [
        loads.start(source, target)
        for source, target in ((qkv_in, qkv_ref), (scales_in, scales_ref), (probs_in, probs_ref), (attn_in, attn_ref))
    ]
    for i in range(4):
        chunk_loads[i] = load_chunk(i)

    total_load.wait()
    for i in range(4, 8):
        for load in chunk_loads[i]:
            load.wait()
        weight_loads[i].wait()
        total_ref[...] += dot(chunk_buffer[i], weight_buffer[i - 4], 1, 1)
    for load in others:
        load.wait()
    for image in range(rows // SEQ):
        at = slice(image * SEQ, (image + 1) * SEQ)
        for head in range(3):
            columns = slice(head * HEAD, (head + 1) * HEAD)
            q_b, k_b, v_b = qkv_ref[0, at, columns], qkv_ref[1, at, columns], qkv_ref[2, at, columns]
            q_scale, k_scale = scales_ref[at, head : head + 1], scales_ref[at, head + 3 : head + 4]
            probs = probs_ref[image, head]
            d_attn = total_ref[at, columns].astype(BF16)
            d_probs = dot(d_attn, v_b, 1, 1)
            grad_buffer[2, at, columns] = dot(probs, d_attn, 0, 0).astype(BF16)
            probs = probs.astype(F32)
            delta = jnp.sum(probs * d_probs, axis=-1, keepdims=True)
            d_scores = (probs * (d_probs - delta) * (1.0 / HEAD**0.5)).astype(BF16)
            d_qn = dot(d_scores, k_b, 1, 0)
            d_kn = dot(d_scores, q_b, 0, 0)
            grad_buffer[0, at, columns] = head_norm_grad(d_qn, q_b.astype(F32), q_scale).astype(BF16)
            grad_buffer[1, at, columns] = head_norm_grad(d_kn, k_b.astype(F32), k_scale).astype(BF16)
    stores.start(grad_buffer, grad_ref)
    for i in (4, 5, 6, 7, 0, 1, 2, 3):
        if i < 4:
            chunk_loads[i][0].wait()
        term = dot(attn_ref[...], chunk_buffer[i], 0, 0).astype(BF16)
        kept_buffer[i], given_buffer[i] = by_core(table_ref[CORE], term)
        stores.start(kept_buffer.at[i], kept_ref.at[table_ref[i]])
        stores.start(given_buffer.at[i], given_ref.at[table_ref[i]])
    for store in stores.started:
        store.wait()


def tail(table, chunks, w_out, attn, total, qkv, scales, probs):
    rows, shard = chunks[0].shape
    heads = w_out.shape[0]
    grad = jax.ShapeDtypeStruct(qkv.shape, BF16)
    half = jax.ShapeDtypeStruct((8, heads, shard // 2), BF16)
    return pl.pallas_call(
        tail_kernel,
        grid_spec=pltpu.PrefetchScalarGridSpec(
            num_scalar_prefetch=1,
            grid=(1,),
            in_specs=[ANYWHERE] * 16,
            out_specs=[ANYWHERE] * 3,
            scratch_shapes=[
                pltpu.VMEM((8, rows, shard), BF16),
                pltpu.VMEM((4, heads, shard), BF16),
                pltpu.VMEM(attn.shape, BF16),
                pltpu.VMEM(total.shape, F32),
                pltpu.VMEM(qkv.shape, BF16),
                pltpu.VMEM(scales.shape, F32),
                pltpu.VMEM(probs.shape, BF16),
                pltpu.VMEM(grad.shape, BF16),
                pltpu.VMEM(half.shape, BF16),
                pltpu.VMEM(half.shape, BF16),
                pltpu.SemaphoreType.DMA((19,)),
                pltpu.SemaphoreType.DMA((17,)),
            ],
        ),
        out_shape=[grad, half, half],
        compiler_params=PARAMS,
        cost_estimate=FREE,
    )(table, w_out, attn, total, qkv, scales, probs, *jax.tree.leaves(chunks))


def normed_kernel(first, count, table_ref, grad_in, weights_ref, *refs):
    out_refs, (grad_ref, weight_buffer, out_buffer, in_sems, out_sems) = refs[:count], refs[count:]
    shard = weight_buffer.shape[2]
    loads, stores = Copies(in_sems), Copies(out_sems)

    def weight_copy(i):
        source = weights_ref.at[:, rows_at(table_ref, first + i, shard), :]
        return pltpu.make_async_copy(source, weight_buffer.at[i], in_sems.at[i + 1])

    loads.start(grad_in, grad_ref)
    for i in range(count):
        weight_copy(i).start()
    loads.started[0].wait()

    @pl.loop(0, count)
    def _(step):
        weight_copy(step).wait()
        out_buffer[step] = sum(dot(grad_ref[j], weight_buffer[step, j], 1, 1) for j in range(3)).astype(BF16)
        for i in range(count):

            @pl.when(step == i)
            def _():
                pltpu.make_async_copy(out_buffer.at[i], out_refs[i], out_sems.at[i]).start()

    for i in range(count):
        pltpu.make_async_copy(out_buffer.at[i], out_refs[i], out_sems.at[i]).wait()


def normed_terms(table, first, count, d_qkv, weights):
    _, rows, columns = d_qkv.shape
    shard = weights.shape[1] // 8
    return pl.pallas_call(
        functools.partial(normed_kernel, first, count),
        grid_spec=pltpu.PrefetchScalarGridSpec(
            num_scalar_prefetch=1,
            grid=(1,),
            in_specs=[ANYWHERE] * 2,
            out_specs=[ANYWHERE] * count,
            scratch_shapes=[
                pltpu.VMEM(d_qkv.shape, BF16),
                pltpu.VMEM((count, 3, shard, columns), BF16),
                pltpu.VMEM((count, rows, shard), BF16),
                pltpu.SemaphoreType.DMA((count + 1,)),
                pltpu.SemaphoreType.DMA((count,)),
            ],
        ),
        out_shape=[jax.ShapeDtypeStruct((rows, shard), BF16)] * count,
        compiler_params=PARAMS,
        cost_estimate=FREE,
    )(table, d_qkv, weights)


def block_kernel(first, count, halves, table_ref, *refs):
    left, out, right = refs[0:2], refs[2:4], refs[4:6]
    out_refs, refs = refs[6 : 6 + (2 if halves else count)], refs[6 + (2 if halves else count) :]
    left_buffer, out_buffer, right_buffer, sum_buffer, in_sems, out_sems = refs
    size = sum_buffer.shape[2]

    def loads(i):
        place = table_ref[first + i]
        pairs = [(left[s].at[place], left_buffer.at[i, s]) for s in range(2)]
        pairs += [(out[s].at[place], out_buffer.at[i, s]) for s in range(2)]
        return [pltpu.make_async_copy(s, t, in_sems.at[2 + 4 * i + n]) for n, (s, t) in enumerate(pairs)]

    def stores(i):
        if not halves:
            return [pltpu.make_async_copy(sum_buffer.at[i], out_refs[i], out_sems.at[i])]
        rows = [pl.ds(part * (size // 2), size // 2) for part in range(2)]
        return [
            pltpu.make_async_copy(sum_buffer.at[i, :, rows[part], :], out_refs[part].at[i], out_sems.at[2 * i + part])
            for part in range(2)
        ]

    sides = [pltpu.make_async_copy(right[s], right_buffer.at[s], in_sems.at[s]) for s in range(2)]
    for copy in sides:
        copy.start()
    for i in range(count):
        for copy in loads(i):
            copy.start()
    for copy in sides:
        copy.wait()

    @pl.loop(0, count)
    def _(step):
        for copy in loads(step):
            copy.wait()
        for j in range(3):
            total = dot(left_buffer[step, 0], right_buffer[0, j], 0, 0) + dot(left_buffer[step, 1], right_buffer[1, j], 0, 0)
            sum_buffer[step, j] = total.astype(BF16)
        sum_buffer[step, 3] = add_rounded(out_buffer[step, 0], out_buffer[step, 1])
        for i in range(count):

            @pl.when(step == i)
            def _():
                for copy in stores(i):
                    copy.start()

    for i in range(count):
        for copy in stores(i):
            copy.wait()


def weight_blocks(table, first, count, left, out, right, halves=False):
    _, rows, size = left[0].shape
    columns = right[0].shape[2]
    if halves:
        out_shape = [jax.ShapeDtypeStruct((count, 4, size // 2, columns), BF16)] * 2
    else:
        out_shape = [jax.ShapeDtypeStruct((4, size, columns), BF16)] * count
    return pl.pallas_call(
        functools.partial(block_kernel, first, count, halves),
        grid_spec=pltpu.PrefetchScalarGridSpec(
            num_scalar_prefetch=1,
            grid=(1,),
            in_specs=[ANYWHERE] * 6,
            out_specs=[ANYWHERE] * len(out_shape),
            scratch_shapes=[
                pltpu.VMEM((count, 2, rows, size), BF16),
                pltpu.VMEM((count, 2, size, columns), BF16),
                pltpu.VMEM((2, 3, rows, columns), BF16),
                pltpu.VMEM((count, 4, size, columns), BF16),
                pltpu.SemaphoreType.DMA((2 + 4 * count,)),
                pltpu.SemaphoreType.DMA((count * (2 if halves else 1),)),
            ],
        ),
        out_shape=out_shape,
        compiler_params=PARAMS,
        cost_estimate=FREE,
    )(table, *left, *out, *right)


def split_kernel(first_ref, second_ref, first_half_ref, second_half_ref):
    first_half_ref[...] = first_ref[...]
    second_half_ref[...] = second_ref[...]


def split_halves(first, second):
    rows, width = first.shape
    half = (rows // 2, width)
    return pl.pallas_call(
        split_kernel,
        grid=(1,),
        in_specs=[pl.BlockSpec(half, functools.partial(lambda part, i: (part, 0), part)) for part in (0, 1)],
        out_specs=[pl.BlockSpec(half, lambda i: (0, 0))] * 2,
        out_shape=[jax.ShapeDtypeStruct(half, BF16)] * 2,
        compiler_params=PARAMS,
        cost_estimate=FREE,
    )(first, second)


def join_kernel(first_ref, second_ref, out_ref):
    half = first_ref.shape[0]
    out_ref[:half] = first_ref[...]
    out_ref[half:] = second_ref[...]


def join_halves(first, second):
    return pl.pallas_call(
        join_kernel,
        out_shape=jax.ShapeDtypeStruct((2 * first.shape[0], first.shape[1]), BF16),
        compiler_params=PARAMS,
        cost_estimate=FREE,
    )(first, second)


def add_kernel(index, up_ref, down_ref, from_left_ref, from_right_ref, up_out, down_out, held, got, in_sems, out_sems):
    half = got.shape[2]
    pieces = [(up_ref, from_left_ref, up_out, pl.ds(0, half)), (down_ref, from_right_ref, down_out, pl.ds(half, half))]
    loads, stores = Copies(in_sems), Copies(out_sems)
    for i, (block, part, _, rows) in enumerate(pieces):
        loads.start(block.at[:, rows, :], held.at[i])
        loads.start(part.at[index], got.at[i])
    for i, (_, _, out, rows) in enumerate(pieces):
        for load in loads.started[2 * i : 2 * i + 2]:
            load.wait()
        held[i] = add_rounded(held[i], got[i])
        stores.start(held.at[i], out.at[:, rows, :])
    for store in stores.started:
        store.wait()


def add_halves(up, down, far, index):
    count, size, columns = up.shape
    half = pltpu.VMEM((2, count, size // 2, columns), BF16)
    return pl.pallas_call(
        functools.partial(add_kernel, index),
        grid=(1,),
        in_specs=[ANYWHERE] * 4,
        out_specs=[ANYWHERE] * 2,
        out_shape=[jax.ShapeDtypeStruct(up.shape, BF16)] * 2,
        scratch_shapes=[half, half, pltpu.SemaphoreType.DMA((4,)), pltpu.SemaphoreType.DMA((2,))],
        input_output_aliases={0: 0, 1: 1},
        compiler_params=pltpu.CompilerParams(vmem_limit_bytes=12 * 2**20),
        cost_estimate=FREE,
    )(up, down, *far)


def add_first(block, part):
    half = part.shape[-2]
    return jnp.concatenate([add_rounded(block[..., :half, :], part), block[..., half:, :]], axis=-2)


def add_last(block, part):
    half = part.shape[-2]
    return jnp.concatenate([block[..., :half, :], add_rounded(block[..., half:, :], part)], axis=-2)


def body(inputs, cotangent, layer_norm_gain, w_qkv, w_out):
    shard = inputs.shape[1]
    dp, mp = lax.axis_index("dp"), lax.axis_index("mp")
    x, yhi = mp // 2, mp % 2
    z, ylo, core = dp // 4, (dp // 2) % 2, dp % 2
    weights = jnp.transpose(w_qkv, (1, 0, 2))
    places = [lax.rem(x + dx, 4) * 2 + lax.rem(yhi + dyhi, 2) for dx, dyhi in KEYS] + [core]
    for dz, e in [(2, 1 - ylo), (2, ylo), (1, 1 - ylo), (3, 1 - ylo), (1, ylo), (3, ylo), (0, 1 - ylo), (0, ylo)]:
        places.append(lax.rem(z + dz, 4) * 2 + e)
    table = jnp.stack(places)

    def first_steps(value):
        return {OWN: value, LEFT: shift(value, dx=1), RIGHT: shift(value, dx=-1), ACROSS: shift(value, dyhi=1)}

    def pick(chunks, keys=KEYS):
        return [chunks[key] for key in keys]

    raw, ct = first_steps(inputs), first_steps(cotangent)
    raw_halves = split_halves(raw[LEFT], raw[RIGHT])
    raw_halves = [shift(raw_halves[0], dx=1), shift(raw_halves[1], dx=-1)]
    raw[ACROSS], ct[LEFT], ct[RIGHT] = fence(raw[ACROSS], ct[LEFT], ct[RIGHT])
    raw[3, 1], raw[1, 1] = shift(raw[ACROSS], dx=1), shift(raw[ACROSS], dx=-1)
    ct_halves = split_halves(ct[LEFT], ct[RIGHT])
    ct_halves, raw_halves, ct = fence(ct_halves, raw_halves, ct)
    ct_halves = [shift(ct_halves[0], dx=1), shift(ct_halves[1], dx=-1)]
    raw[FAR] = join_halves(*raw_halves)
    raw[2, 1] = shift(raw[FAR], dyhi=1)
    d_attn = near_d_attn(table, pick(ct, KEYS[:4]), w_out)
    gain = lax.dynamic_slice_in_dim(layer_norm_gain, mp * shard, shard, 0)
    raw[3, 1], raw[1, 1], ct[ACROSS], d_attn, gain = fence(raw[3, 1], raw[1, 1], ct[ACROSS], d_attn, gain)
    ct[3, 1], ct[1, 1] = shift(ct[ACROSS], dx=1), shift(ct[ACROSS], dx=-1)
    ct[FAR] = ct_halves
    raw, ct[FAR] = fence(raw, ct[FAR])
    ct[2, 1] = [shift(part, dyhi=1) for part in ct[FAR]]
    *normed_sides, row_mean, row_scale, qkv, scales, attn, probs = front(table, pick(raw), weights, layer_norm_gain)
    ct, qkv, scales, normed_sides, attn, probs = fence(ct, qkv, scales, normed_sides, attn, probs)

    normed_sides = (normed_sides[0], shift(normed_sides[1], dcore=1))
    d_qkv, *out_sides = tail(table, pick(ct), w_out, attn, d_attn, qkv, scales, probs)
    d_qkv, out_sides, normed_sides = fence(d_qkv, out_sides, normed_sides)

    qkv_sides = (d_qkv, shift(d_qkv, dcore=1))
    out_sides = (out_sides[0], shift(out_sides[1], dcore=1))
    first_terms = normed_terms(table, 5, 3, d_qkv, weights)
    first_terms, out_sides, qkv_sides = fence(first_terms, out_sides, qkv_sides)
    far_blocks = weight_blocks(table, FAR_BLOCKS, 2, normed_sides, out_sides, qkv_sides, True)
    first_terms, far_blocks, d_qkv, out_sides, qkv_sides = fence(first_terms, far_blocks, d_qkv, out_sides, qkv_sides)

    far_across, left_across, right_across = (
        shift(first_terms[0], dyhi=1),
        shift(first_terms[1], dx=1),
        shift(first_terms[2], dx=-1),
    )
    far_blocks = [shift(far_blocks[0], dz=1), shift(far_blocks[1], dz=-1)]
    across_term, far_term = normed_terms(table, 3, 2, d_qkv, weights)
    blocks = weight_blocks(table, NEXT_BLOCKS, 5, normed_sides, out_sides, qkv_sides)
    far_across, left_across, right_across, far_blocks, blocks, far_term, across_term = fence(
        far_across, left_across, right_across, far_blocks, blocks, far_term, across_term
    )

    up, down = add_halves(blocks[0], blocks[1], far_blocks, 0)
    up, down, far_term, far_across, across_term = fence(up, down, far_term, far_across, across_term)
    other = (shift(up, dz=1), shift(down, dz=-1))
    far_term = add_rounded(far_term, far_across)
    far_left, far_right = shift(far_term[:SEQ], dx=1), shift(far_term[SEQ:], dx=-1)
    across_sum = shift(add_rounded(across_term, left_across, right_across), dyhi=1)
    far_left, far_right, d_qkv = fence(far_left, far_right, d_qkv)
    own_term, left_term, right_term = normed_terms(table, 0, 3, d_qkv, weights)
    up, down = add_halves(blocks[2], blocks[3], far_blocks, 1)
    right_term, left_term = add_first(right_term, far_left), add_last(left_term, far_right)
    standardized = (inputs.astype(F32) - row_mean) * row_scale
    other, across_sum, up, down, standardized, right_term, left_term, qkv_sides = fence(
        other, across_sum, up, down, standardized, right_term, left_term, qkv_sides
    )

    from_left, from_right = shift(right_term, dx=1), shift(left_term, dx=-1)
    mine = (shift(up, dz=1), shift(down, dz=-1))
    other_got = shift(add_rounded(blocks[4], *other), dylo=1)
    own_block = weight_blocks(table, LAST_BLOCK, 1, normed_sides, out_sides, qkv_sides)[0]
    own_block, from_left, from_right = fence(own_block, from_left, from_right)
    d_normed = add(own_term, from_left, from_right, across_sum)
    scaled = d_normed * gain
    sums = jnp.stack([jnp.sum(scaled, axis=-1), jnp.sum(scaled * standardized, axis=-1)])
    sums = sums + shift(sums, dx=1) + shift(sums, dx=-1) + shift(sums, dx=2)
    means = (sums + shift(sums, dyhi=1)) / (8 * shard)
    gain_sum = jnp.sum(d_normed * standardized, axis=0).reshape(6, -1)
    gain_sum = gain_sum + shift(gain_sum, dcore=1)
    gain_sum = gain_sum + lax.ppermute(gain_sum, AXES, mirrored(1))
    gain_sum = gain_sum + lax.ppermute(gain_sum, AXES, mirrored(3))
    total = add_rounded(own_block, *mine, other_got)
    total, means, gain_sum = fence(total, means, gain_sum)

    gain_gradient = (gain_sum + shift(gain_sum, dylo=1)).reshape(shard)
    back = row_scale * (scaled - means[0][:, None] - standardized * means[1][:, None])
    input_grad = (cotangent.astype(F32) + back).astype(BF16)
    return input_grad, jnp.transpose(total[:3], (1, 0, 2)), total[3], gain_gradient


def solution(mesh):
    in_specs = (P("dp", "mp"), P("dp", "mp"), P(), P(None, None, "mp"), P("mp", None))
    out_specs = (P("dp", "mp"), P("dp", None, "mp"), P("mp", "dp"), P("mp"))
    return jax.shard_map(body, mesh=mesh, in_specs=in_specs, out_specs=out_specs, check_vma=False)
```

```python
import functools

import jax
import jax.numpy as jnp
from jax import lax
from jax.experimental import pallas as pl
from jax.experimental.pallas import tpu as pltpu
from jax.sharding import PartitionSpec as P

HEAD = 128
SEQ = 256
AXES = ("dp", "mp")
F32 = jnp.float32
BF16 = jnp.bfloat16


def place(index):
    dp, mp = divmod(index, 8)
    return mp // 2, (mp % 2) * 2 + (dp // 2) % 2, dp // 4, dp % 2


def index_of(x, y, z, core):
    x, y, z = x % 4, y % 4, z % 4
    return (z * 4 + (y % 2) * 2 + core) * 8 + x * 2 + y // 2


def shift(value, dx=0, dyhi=0, dylo=0, dz=0, dcore=0):
    pairs = []
    for index in range(128):
        x, y, z, core = place(index)
        pairs.append((index, index_of(x + dx, y ^ (2 * dyhi) ^ dylo, z + dz, core ^ dcore)))
    return lax.ppermute(value, AXES, pairs)


def mirrored(flip):
    pairs = []
    for index in range(128):
        x, y, z, core = place(index)
        pairs.append((index, index_of(x, y, z ^ flip, core)))
    return pairs


def fence(*values):
    return lax.optimization_barrier(values)


def dot(a, b, ca, cb):
    return lax.dot_general(a, b, (((ca,), (cb,)), ((), ())), preferred_element_type=F32)


def add(*terms):
    return sum(t.astype(F32) for t in terms)


def add_rounded(*terms):
    return add(*terms).astype(BF16)


def head_norm(values):
    centered = values - jnp.mean(values, axis=-1, keepdims=True)
    scale = lax.rsqrt(jnp.mean(centered * centered, axis=-1, keepdims=True) + 1e-06)
    return centered * scale, scale


def head_norm_grad(grad, normalized, scale):
    return scale * (
        grad
        - jnp.mean(grad, axis=-1, keepdims=True)
        - normalized * jnp.mean(grad * normalized, axis=-1, keepdims=True)
    )


FREE = pl.CostEstimate(flops=0, bytes_accessed=0, transcendentals=0)
PARAMS = pltpu.CompilerParams(vmem_limit_bytes=60 * 2**20)


def whole(array):
    return pl.BlockSpec(array.shape, lambda i, table: (0,) * array.ndim)


def by_core(core, values):
    half = values.shape[1] // 2
    low, high = values[:, :half], values[:, half:]
    return jnp.where(core == 0, low, high), jnp.where(core == 0, high, low)


ANYWHERE = pl.BlockSpec(memory_space=pl.ANY)
OWN, LEFT, RIGHT, ACROSS, FAR = (0, 0), (3, 0), (1, 0), (0, 1), (2, 0)
KEYS = [OWN, LEFT, RIGHT, ACROSS, FAR, (2, 1), (1, 1), (3, 1)]
CORE, FAR_BLOCKS, NEXT_BLOCKS, LAST_BLOCK = 8, 9, 11, 16


class Copies:
    def __init__(self, sems):
        self.sems, self.started = sems, []

    def start(self, source, target):
        copy = pltpu.make_async_copy(source, target, self.sems.at[len(self.started)])
        copy.start()
        self.started.append(copy)
        return copy


def rows_at(table_ref, index, size):
    return pl.ds(pl.multiple_of(table_ref[index] * size, size), size)


def front_kernel(table_ref, gain_ref, weights_ref, *refs):
    chunks, refs = refs[:8], refs[8:]
    kept_ref, given_ref, mean_ref, scale_ref, qkv_ref, scales_ref, attn_ref, probs_ref = refs[:8]
    chunk_buffer, weight_buffer, kept_buffer, given_buffer, total_ref, in_sems, out_sems = refs[8:]
    rows, shard = chunks[0].shape
    loads, stores = Copies(in_sems), Copies(out_sems)
    chunk_loads = [loads.start(chunks[i], chunk_buffer.at[i]) for i in range(8)]
    for load in chunk_loads:
        load.wait()
    weight_loads = [
        loads.start(weights_ref.at[:, rows_at(table_ref, i, shard), :], weight_buffer.at[i]) for i in range(8)
    ]

    @pl.loop(0, rows // 64)
    def _(index):
        at = pl.ds(pl.multiple_of(index * 64, 64), 64)
        total = sum(chunk_buffer[i, at, :].astype(F32) for i in range(8))
        mean = jnp.sum(total, axis=-1, keepdims=True) / (8 * shard)
        spread = sum(jnp.square(chunk_buffer[i, at, :].astype(F32) - mean) for i in range(8))
        variance = jnp.sum(spread, axis=-1, keepdims=True) / (8 * shard)
        mean_ref[at, :] = mean
        scale_ref[at, :] = lax.rsqrt(variance + 1e-06)

    for i in range(8):
        standardized = (chunk_buffer[i].astype(F32) - mean_ref[...]) * scale_ref[...]
        normed = (standardized * gain_ref[table_ref[i]]).astype(BF16)
        kept_buffer[i], given_buffer[i] = by_core(table_ref[CORE], normed)
        stores.start(kept_buffer.at[i], kept_ref.at[table_ref[i]])
        stores.start(given_buffer.at[i], given_ref.at[table_ref[i]])
        weight_loads[i].wait()
        for j in range(3):
            term = dot(normed, weight_buffer[i, j], 1, 0)
            if i:
                total_ref[j] += term
            else:
                total_ref[j] = term

    for image in range(rows // SEQ):
        at = slice(image * SEQ, (image + 1) * SEQ)
        for head in range(3):
            columns = slice(head * HEAD, (head + 1) * HEAD)
            q_n, scales_ref[at, head : head + 1] = head_norm(total_ref[0, at, columns])
            k_n, scales_ref[at, head + 3 : head + 4] = head_norm(total_ref[1, at, columns])
            q_b, k_b, v_b = q_n.astype(BF16), k_n.astype(BF16), total_ref[2, at, columns].astype(BF16)
            qkv_ref[0, at, columns], qkv_ref[1, at, columns], qkv_ref[2, at, columns] = q_b, k_b, v_b
            weights = jnp.exp(dot(q_b, k_b, 1, 1) * (1.0 / HEAD**0.5))
            probs = (weights / jnp.sum(weights, axis=-1, keepdims=True)).astype(BF16)
            probs_ref[image, head] = probs
            attn_ref[at, columns] = dot(probs, v_b, 1, 0).astype(BF16)
    for store in stores.started:
        store.wait()


def front(table, chunks, weights, gain):
    rows, shard = chunks[0].shape
    columns = weights.shape[2]
    half = jax.ShapeDtypeStruct((8, rows, shard // 2), BF16)
    column = jax.ShapeDtypeStruct((rows, 1), F32)
    qkv = jax.ShapeDtypeStruct((3, rows, columns), BF16)
    scales = jax.ShapeDtypeStruct((rows, 8), F32)
    attn = jax.ShapeDtypeStruct((rows, columns), BF16)
    probs = jax.ShapeDtypeStruct((rows // SEQ, 3, SEQ, SEQ), BF16)
    return pl.pallas_call(
        front_kernel,
        grid_spec=pltpu.PrefetchScalarGridSpec(
            num_scalar_prefetch=1,
            grid=(1,),
            in_specs=[whole(jax.ShapeDtypeStruct((8, 1, shard), F32))] + [ANYWHERE] * 9,
            out_specs=[ANYWHERE] * 2 + [whole(o) for o in (column, column, qkv, scales, attn, probs)],
            scratch_shapes=[
                pltpu.VMEM((8, rows, shard), BF16),
                pltpu.VMEM((8, 3, shard, columns), BF16),
                pltpu.VMEM(half.shape, BF16),
                pltpu.VMEM(half.shape, BF16),
                pltpu.VMEM(qkv.shape, F32),
                pltpu.SemaphoreType.DMA((16,)),
                pltpu.SemaphoreType.DMA((16,)),
            ],
        ),
        out_shape=[half, half, column, column, qkv, scales, attn, probs],
        compiler_params=PARAMS,
        cost_estimate=FREE,
    )(table, gain.reshape(8, 1, shard), weights, *chunks)


def near_kernel(table_ref, *refs):
    chunks, (weight_ref, total_ref) = refs[:4], refs[4:]
    for step in range(4):

        @pl.when(pl.program_id(0) == step)
        def _():
            term = dot(chunks[step][...], weight_ref[...], 1, 1)
            if step:
                total_ref[...] += term
            else:
                total_ref[...] = term


def near_d_attn(table, chunks, w_out):
    rows, shard = chunks[0].shape
    heads = w_out.shape[0]
    out = jax.ShapeDtypeStruct((rows, heads), F32)
    return pl.pallas_call(
        near_kernel,
        grid_spec=pltpu.PrefetchScalarGridSpec(
            num_scalar_prefetch=1,
            grid=(4,),
            in_specs=[whole(c) for c in chunks] + [pl.BlockSpec((heads, shard), lambda i, table: (0, table[i]))],
            out_specs=whole(out),
        ),
        out_shape=out,
        compiler_params=PARAMS,
        cost_estimate=FREE,
    )(table, *chunks, w_out)


def tail_kernel(table_ref, w_out_ref, attn_in, total_in, qkv_in, scales_in, probs_in, *refs):
    chunks, refs = refs[:10], refs[10:]
    grad_ref, kept_ref, given_ref = refs[:3]
    chunk_buffer, weight_buffer, attn_ref, total_ref, qkv_ref, scales_ref, probs_ref = refs[3:10]
    grad_buffer, kept_buffer, given_buffer, in_sems, out_sems = refs[10:]
    rows, shard = chunks[0].shape
    loads, stores = Copies(in_sems), Copies(out_sems)
    total_load = loads.start(total_in, total_ref)
    chunk_loads, weight_loads = {}, {}
    parts = [chunks[0:1], chunks[1:2], chunks[2:3], chunks[3:4], chunks[4:6], chunks[6:8], chunks[8:9], chunks[9:10]]

    def load_chunk(i):
        size = rows // len(parts[i])
        return [loads.start(c, chunk_buffer.at[i, pl.ds(n * size, size), :]) for n, c in enumerate(parts[i])]

    for i in range(4, 8):
        chunk_loads[i] = load_chunk(i)
        columns = pl.ds(pl.multiple_of(table_ref[i] * shard, shard), shard)
        weight_loads[i] = loads.start(w_out_ref.at[:, columns], weight_buffer.at[i - 4])
    others = [
        loads.start(source, target)
        for source, target in ((qkv_in, qkv_ref), (scales_in, scales_ref), (probs_in, probs_ref), (attn_in, attn_ref))
    ]
    for i in range(4):
        chunk_loads[i] = load_chunk(i)

    total_load.wait()
    for i in range(4, 8):
        for load in chunk_loads[i]:
            load.wait()
        weight_loads[i].wait()
        total_ref[...] += dot(chunk_buffer[i], weight_buffer[i - 4], 1, 1)
    for load in others:
        load.wait()
    for image in range(rows // SEQ):
        at = slice(image * SEQ, (image + 1) * SEQ)
        for head in range(3):
            columns = slice(head * HEAD, (head + 1) * HEAD)
            q_b, k_b, v_b = qkv_ref[0, at, columns], qkv_ref[1, at, columns], qkv_ref[2, at, columns]
            q_scale, k_scale = scales_ref[at, head : head + 1], scales_ref[at, head + 3 : head + 4]
            probs = probs_ref[image, head]
            d_attn = total_ref[at, columns].astype(BF16)
            d_probs = dot(d_attn, v_b, 1, 1)
            grad_buffer[2, at, columns] = dot(probs, d_attn, 0, 0).astype(BF16)
            probs = probs.astype(F32)
            delta = jnp.sum(probs * d_probs, axis=-1, keepdims=True)
            d_scores = (probs * (d_probs - delta) * (1.0 / HEAD**0.5)).astype(BF16)
            d_qn = dot(d_scores, k_b, 1, 0)
            d_kn = dot(d_scores, q_b, 0, 0)
            grad_buffer[0, at, columns] = head_norm_grad(d_qn, q_b.astype(F32), q_scale).astype(BF16)
            grad_buffer[1, at, columns] = head_norm_grad(d_kn, k_b.astype(F32), k_scale).astype(BF16)
    stores.start(grad_buffer, grad_ref)
    for i in (4, 5, 6, 7, 0, 1, 2, 3):
        if i < 4:
            chunk_loads[i][0].wait()
        term = dot(attn_ref[...], chunk_buffer[i], 0, 0).astype(BF16)
        kept_buffer[i], given_buffer[i] = by_core(table_ref[CORE], term)
        stores.start(kept_buffer.at[i], kept_ref.at[table_ref[i]])
        stores.start(given_buffer.at[i], given_ref.at[table_ref[i]])
    for store in stores.started:
        store.wait()


def tail(table, chunks, w_out, attn, total, qkv, scales, probs):
    rows, shard = chunks[0].shape
    heads = w_out.shape[0]
    grad = jax.ShapeDtypeStruct(qkv.shape, BF16)
    half = jax.ShapeDtypeStruct((8, heads, shard // 2), BF16)
    return pl.pallas_call(
        tail_kernel,
        grid_spec=pltpu.PrefetchScalarGridSpec(
            num_scalar_prefetch=1,
            grid=(1,),
            in_specs=[ANYWHERE] * 16,
            out_specs=[ANYWHERE] * 3,
            scratch_shapes=[
                pltpu.VMEM((8, rows, shard), BF16),
                pltpu.VMEM((4, heads, shard), BF16),
                pltpu.VMEM(attn.shape, BF16),
                pltpu.VMEM(total.shape, F32),
                pltpu.VMEM(qkv.shape, BF16),
                pltpu.VMEM(scales.shape, F32),
                pltpu.VMEM(probs.shape, BF16),
                pltpu.VMEM(grad.shape, BF16),
                pltpu.VMEM(half.shape, BF16),
                pltpu.VMEM(half.shape, BF16),
                pltpu.SemaphoreType.DMA((19,)),
                pltpu.SemaphoreType.DMA((17,)),
            ],
        ),
        out_shape=[grad, half, half],
        compiler_params=PARAMS,
        cost_estimate=FREE,
    )(table, w_out, attn, total, qkv, scales, probs, *jax.tree.leaves(chunks))


def normed_kernel(first, count, table_ref, grad_in, weights_ref, *refs):
    out_refs, (grad_ref, weight_buffer, out_buffer, in_sems, out_sems) = refs[:count], refs[count:]
    shard = weight_buffer.shape[2]
    loads, stores = Copies(in_sems), Copies(out_sems)

    def weight_copy(i):
        source = weights_ref.at[:, rows_at(table_ref, first + i, shard), :]
        return pltpu.make_async_copy(source, weight_buffer.at[i], in_sems.at[i + 1])

    loads.start(grad_in, grad_ref)
    for i in range(count):
        weight_copy(i).start()
    loads.started[0].wait()

    @pl.loop(0, count)
    def _(step):
        weight_copy(step).wait()
        out_buffer[step] = sum(dot(grad_ref[j], weight_buffer[step, j], 1, 1) for j in range(3)).astype(BF16)
        for i in range(count):

            @pl.when(step == i)
            def _():
                pltpu.make_async_copy(out_buffer.at[i], out_refs[i], out_sems.at[i]).start()

    for i in range(count):
        pltpu.make_async_copy(out_buffer.at[i], out_refs[i], out_sems.at[i]).wait()


def normed_terms(table, first, count, d_qkv, weights):
    _, rows, columns = d_qkv.shape
    shard = weights.shape[1] // 8
    return pl.pallas_call(
        functools.partial(normed_kernel, first, count),
        grid_spec=pltpu.PrefetchScalarGridSpec(
            num_scalar_prefetch=1,
            grid=(1,),
            in_specs=[ANYWHERE] * 2,
            out_specs=[ANYWHERE] * count,
            scratch_shapes=[
                pltpu.VMEM(d_qkv.shape, BF16),
                pltpu.VMEM((count, 3, shard, columns), BF16),
                pltpu.VMEM((count, rows, shard), BF16),
                pltpu.SemaphoreType.DMA((count + 1,)),
                pltpu.SemaphoreType.DMA((count,)),
            ],
        ),
        out_shape=[jax.ShapeDtypeStruct((rows, shard), BF16)] * count,
        compiler_params=PARAMS,
        cost_estimate=FREE,
    )(table, d_qkv, weights)


def block_kernel(first, count, halves, table_ref, *refs):
    left, out, right = refs[0:2], refs[2:4], refs[4:6]
    out_refs, refs = refs[6 : 6 + (2 if halves else count)], refs[6 + (2 if halves else count) :]
    left_buffer, out_buffer, right_buffer, sum_buffer, in_sems, out_sems = refs
    size = sum_buffer.shape[2]

    def loads(i):
        place = table_ref[first + i]
        pairs = [(left[s].at[place], left_buffer.at[i, s]) for s in range(2)]
        pairs += [(out[s].at[place], out_buffer.at[i, s]) for s in range(2)]
        return [pltpu.make_async_copy(s, t, in_sems.at[2 + 4 * i + n]) for n, (s, t) in enumerate(pairs)]

    def stores(i):
        if not halves:
            return [pltpu.make_async_copy(sum_buffer.at[i], out_refs[i], out_sems.at[i])]
        rows = [pl.ds(part * (size // 2), size // 2) for part in range(2)]
        return [
            pltpu.make_async_copy(sum_buffer.at[i, :, rows[part], :], out_refs[part].at[i], out_sems.at[2 * i + part])
            for part in range(2)
        ]

    sides = [pltpu.make_async_copy(right[s], right_buffer.at[s], in_sems.at[s]) for s in range(2)]
    for copy in sides:
        copy.start()
    for i in range(count):
        for copy in loads(i):
            copy.start()
    for copy in sides:
        copy.wait()

    @pl.loop(0, count)
    def _(step):
        for copy in loads(step):
            copy.wait()
        for j in range(3):
            total = dot(left_buffer[step, 0], right_buffer[0, j], 0, 0) + dot(left_buffer[step, 1], right_buffer[1, j], 0, 0)
            sum_buffer[step, j] = total.astype(BF16)
        sum_buffer[step, 3] = add_rounded(out_buffer[step, 0], out_buffer[step, 1])
        for i in range(count):

            @pl.when(step == i)
            def _():
                for copy in stores(i):
                    copy.start()

    for i in range(count):
        for copy in stores(i):
            copy.wait()


def weight_blocks(table, first, count, left, out, right, halves=False):
    _, rows, size = left[0].shape
    columns = right[0].shape[2]
    if halves:
        out_shape = [jax.ShapeDtypeStruct((count, 4, size // 2, columns), BF16)] * 2
    else:
        out_shape = [jax.ShapeDtypeStruct((4, size, columns), BF16)] * count
    return pl.pallas_call(
        functools.partial(block_kernel, first, count, halves),
        grid_spec=pltpu.PrefetchScalarGridSpec(
            num_scalar_prefetch=1,
            grid=(1,),
            in_specs=[ANYWHERE] * 6,
            out_specs=[ANYWHERE] * len(out_shape),
            scratch_shapes=[
                pltpu.VMEM((count, 2, rows, size), BF16),
                pltpu.VMEM((count, 2, size, columns), BF16),
                pltpu.VMEM((2, 3, rows, columns), BF16),
                pltpu.VMEM((count, 4, size, columns), BF16),
                pltpu.SemaphoreType.DMA((2 + 4 * count,)),
                pltpu.SemaphoreType.DMA((count * (2 if halves else 1),)),
            ],
        ),
        out_shape=out_shape,
        compiler_params=PARAMS,
        cost_estimate=FREE,
    )(table, *left, *out, *right)


def split_kernel(first_ref, second_ref, first_half_ref, second_half_ref):
    first_half_ref[...] = first_ref[...]
    second_half_ref[...] = second_ref[...]


def split_halves(first, second):
    rows, width = first.shape
    half = (rows // 2, width)
    return pl.pallas_call(
        split_kernel,
        grid=(1,),
        in_specs=[pl.BlockSpec(half, functools.partial(lambda part, i: (part, 0), part)) for part in (0, 1)],
        out_specs=[pl.BlockSpec(half, lambda i: (0, 0))] * 2,
        out_shape=[jax.ShapeDtypeStruct(half, BF16)] * 2,
        compiler_params=PARAMS,
        cost_estimate=FREE,
    )(first, second)


def join_kernel(first_ref, second_ref, out_ref):
    half = first_ref.shape[0]
    out_ref[:half] = first_ref[...]
    out_ref[half:] = second_ref[...]


def join_halves(first, second):
    return pl.pallas_call(
        join_kernel,
        out_shape=jax.ShapeDtypeStruct((2 * first.shape[0], first.shape[1]), BF16),
        compiler_params=PARAMS,
        cost_estimate=FREE,
    )(first, second)


def add_kernel(index, up_ref, down_ref, from_left_ref, from_right_ref, up_out, down_out, held, got, in_sems, out_sems):
    half = got.shape[2]
    pieces = [(up_ref, from_left_ref, up_out, pl.ds(0, half)), (down_ref, from_right_ref, down_out, pl.ds(half, half))]
    loads, stores = Copies(in_sems), Copies(out_sems)
    for i, (block, part, _, rows) in enumerate(pieces):
        loads.start(block.at[:, rows, :], held.at[i])
        loads.start(part.at[index], got.at[i])
    for i, (_, _, out, rows) in enumerate(pieces):
        for load in loads.started[2 * i : 2 * i + 2]:
            load.wait()
        held[i] = add_rounded(held[i], got[i])
        stores.start(held.at[i], out.at[:, rows, :])
    for store in stores.started:
        store.wait()


def add_halves(up, down, far, index):
    count, size, columns = up.shape
    half = pltpu.VMEM((2, count, size // 2, columns), BF16)
    return pl.pallas_call(
        functools.partial(add_kernel, index),
        grid=(1,),
        in_specs=[ANYWHERE] * 4,
        out_specs=[ANYWHERE] * 2,
        out_shape=[jax.ShapeDtypeStruct(up.shape, BF16)] * 2,
        scratch_shapes=[half, half, pltpu.SemaphoreType.DMA((4,)), pltpu.SemaphoreType.DMA((2,))],
        input_output_aliases={0: 0, 1: 1},
        compiler_params=pltpu.CompilerParams(vmem_limit_bytes=12 * 2**20),
        cost_estimate=FREE,
    )(up, down, *far)


def add_first(block, part):
    half = part.shape[-2]
    return jnp.concatenate([add_rounded(block[..., :half, :], part), block[..., half:, :]], axis=-2)


def add_last(block, part):
    half = part.shape[-2]
    return jnp.concatenate([block[..., :half, :], add_rounded(block[..., half:, :], part)], axis=-2)


def body(inputs, cotangent, layer_norm_gain, w_qkv, w_out):
    shard = inputs.shape[1]
    dp, mp = lax.axis_index("dp"), lax.axis_index("mp")
    x, yhi = mp // 2, mp % 2
    z, ylo, core = dp // 4, (dp // 2) % 2, dp % 2
    weights = jnp.transpose(w_qkv, (1, 0, 2))
    places = [lax.rem(x + dx, 4) * 2 + lax.rem(yhi + dyhi, 2) for dx, dyhi in KEYS] + [core]
    for dz, e in [(2, 1 - ylo), (2, ylo), (1, 1 - ylo), (3, 1 - ylo), (1, ylo), (3, ylo), (0, 1 - ylo), (0, ylo)]:
        places.append(lax.rem(z + dz, 4) * 2 + e)
    table = jnp.stack(places)

    def first_steps(value):
        return {OWN: value, LEFT: shift(value, dx=1), RIGHT: shift(value, dx=-1), ACROSS: shift(value, dyhi=1)}

    def pick(chunks, keys=KEYS):
        return [chunks[key] for key in keys]

    raw, ct = first_steps(inputs), first_steps(cotangent)
    raw_halves = split_halves(raw[LEFT], raw[RIGHT])
    raw_halves = [shift(raw_halves[0], dx=1), shift(raw_halves[1], dx=-1)]
    raw[ACROSS], ct[LEFT], ct[RIGHT] = fence(raw[ACROSS], ct[LEFT], ct[RIGHT])
    raw[3, 1], raw[1, 1] = shift(raw[ACROSS], dx=1), shift(raw[ACROSS], dx=-1)
    ct_halves = split_halves(ct[LEFT], ct[RIGHT])
    ct_halves, raw_halves, ct = fence(ct_halves, raw_halves, ct)
    ct_halves = [shift(ct_halves[0], dx=1), shift(ct_halves[1], dx=-1)]
    raw[FAR] = join_halves(*raw_halves)
    raw[2, 1] = shift(raw[FAR], dyhi=1)
    d_attn = near_d_attn(table, pick(ct, KEYS[:4]), w_out)
    gain = lax.dynamic_slice_in_dim(layer_norm_gain, mp * shard, shard, 0)
    raw[3, 1], raw[1, 1], ct[ACROSS], d_attn, gain = fence(raw[3, 1], raw[1, 1], ct[ACROSS], d_attn, gain)
    ct[3, 1], ct[1, 1] = shift(ct[ACROSS], dx=1), shift(ct[ACROSS], dx=-1)
    ct[FAR] = ct_halves
    raw, ct[FAR] = fence(raw, ct[FAR])
    ct[2, 1] = [shift(part, dyhi=1) for part in ct[FAR]]
    *normed_sides, row_mean, row_scale, qkv, scales, attn, probs = front(table, pick(raw), weights, layer_norm_gain)
    ct, qkv, scales, normed_sides, attn, probs = fence(ct, qkv, scales, normed_sides, attn, probs)

    normed_sides = (normed_sides[0], shift(normed_sides[1], dcore=1))
    d_qkv, *out_sides = tail(table, pick(ct), w_out, attn, d_attn, qkv, scales, probs)
    d_qkv, out_sides, normed_sides = fence(d_qkv, out_sides, normed_sides)

    qkv_sides = (d_qkv, shift(d_qkv, dcore=1))
    out_sides = (out_sides[0], shift(out_sides[1], dcore=1))
    first_terms = normed_terms(table, 5, 3, d_qkv, weights)
    first_terms, out_sides, qkv_sides = fence(first_terms, out_sides, qkv_sides)
    far_blocks = weight_blocks(table, FAR_BLOCKS, 2, normed_sides, out_sides, qkv_sides, True)
    first_terms, far_blocks, d_qkv, out_sides, qkv_sides = fence(first_terms, far_blocks, d_qkv, out_sides, qkv_sides)

    far_across, left_across, right_across = (
        shift(first_terms[0], dyhi=1),
        shift(first_terms[1], dx=1),
        shift(first_terms[2], dx=-1),
    )
    far_blocks = [shift(far_blocks[0], dz=1), shift(far_blocks[1], dz=-1)]
    across_term, far_term = normed_terms(table, 3, 2, d_qkv, weights)
    blocks = weight_blocks(table, NEXT_BLOCKS, 5, normed_sides, out_sides, qkv_sides)
    far_across, left_across, right_across, far_blocks, blocks, far_term, across_term = fence(
        far_across, left_across, right_across, far_blocks, blocks, far_term, across_term
    )

    up, down = add_halves(blocks[0], blocks[1], far_blocks, 0)
    up, down, far_term, far_across, across_term = fence(up, down, far_term, far_across, across_term)
    other = (shift(up, dz=1), shift(down, dz=-1))
    far_term = add_rounded(far_term, far_across)
    far_left, far_right = shift(far_term[:SEQ], dx=1), shift(far_term[SEQ:], dx=-1)
    across_sum = shift(add_rounded(across_term, left_across, right_across), dyhi=1)
    far_left, far_right, d_qkv = fence(far_left, far_right, d_qkv)
    own_term, left_term, right_term = normed_terms(table, 0, 3, d_qkv, weights)
    up, down = add_halves(blocks[2], blocks[3], far_blocks, 1)
    right_term, left_term = add_first(right_term, far_left), add_last(left_term, far_right)
    standardized = (inputs.astype(F32) - row_mean) * row_scale
    other, across_sum, up, down, standardized, right_term, left_term, qkv_sides = fence(
        other, across_sum, up, down, standardized, right_term, left_term, qkv_sides
    )

    from_left, from_right = shift(right_term, dx=1), shift(left_term, dx=-1)
    mine = (shift(up, dz=1), shift(down, dz=-1))
    other_got = shift(add_rounded(blocks[4], *other), dylo=1)
    own_block = weight_blocks(table, LAST_BLOCK, 1, normed_sides, out_sides, qkv_sides)[0]
    own_block, from_left, from_right = fence(own_block, from_left, from_right)
    d_normed = add(own_term, from_left, from_right, across_sum)
    scaled = d_normed * gain
    sums = jnp.stack([jnp.sum(scaled, axis=-1), jnp.sum(scaled * standardized, axis=-1)])
    sums = sums + shift(sums, dx=1) + shift(sums, dx=-1) + shift(sums, dx=2)
    means = (sums + shift(sums, dyhi=1)) / (8 * shard)
    gain_sum = jnp.sum(d_normed * standardized, axis=0).reshape(6, -1)
    gain_sum = gain_sum + shift(gain_sum, dcore=1)
    gain_sum = gain_sum + lax.ppermute(gain_sum, AXES, mirrored(1))
    other_gain = lax.ppermute(gain_sum, AXES, mirrored(3))
    total = add_rounded(own_block, *mine, other_got)
    total, means, gain_sum = fence(total, means, gain_sum)

    gain_sum = gain_sum + other_gain
    gain_gradient = (gain_sum + shift(gain_sum, dylo=1)).reshape(shard)
    back = row_scale * (scaled - means[0][:, None] - standardized * means[1][:, None])
    input_grad = (cotangent.astype(F32) + back).astype(BF16)
    return input_grad, jnp.transpose(total[:3], (1, 0, 2)), total[3], gain_gradient


def solution(mesh):
    in_specs = (P("dp", "mp"), P("dp", "mp"), P(), P(None, None, "mp"), P("mp", None))
    out_specs = (P("dp", "mp"), P("dp", None, "mp"), P("mp", "dp"), P("mp"))
    return jax.shard_map(body, mesh=mesh, in_specs=in_specs, out_specs=out_specs, check_vma=False)
```

```python
import functools

import jax
import jax.numpy as jnp
from jax import lax
from jax.experimental import pallas as pl
from jax.experimental.pallas import tpu as pltpu
from jax.sharding import PartitionSpec as P

HEAD = 128
SEQ = 256
AXES = ("dp", "mp")
F32 = jnp.float32
BF16 = jnp.bfloat16


def place(index):
    dp, mp = divmod(index, 8)
    return mp // 2, (mp % 2) * 2 + (dp // 2) % 2, dp // 4, dp % 2


def index_of(x, y, z, core):
    x, y, z = x % 4, y % 4, z % 4
    return (z * 4 + (y % 2) * 2 + core) * 8 + x * 2 + y // 2


def shift(value, dx=0, dyhi=0, dylo=0, dz=0, dcore=0):
    pairs = []
    for index in range(128):
        x, y, z, core = place(index)
        pairs.append((index, index_of(x + dx, y ^ (2 * dyhi) ^ dylo, z + dz, core ^ dcore)))
    return lax.ppermute(value, AXES, pairs)


def mirrored(flip):
    pairs = []
    for index in range(128):
        x, y, z, core = place(index)
        pairs.append((index, index_of(x, y, z ^ flip, core)))
    return pairs


def fence(*values):
    return lax.optimization_barrier(values)


def dot(a, b, ca, cb):
    return lax.dot_general(a, b, (((ca,), (cb,)), ((), ())), preferred_element_type=F32)


def add(*terms):
    return sum(t.astype(F32) for t in terms)


def add_rounded(*terms):
    return add(*terms).astype(BF16)


def head_norm(values):
    centered = values - jnp.mean(values, axis=-1, keepdims=True)
    scale = lax.rsqrt(jnp.mean(centered * centered, axis=-1, keepdims=True) + 1e-06)
    return centered * scale, scale


def head_norm_grad(grad, normalized, scale):
    return scale * (
        grad
        - jnp.mean(grad, axis=-1, keepdims=True)
        - normalized * jnp.mean(grad * normalized, axis=-1, keepdims=True)
    )


FREE = pl.CostEstimate(flops=0, bytes_accessed=0, transcendentals=0)
PARAMS = pltpu.CompilerParams(vmem_limit_bytes=60 * 2**20)


def whole(array):
    return pl.BlockSpec(array.shape, lambda i, table: (0,) * array.ndim)


def by_core(core, values):
    half = values.shape[1] // 2
    low, high = values[:, :half], values[:, half:]
    return jnp.where(core == 0, low, high), jnp.where(core == 0, high, low)


ANYWHERE = pl.BlockSpec(memory_space=pl.ANY)
OWN, LEFT, RIGHT, ACROSS, FAR = (0, 0), (3, 0), (1, 0), (0, 1), (2, 0)
KEYS = [OWN, LEFT, RIGHT, ACROSS, FAR, (2, 1), (1, 1), (3, 1)]
CORE, FAR_BLOCKS, NEXT_BLOCKS, LAST_BLOCK = 8, 9, 11, 16


class Copies:
    def __init__(self, sems):
        self.sems, self.started = sems, []

    def start(self, source, target):
        copy = pltpu.make_async_copy(source, target, self.sems.at[len(self.started)])
        copy.start()
        self.started.append(copy)
        return copy


def rows_at(table_ref, index, size):
    return pl.ds(pl.multiple_of(table_ref[index] * size, size), size)


def front_kernel(table_ref, gain_ref, weights_ref, *refs):
    chunks, refs = refs[:8], refs[8:]
    kept_ref, given_ref, mean_ref, scale_ref, qkv_ref, scales_ref, attn_ref, probs_ref = refs[:8]
    chunk_buffer, weight_buffer, kept_buffer, given_buffer, total_ref, in_sems, out_sems = refs[8:]
    rows, shard = chunks[0].shape
    loads, stores = Copies(in_sems), Copies(out_sems)
    chunk_loads = [loads.start(chunks[i], chunk_buffer.at[i]) for i in range(8)]
    for load in chunk_loads:
        load.wait()
    weight_loads = [
        loads.start(weights_ref.at[:, rows_at(table_ref, i, shard), :], weight_buffer.at[i]) for i in range(8)
    ]

    @pl.loop(0, rows // 64)
    def _(index):
        at = pl.ds(pl.multiple_of(index * 64, 64), 64)
        total = sum(chunk_buffer[i, at, :].astype(F32) for i in range(8))
        mean = jnp.sum(total, axis=-1, keepdims=True) / (8 * shard)
        spread = sum(jnp.square(chunk_buffer[i, at, :].astype(F32) - mean) for i in range(8))
        variance = jnp.sum(spread, axis=-1, keepdims=True) / (8 * shard)
        mean_ref[at, :] = mean
        scale_ref[at, :] = lax.rsqrt(variance + 1e-06)

    for i in range(8):
        standardized = (chunk_buffer[i].astype(F32) - mean_ref[...]) * scale_ref[...]
        normed = (standardized * gain_ref[table_ref[i]]).astype(BF16)
        kept_buffer[i], given_buffer[i] = by_core(table_ref[CORE], normed)
        stores.start(kept_buffer.at[i], kept_ref.at[table_ref[i]])
        stores.start(given_buffer.at[i], given_ref.at[table_ref[i]])
        weight_loads[i].wait()
        for j in range(3):
            term = dot(normed, weight_buffer[i, j], 1, 0)
            if i:
                total_ref[j] += term
            else:
                total_ref[j] = term

    for image in range(rows // SEQ):
        at = slice(image * SEQ, (image + 1) * SEQ)
        for head in range(3):
            columns = slice(head * HEAD, (head + 1) * HEAD)
            q_n, scales_ref[at, head : head + 1] = head_norm(total_ref[0, at, columns])
            k_n, scales_ref[at, head + 3 : head + 4] = head_norm(total_ref[1, at, columns])
            q_b, k_b, v_b = q_n.astype(BF16), k_n.astype(BF16), total_ref[2, at, columns].astype(BF16)
            qkv_ref[0, at, columns], qkv_ref[1, at, columns], qkv_ref[2, at, columns] = q_b, k_b, v_b
            weights = jnp.exp(dot(q_b, k_b, 1, 1) * (1.0 / HEAD**0.5))
            probs = (weights / jnp.sum(weights, axis=-1, keepdims=True)).astype(BF16)
            probs_ref[image, head] = probs
            attn_ref[at, columns] = dot(probs, v_b, 1, 0).astype(BF16)
    for store in stores.started:
        store.wait()


def front(table, chunks, weights, gain):
    rows, shard = chunks[0].shape
    columns = weights.shape[2]
    half = jax.ShapeDtypeStruct((8, rows, shard // 2), BF16)
    column = jax.ShapeDtypeStruct((rows, 1), F32)
    qkv = jax.ShapeDtypeStruct((3, rows, columns), BF16)
    scales = jax.ShapeDtypeStruct((rows, 8), F32)
    attn = jax.ShapeDtypeStruct((rows, columns), BF16)
    probs = jax.ShapeDtypeStruct((rows // SEQ, 3, SEQ, SEQ), BF16)
    return pl.pallas_call(
        front_kernel,
        grid_spec=pltpu.PrefetchScalarGridSpec(
            num_scalar_prefetch=1,
            grid=(1,),
            in_specs=[whole(jax.ShapeDtypeStruct((8, 1, shard), F32))] + [ANYWHERE] * 9,
            out_specs=[ANYWHERE] * 2 + [whole(o) for o in (column, column, qkv, scales, attn, probs)],
            scratch_shapes=[
                pltpu.VMEM((8, rows, shard), BF16),
                pltpu.VMEM((8, 3, shard, columns), BF16),
                pltpu.VMEM(half.shape, BF16),
                pltpu.VMEM(half.shape, BF16),
                pltpu.VMEM(qkv.shape, F32),
                pltpu.SemaphoreType.DMA((16,)),
                pltpu.SemaphoreType.DMA((16,)),
            ],
        ),
        out_shape=[half, half, column, column, qkv, scales, attn, probs],
        compiler_params=PARAMS,
        cost_estimate=FREE,
    )(table, gain.reshape(8, 1, shard), weights, *chunks)


def near_kernel(table_ref, *refs):
    chunks, (weight_ref, total_ref) = refs[:4], refs[4:]
    for step in range(4):

        @pl.when(pl.program_id(0) == step)
        def _():
            term = dot(chunks[step][...], weight_ref[...], 1, 1)
            if step:
                total_ref[...] += term
            else:
                total_ref[...] = term


def near_d_attn(table, chunks, w_out):
    rows, shard = chunks[0].shape
    heads = w_out.shape[0]
    out = jax.ShapeDtypeStruct((rows, heads), F32)
    return pl.pallas_call(
        near_kernel,
        grid_spec=pltpu.PrefetchScalarGridSpec(
            num_scalar_prefetch=1,
            grid=(4,),
            in_specs=[whole(c) for c in chunks] + [pl.BlockSpec((heads, shard), lambda i, table: (0, table[i]))],
            out_specs=whole(out),
        ),
        out_shape=out,
        compiler_params=PARAMS,
        cost_estimate=FREE,
    )(table, *chunks, w_out)


def tail_kernel(table_ref, w_out_ref, attn_in, total_in, qkv_in, scales_in, probs_in, *refs):
    chunks, refs = refs[:10], refs[10:]
    grad_ref, kept_ref, given_ref = refs[:3]
    chunk_buffer, weight_buffer, attn_ref, total_ref, qkv_ref, scales_ref, probs_ref = refs[3:10]
    grad_buffer, kept_buffer, given_buffer, in_sems, out_sems = refs[10:]
    rows, shard = chunks[0].shape
    loads, stores = Copies(in_sems), Copies(out_sems)
    total_load = loads.start(total_in, total_ref)
    chunk_loads, weight_loads = {}, {}
    parts = [chunks[0:1], chunks[1:2], chunks[2:3], chunks[3:4], chunks[4:6], chunks[6:8], chunks[8:9], chunks[9:10]]

    def load_chunk(i):
        size = rows // len(parts[i])
        return [loads.start(c, chunk_buffer.at[i, pl.ds(n * size, size), :]) for n, c in enumerate(parts[i])]

    for i in range(4, 8):
        chunk_loads[i] = load_chunk(i)
        columns = pl.ds(pl.multiple_of(table_ref[i] * shard, shard), shard)
        weight_loads[i] = loads.start(w_out_ref.at[:, columns], weight_buffer.at[i - 4])
    others = [
        loads.start(source, target)
        for source, target in ((qkv_in, qkv_ref), (scales_in, scales_ref), (probs_in, probs_ref), (attn_in, attn_ref))
    ]
    for i in range(4):
        chunk_loads[i] = load_chunk(i)

    total_load.wait()
    for i in range(4, 8):
        for load in chunk_loads[i]:
            load.wait()
        weight_loads[i].wait()
        total_ref[...] += dot(chunk_buffer[i], weight_buffer[i - 4], 1, 1)
    for load in others:
        load.wait()
    for image in range(rows // SEQ):
        at = slice(image * SEQ, (image + 1) * SEQ)
        for head in range(3):
            columns = slice(head * HEAD, (head + 1) * HEAD)
            q_b, k_b, v_b = qkv_ref[0, at, columns], qkv_ref[1, at, columns], qkv_ref[2, at, columns]
            q_scale, k_scale = scales_ref[at, head : head + 1], scales_ref[at, head + 3 : head + 4]
            probs = probs_ref[image, head]
            d_attn = total_ref[at, columns].astype(BF16)
            d_probs = dot(d_attn, v_b, 1, 1)
            grad_buffer[2, at, columns] = dot(probs, d_attn, 0, 0).astype(BF16)
            probs = probs.astype(F32)
            delta = jnp.sum(probs * d_probs, axis=-1, keepdims=True)
            d_scores = (probs * (d_probs - delta) * (1.0 / HEAD**0.5)).astype(BF16)
            d_qn = dot(d_scores, k_b, 1, 0)
            d_kn = dot(d_scores, q_b, 0, 0)
            grad_buffer[0, at, columns] = head_norm_grad(d_qn, q_b.astype(F32), q_scale).astype(BF16)
            grad_buffer[1, at, columns] = head_norm_grad(d_kn, k_b.astype(F32), k_scale).astype(BF16)
    stores.start(grad_buffer, grad_ref)
    for i in (4, 5, 6, 7, 0, 1, 2, 3):
        if i < 4:
            chunk_loads[i][0].wait()
        term = dot(attn_ref[...], chunk_buffer[i], 0, 0).astype(BF16)
        kept_buffer[i], given_buffer[i] = by_core(table_ref[CORE], term)
        stores.start(kept_buffer.at[i], kept_ref.at[table_ref[i]])
        stores.start(given_buffer.at[i], given_ref.at[table_ref[i]])
    for store in stores.started:
        store.wait()


def tail(table, chunks, w_out, attn, total, qkv, scales, probs):
    rows, shard = chunks[0].shape
    heads = w_out.shape[0]
    grad = jax.ShapeDtypeStruct(qkv.shape, BF16)
    half = jax.ShapeDtypeStruct((8, heads, shard // 2), BF16)
    return pl.pallas_call(
        tail_kernel,
        grid_spec=pltpu.PrefetchScalarGridSpec(
            num_scalar_prefetch=1,
            grid=(1,),
            in_specs=[ANYWHERE] * 16,
            out_specs=[ANYWHERE] * 3,
            scratch_shapes=[
                pltpu.VMEM((8, rows, shard), BF16),
                pltpu.VMEM((4, heads, shard), BF16),
                pltpu.VMEM(attn.shape, BF16),
                pltpu.VMEM(total.shape, F32),
                pltpu.VMEM(qkv.shape, BF16),
                pltpu.VMEM(scales.shape, F32),
                pltpu.VMEM(probs.shape, BF16),
                pltpu.VMEM(grad.shape, BF16),
                pltpu.VMEM(half.shape, BF16),
                pltpu.VMEM(half.shape, BF16),
                pltpu.SemaphoreType.DMA((19,)),
                pltpu.SemaphoreType.DMA((17,)),
            ],
        ),
        out_shape=[grad, half, half],
        compiler_params=PARAMS,
        cost_estimate=FREE,
    )(table, w_out, attn, total, qkv, scales, probs, *jax.tree.leaves(chunks))


def normed_kernel(first, count, table_ref, grad_in, weights_ref, *refs):
    out_refs, (grad_ref, weight_buffer, out_buffer, in_sems, out_sems) = refs[:count], refs[count:]
    shard = weight_buffer.shape[2]
    loads, stores = Copies(in_sems), Copies(out_sems)

    def weight_copy(i):
        source = weights_ref.at[:, rows_at(table_ref, first + i, shard), :]
        return pltpu.make_async_copy(source, weight_buffer.at[i], in_sems.at[i + 1])

    loads.start(grad_in, grad_ref)
    for i in range(count):
        weight_copy(i).start()
    loads.started[0].wait()

    @pl.loop(0, count)
    def _(step):
        weight_copy(step).wait()
        out_buffer[step] = sum(dot(grad_ref[j], weight_buffer[step, j], 1, 1) for j in range(3)).astype(BF16)
        for i in range(count):

            @pl.when(step == i)
            def _():
                pltpu.make_async_copy(out_buffer.at[i], out_refs[i], out_sems.at[i]).start()

    for i in range(count):
        pltpu.make_async_copy(out_buffer.at[i], out_refs[i], out_sems.at[i]).wait()


def normed_terms(table, first, count, d_qkv, weights):
    _, rows, columns = d_qkv.shape
    shard = weights.shape[1] // 8
    return pl.pallas_call(
        functools.partial(normed_kernel, first, count),
        grid_spec=pltpu.PrefetchScalarGridSpec(
            num_scalar_prefetch=1,
            grid=(1,),
            in_specs=[ANYWHERE] * 2,
            out_specs=[ANYWHERE] * count,
            scratch_shapes=[
                pltpu.VMEM(d_qkv.shape, BF16),
                pltpu.VMEM((count, 3, shard, columns), BF16),
                pltpu.VMEM((count, rows, shard), BF16),
                pltpu.SemaphoreType.DMA((count + 1,)),
                pltpu.SemaphoreType.DMA((count,)),
            ],
        ),
        out_shape=[jax.ShapeDtypeStruct((rows, shard), BF16)] * count,
        compiler_params=PARAMS,
        cost_estimate=FREE,
    )(table, d_qkv, weights)


def block_kernel(first, count, halves, table_ref, *refs):
    left, out, right = refs[0:2], refs[2:4], refs[4:6]
    out_refs, refs = refs[6 : 6 + (2 if halves else count)], refs[6 + (2 if halves else count) :]
    left_buffer, out_buffer, right_buffer, sum_buffer, in_sems, out_sems = refs
    size = sum_buffer.shape[2]

    def loads(i):
        place = table_ref[first + i]
        pairs = [(left[s].at[place], left_buffer.at[i, s]) for s in range(2)]
        pairs += [(out[s].at[place], out_buffer.at[i, s]) for s in range(2)]
        return [pltpu.make_async_copy(s, t, in_sems.at[2 + 4 * i + n]) for n, (s, t) in enumerate(pairs)]

    def stores(i):
        if not halves:
            return [pltpu.make_async_copy(sum_buffer.at[i], out_refs[i], out_sems.at[i])]
        rows = [pl.ds(part * (size // 2), size // 2) for part in range(2)]
        return [
            pltpu.make_async_copy(sum_buffer.at[i, :, rows[part], :], out_refs[part].at[i], out_sems.at[2 * i + part])
            for part in range(2)
        ]

    sides = [pltpu.make_async_copy(right[s], right_buffer.at[s], in_sems.at[s]) for s in range(2)]
    for copy in sides:
        copy.start()
    for i in range(count):
        for copy in loads(i):
            copy.start()
    for copy in sides:
        copy.wait()

    @pl.loop(0, count)
    def _(step):
        for copy in loads(step):
            copy.wait()
        for j in range(3):
            total = dot(left_buffer[step, 0], right_buffer[0, j], 0, 0) + dot(left_buffer[step, 1], right_buffer[1, j], 0, 0)
            sum_buffer[step, j] = total.astype(BF16)
        sum_buffer[step, 3] = add_rounded(out_buffer[step, 0], out_buffer[step, 1])
        for i in range(count):

            @pl.when(step == i)
            def _():
                for copy in stores(i):
                    copy.start()

    for i in range(count):
        for copy in stores(i):
            copy.wait()


def weight_blocks(table, first, count, left, out, right, halves=False):
    _, rows, size = left[0].shape
    columns = right[0].shape[2]
    if halves:
        out_shape = [jax.ShapeDtypeStruct((count, 4, size // 2, columns), BF16)] * 2
    else:
        out_shape = [jax.ShapeDtypeStruct((4, size, columns), BF16)] * count
    return pl.pallas_call(
        functools.partial(block_kernel, first, count, halves),
        grid_spec=pltpu.PrefetchScalarGridSpec(
            num_scalar_prefetch=1,
            grid=(1,),
            in_specs=[ANYWHERE] * 6,
            out_specs=[ANYWHERE] * len(out_shape),
            scratch_shapes=[
                pltpu.VMEM((count, 2, rows, size), BF16),
                pltpu.VMEM((count, 2, size, columns), BF16),
                pltpu.VMEM((2, 3, rows, columns), BF16),
                pltpu.VMEM((count, 4, size, columns), BF16),
                pltpu.SemaphoreType.DMA((2 + 4 * count,)),
                pltpu.SemaphoreType.DMA((count * (2 if halves else 1),)),
            ],
        ),
        out_shape=out_shape,
        compiler_params=PARAMS,
        cost_estimate=FREE,
    )(table, *left, *out, *right)


def split_kernel(first_ref, second_ref, first_half_ref, second_half_ref):
    first_half_ref[...] = first_ref[...]
    second_half_ref[...] = second_ref[...]


def split_halves(first, second):
    rows, width = first.shape
    half = (rows // 2, width)
    return pl.pallas_call(
        split_kernel,
        grid=(1,),
        in_specs=[pl.BlockSpec(half, functools.partial(lambda part, i: (part, 0), part)) for part in (0, 1)],
        out_specs=[pl.BlockSpec(half, lambda i: (0, 0))] * 2,
        out_shape=[jax.ShapeDtypeStruct(half, BF16)] * 2,
        compiler_params=PARAMS,
        cost_estimate=FREE,
    )(first, second)


def join_kernel(first_ref, second_ref, out_ref):
    half = first_ref.shape[0]
    out_ref[:half] = first_ref[...]
    out_ref[half:] = second_ref[...]


def join_halves(first, second):
    return pl.pallas_call(
        join_kernel,
        out_shape=jax.ShapeDtypeStruct((2 * first.shape[0], first.shape[1]), BF16),
        compiler_params=PARAMS,
        cost_estimate=FREE,
    )(first, second)


def add_kernel(index, up_ref, down_ref, from_left_ref, from_right_ref, up_out, down_out, held, got, in_sems, out_sems):
    half = got.shape[-2]
    at = lambda rows: (slice(None),) * (len(got.shape) - 3) + (rows, slice(None))
    pieces = [(up_ref, from_left_ref, up_out, pl.ds(0, half)), (down_ref, from_right_ref, down_out, pl.ds(half, half))]
    loads, stores = Copies(in_sems), Copies(out_sems)
    for i, (block, part, _, rows) in enumerate(pieces):
        loads.start(block.at[at(rows)], held.at[i])
        loads.start(part if index is None else part.at[index], got.at[i])
    for i, (_, _, out, rows) in enumerate(pieces):
        for load in loads.started[2 * i : 2 * i + 2]:
            load.wait()
        held[i] = add_rounded(held[i], got[i])
        stores.start(held.at[i], out.at[at(rows)])
    for store in stores.started:
        store.wait()


def add_halves(up, down, far, index=None):
    *count, size, columns = up.shape
    half = pltpu.VMEM((2, *count, size // 2, columns), BF16)
    return pl.pallas_call(
        functools.partial(add_kernel, index),
        grid=(1,),
        in_specs=[ANYWHERE] * 4,
        out_specs=[ANYWHERE] * 2,
        out_shape=[jax.ShapeDtypeStruct(up.shape, BF16)] * 2,
        scratch_shapes=[half, half, pltpu.SemaphoreType.DMA((4,)), pltpu.SemaphoreType.DMA((2,))],
        input_output_aliases={0: 0, 1: 1},
        compiler_params=pltpu.CompilerParams(vmem_limit_bytes=12 * 2**20),
        cost_estimate=FREE,
    )(up, down, *far)


def body(inputs, cotangent, layer_norm_gain, w_qkv, w_out):
    shard = inputs.shape[1]
    dp, mp = lax.axis_index("dp"), lax.axis_index("mp")
    x, yhi = mp // 2, mp % 2
    z, ylo, core = dp // 4, (dp // 2) % 2, dp % 2
    weights = jnp.transpose(w_qkv, (1, 0, 2))
    places = [lax.rem(x + dx, 4) * 2 + lax.rem(yhi + dyhi, 2) for dx, dyhi in KEYS] + [core]
    for dz, e in [(2, 1 - ylo), (2, ylo), (1, 1 - ylo), (3, 1 - ylo), (1, ylo), (3, ylo), (0, 1 - ylo), (0, ylo)]:
        places.append(lax.rem(z + dz, 4) * 2 + e)
    table = jnp.stack(places)

    def first_steps(value):
        return {OWN: value, LEFT: shift(value, dx=1), RIGHT: shift(value, dx=-1), ACROSS: shift(value, dyhi=1)}

    def pick(chunks, keys=KEYS):
        return [chunks[key] for key in keys]

    raw, ct = first_steps(inputs), first_steps(cotangent)
    raw_halves = split_halves(raw[LEFT], raw[RIGHT])
    raw_halves = [shift(raw_halves[0], dx=1), shift(raw_halves[1], dx=-1)]
    raw[ACROSS], ct[LEFT], ct[RIGHT] = fence(raw[ACROSS], ct[LEFT], ct[RIGHT])
    raw[3, 1], raw[1, 1] = shift(raw[ACROSS], dx=1), shift(raw[ACROSS], dx=-1)
    ct_halves = split_halves(ct[LEFT], ct[RIGHT])
    ct_halves, raw_halves, ct = fence(ct_halves, raw_halves, ct)
    ct_halves = [shift(ct_halves[0], dx=1), shift(ct_halves[1], dx=-1)]
    raw[FAR] = join_halves(*raw_halves)
    raw[2, 1] = shift(raw[FAR], dyhi=1)
    d_attn = near_d_attn(table, pick(ct, KEYS[:4]), w_out)
    gain = lax.dynamic_slice_in_dim(layer_norm_gain, mp * shard, shard, 0)
    raw[3, 1], raw[1, 1], ct[ACROSS], d_attn, gain = fence(raw[3, 1], raw[1, 1], ct[ACROSS], d_attn, gain)
    ct[3, 1], ct[1, 1] = shift(ct[ACROSS], dx=1), shift(ct[ACROSS], dx=-1)
    ct[FAR] = ct_halves
    raw, ct[FAR] = fence(raw, ct[FAR])
    ct[2, 1] = [shift(part, dyhi=1) for part in ct[FAR]]
    *normed_sides, row_mean, row_scale, qkv, scales, attn, probs = front(table, pick(raw), weights, layer_norm_gain)
    ct, qkv, scales, normed_sides, attn, probs = fence(ct, qkv, scales, normed_sides, attn, probs)

    normed_sides = (normed_sides[0], shift(normed_sides[1], dcore=1))
    d_qkv, *out_sides = tail(table, pick(ct), w_out, attn, d_attn, qkv, scales, probs)
    d_qkv, out_sides, normed_sides = fence(d_qkv, out_sides, normed_sides)

    qkv_sides = (d_qkv, shift(d_qkv, dcore=1))
    out_sides = (out_sides[0], shift(out_sides[1], dcore=1))
    first_terms = normed_terms(table, 5, 3, d_qkv, weights)
    first_terms, out_sides, qkv_sides = fence(first_terms, out_sides, qkv_sides)
    far_blocks = weight_blocks(table, FAR_BLOCKS, 2, normed_sides, out_sides, qkv_sides, True)
    first_terms, far_blocks, d_qkv, out_sides, qkv_sides = fence(first_terms, far_blocks, d_qkv, out_sides, qkv_sides)

    far_across, left_across, right_across = (
        shift(first_terms[0], dyhi=1),
        shift(first_terms[1], dx=1),
        shift(first_terms[2], dx=-1),
    )
    far_blocks = [shift(far_blocks[0], dz=1), shift(far_blocks[1], dz=-1)]
    across_term, far_term = normed_terms(table, 3, 2, d_qkv, weights)
    blocks = weight_blocks(table, NEXT_BLOCKS, 5, normed_sides, out_sides, qkv_sides)
    far_across, left_across, right_across, far_blocks, blocks, far_term, across_term = fence(
        far_across, left_across, right_across, far_blocks, blocks, far_term, across_term
    )

    up, down = add_halves(blocks[0], blocks[1], far_blocks, 0)
    up, down, far_term, far_across, across_term = fence(up, down, far_term, far_across, across_term)
    other = (shift(up, dz=1), shift(down, dz=-1))
    far_term = add_rounded(far_term, far_across)
    far_left, far_right = shift(far_term[:SEQ], dx=1), shift(far_term[SEQ:], dx=-1)
    across_sum = shift(add_rounded(across_term, left_across, right_across), dyhi=1)
    far_left, far_right, d_qkv = fence(far_left, far_right, d_qkv)
    own_term, left_term, right_term = normed_terms(table, 0, 3, d_qkv, weights)
    up, down = add_halves(blocks[2], blocks[3], far_blocks, 1)
    right_term, left_term = add_halves(right_term, left_term, (far_left, far_right))
    standardized = (inputs.astype(F32) - row_mean) * row_scale
    other, across_sum, up, down, standardized, right_term, left_term, qkv_sides = fence(
        other, across_sum, up, down, standardized, right_term, left_term, qkv_sides
    )

    from_left, from_right = shift(right_term, dx=1), shift(left_term, dx=-1)
    mine = (shift(up, dz=1), shift(down, dz=-1))
    other_got = shift(add_rounded(blocks[4], *other), dylo=1)
    own_block = weight_blocks(table, LAST_BLOCK, 1, normed_sides, out_sides, qkv_sides)[0]
    own_block, from_left, from_right = fence(own_block, from_left, from_right)
    d_normed = add(own_term, from_left, from_right, across_sum)
    scaled = d_normed * gain
    sums = jnp.stack([jnp.sum(scaled, axis=-1), jnp.sum(scaled * standardized, axis=-1)])
    sums = sums + shift(sums, dx=1) + shift(sums, dx=-1) + shift(sums, dx=2)
    means = (sums + shift(sums, dyhi=1)) / (8 * shard)
    gain_sum = jnp.sum(d_normed * standardized, axis=0).reshape(6, -1)
    gain_sum = gain_sum + shift(gain_sum, dcore=1)
    gain_sum = gain_sum + lax.ppermute(gain_sum, AXES, mirrored(1))
    other_gain = lax.ppermute(gain_sum, AXES, mirrored(3))
    total = add_rounded(own_block, *mine, other_got)
    total, means, gain_sum = fence(total, means, gain_sum)

    gain_sum = gain_sum + other_gain
    gain_gradient = (gain_sum + shift(gain_sum, dylo=1)).reshape(shard)
    back = row_scale * (scaled - means[0][:, None] - standardized * means[1][:, None])
    input_grad = (cotangent.astype(F32) + back).astype(BF16)
    return input_grad, jnp.transpose(total[:3], (1, 0, 2)), total[3], gain_gradient


def solution(mesh):
    in_specs = (P("dp", "mp"), P("dp", "mp"), P(), P(None, None, "mp"), P("mp", None))
    out_specs = (P("dp", "mp"), P("dp", None, "mp"), P("mp", "dp"), P("mp"))
    return jax.shard_map(body, mesh=mesh, in_specs=in_specs, out_specs=out_specs, check_vma=False)
```
